32 devices in a mesh: dp: 2 (over y), ctx: 4 (over x, core), expert: 4 (over z).
Axes of the slice: x: 2, y: 2, z: 4, core: 2. Of those that a mesh axis runs over, the one named last changes fastest.
Arguments:
- tokens: bfloat16 [8, 1024, 2048], P(('dp', 'expert'), 'ctx'), may hold values from -6 to 6
- w_query: bfloat16 [2048, 2048], P(('dp', 'ctx', 'expert')), may hold values from -0.125 to 0.125
- w_key: bfloat16 [2048, 2048], P(('dp', 'ctx', 'expert')), may hold values from -0.125 to 0.125
- w_value: bfloat16 [2048, 2048], P(('dp', 'ctx', 'expert')), may hold values from -0.125 to 0.125
- w_output: bfloat16 [2048, 2048], P(('dp', 'ctx', 'expert')), may hold values from -2 to 2
- w_router: bfloat16 [2048, 16], P(('dp', 'ctx', 'expert')), may hold values from -0.0625 to 0.0625
- norm_gains: bfloat16 [4, 2048], P(None, ('dp', 'ctx', 'expert')), may hold values from 0.5 to 1.5
- w_gate: bfloat16 [16, 2048, 1024], P(('ctx', 'expert')), may hold values from -0.125 to 0.125
- w_up: bfloat16 [16, 2048, 1024], P(('ctx', 'expert')), may hold values from -0.125 to 0.125
- w_down: bfloat16 [16, 1024, 2048], P(('ctx', 'expert')), may hold values from -5 to 5
- routes: int32 [8, 1024, 8], P(('dp', 'expert'), 'ctx'), may hold values from 0 to 15, all different within a row; in each aligned block of 256 rows (0 to 255, 256 to 511, ..., all dimensions but the last counted through in order) at most 160 rows name the same one
- positions: int32 [8, 1024], P(('dp', 'expert')), may hold values from 0 to 1023, each once within a row
- lengths: int32 [8], P(('dp', 'expert')), may hold values from 512 to 1024
- cotangent: bfloat16 [8, 1024, 2048], P(('dp', 'expert'), 'ctx'), may hold values from -6 to 6
Outputs:
- mixed: bfloat16 [8, 1024, 2048], P(('dp', 'expert'), 'ctx')
- grad_tokens: float32 [8, 1024, 2048], P(('dp', 'expert'), 'ctx')
- grad_query: float32 [2048, 2048], P(('dp', 'ctx', 'expert'))
- grad_key: float32 [2048, 2048], P(('dp', 'ctx', 'expert'))
- grad_value: float32 [2048, 2048], P(('dp', 'ctx', 'expert'))
- grad_output: float32 [2048, 2048], P(('dp', 'ctx', 'expert'))
- grad_router: float32 [2048, 16], P(('dp', 'ctx', 'expert'))
- grad_gains: float32 [4, 2048], P(None, ('dp', 'ctx', 'expert'))
- grad_gate: float32 [16, 2048, 1024], P(('ctx', 'expert'))
- grad_up: float32 [16, 2048, 1024], P(('ctx', 'expert'))
- grad_down: float32 [16, 1024, 2048], P(('ctx', 'expert'))
The draws below stay inside these ranges and needn't reach their ends.
Inputs may be any that keep to these rules, and one draw needn't show every extreme that they name: `routes`: in each aligned block of 256 rows (the rows of one device) no expert is named by more than 160 rows; a row names 8 different experts. `positions`: each row holds every position once.
All inputs are finite; a program needn't handle non-finite values.
Results may differ from the reference program's by a relative error of at most 0.025.
Values may be sent and summed in bfloat16 or wider, within the bound.
No kernel may reach another device: no remote copies, remote signals or barrier semaphores. Data moves between devices by JAX's collectives and lax.ppermute only.
A program may use at most 320 MiB of HBM per device.

```python
import math
import jax
import jax.numpy as jnp
import numpy as np
from jax import lax

D = 2048
HEADS = 16
HEAD_DIM = 128
FF = 1024
TOP = 8
SEQ = 1024
ROWS = 256
SEQS = 8
EXPERTS = 16
CAP = 160
N_CTX = 4


def draw_lengths(key, part):
    key = jax.random.fold_in(key, 7)
    first_key, second_key = jax.random.split(key)
    drawn = jax.random.randint(first_key, (SEQS,), SEQ // 2, SEQ + 1)
    shuffled = jax.random.permutation(second_key, SEQS)
    drawn = jnp.where(shuffled == 0, SEQ, drawn)
    return jnp.where(shuffled == 1, SEQ // 2, drawn).astype(jnp.int32)


def shard_levels(rng, shape, cuts, least, high):
    def one(axis_at, parts):
        heights = jax.random.uniform(jax.random.fold_in(jax.random.fold_in(rng, 6), axis_at), (parts,), jnp.float32, least / len(cuts), high / len(cuts))
        return jnp.repeat(jnp.exp(heights), shape[axis_at] // parts).reshape((-1,) + (1,) * (len(shape) - axis_at - 1))

    factor_of = one(*cuts[0])
    for cut in cuts[1:]:
        factor_of = factor_of * one(*cut)
    return factor_of


def shared_out(rng, own, number, rows, count, top, limit, lean):
    order = jax.random.permutation(rng, count)
    crowded, ordinary = portions_of(count, rows * top, limit, lean, True), portions_of(count, rows * top, limit, lean, False)
    places = jnp.arange(count)

    def named(tallies, rotation):
        used = int((tallies > 0).sum())
        fixed = max(1, used // 4)
        passed = fixed + (places - fixed + rotation * (used - fixed)) % max(1, count - fixed)
        return jnp.zeros((count,), jnp.int32).at[order[jnp.where(places < fixed, places, passed)]].set(jnp.asarray(tallies, jnp.int32))

    tallies = jnp.where(number % 4 == 0, named(crowded, number // 4), named(ordinary, number - number // 4 - 1))
    mixed = jax.random.permutation(jax.random.fold_in(own, 3), count)
    donor, taker = mixed[0:count // 2 * 2:2], mixed[1:count // 2 * 2:2]
    slack = jnp.minimum(tallies[donor] - 1, limit - tallies[taker]) // 2
    slack = jnp.where((donor == order[0]) | (taker == order[0]) | (tallies[taker] == 0), 0, jnp.maximum(slack, 0))
    passed = jax.random.randint(jax.random.fold_in(own, 4), (count // 2,), 0, 1 << 20) % (slack + 1)
    tallies = tallies.at[donor].add(-passed).at[taker].add(passed)
    labels = jnp.searchsorted(jnp.cumsum(tallies), jnp.arange(rows * top), side="right").astype(jnp.int32)
    grid = labels.reshape(top, rows).T
    grid = grid[jax.random.permutation(jax.random.fold_in(own, 1), rows)]
    rotation = jax.random.randint(jax.random.fold_in(own, 2), (rows, 1), 0, top)
    return jnp.take_along_axis(grid, (jnp.arange(top)[None, :] + rotation) % top, axis=1)


def portions_of(number_of, total, limit, slope, full):
    weights = [(1 << 20) // math.isqrt(standing ** slope) + 1 for standing in range(1, number_of + 1)]
    largest = limit if full else min(limit, max(-(-total // number_of), total * weights[0] // sum(weights)))
    least = 1 if total - largest >= number_of - 1 else 0
    counts, rest = [largest] + [least] * (number_of - 1), total - largest - least * (number_of - 1)
    while rest > 0:
        candidates = [i for i in range(1, number_of) if counts[i] < largest] or [i for i in range(1, number_of) if counts[i] < limit]
        whole, left = sum([weights[i] for i in candidates]), rest
        for i in candidates:
            extra = min(limit - counts[i], max(1, left * weights[i] // whole), rest)
            counts[i] = counts[i] + extra
            rest = rest - extra
    return np.array(counts)


def gaussian(key, extent, spread, bound, cuts=(), kind=jnp.bfloat16):
    values = jax.random.normal(key, extent, jnp.float32) * spread
    if len(cuts) > 0:
        values = shard_levels(key, extent, cuts, -0.22, 0.18) * values
    return jnp.clip(values, min=-bound, max=bound).astype(kind)


def setup_inputs(seed: int = 0) -> dict:
    streams_of = jax.random.split(jax.random.key(seed), 15)
    tokens = gaussian(streams_of[0], (SEQS, SEQ, D), 1.0, 6.0, ((0, 8), (1, 4)))
    w_query = gaussian(streams_of[1], (D, D), D ** -0.5, 0.125, ((0, 32),))
    w_key = gaussian(streams_of[2], (D, D), D ** -0.5, 0.125, ((0, 32),))
    w_value = gaussian(streams_of[3], (D, D), D ** -0.5, 0.125, ((0, 32),))
    w_output = gaussian(streams_of[4], (D, D), (max(D // 256, 8)) ** -0.5, 2.0, ((0, 32),))
    w_router = gaussian(streams_of[5], (D, EXPERTS), (4 * D) ** -0.5, 0.0625, ((0, 32),))
    norm_gains = jnp.clip(1.0 + 0.1 * jax.random.normal(streams_of[6], (4, D), jnp.float32), 0.5, 1.5).astype(jnp.bfloat16)
    w_gate = gaussian(streams_of[7], (EXPERTS, D, FF), D ** -0.5, 0.125, ((0, 16),))
    w_up = gaussian(streams_of[8], (EXPERTS, D, FF), D ** -0.5, 0.125, ((0, 16),))
    w_down = gaussian(streams_of[9], (EXPERTS, FF, D), (0.67 * EXPERTS * FF ** -0.5), 5.0, ((0, 16),))
    routes_keys = jax.random.split(jax.random.fold_in(streams_of[10], 1), SEQS * SEQ // ROWS)
    routes_turns = jax.random.permutation(jax.random.fold_in(streams_of[10], 3), SEQS * SEQ // ROWS)
    routes = jax.vmap(lambda own, number: shared_out(jax.random.fold_in(streams_of[10], 2), own, number, ROWS, EXPERTS, TOP, CAP, 2))(routes_keys, routes_turns).reshape((SEQS, SEQ, TOP))
    positions = jax.vmap(lambda own: jax.random.permutation(own, SEQ))(jax.random.split(streams_of[11], SEQS)).reshape((SEQS, SEQ)).astype(jnp.int32)
    lengths = draw_lengths(jax.random.fold_in(streams_of[14], 71), 0)
    cotangent = gaussian(streams_of[13], (SEQS, SEQ, D), 1.0, 6.0, ((0, 8), (1, 4)))
    return {"tokens": tokens, "w_query": w_query, "w_key": w_key, "w_value": w_value, "w_output": w_output, "w_router": w_router, "norm_gains": norm_gains, "w_gate": w_gate, "w_up": w_up, "w_down": w_down, "routes": routes, "positions": positions, "lengths": lengths, "cotangent": cotangent}


@jax.custom_vjp
def low(v):
    return lax.optimization_barrier(v.astype(jnp.bfloat16)).astype(jnp.float32)

@jax.custom_vjp
def low_back(v):
    return v

def low_keep(v):
    return (low(v), None)

def low_pass(kept, grad):
    return (grad,)

def back_keep(v):
    return (v, None)

def back_low(kept, grad):
    return (low(grad),)
low.defvjp(low_keep, low_pass)
low_back.defvjp(back_keep, back_low)
epsilon = 1e-05
rope_base = 10000.0
highest = lax.Precision.HIGHEST

def matmul(left, right):
    return jnp.dot(left, right, precision=highest, preferred_element_type=jnp.float32)

def rms_normed(values, gain):
    return values * lax.rsqrt(lax.optimization_barrier(jnp.mean(values * values, axis=-1, keepdims=True)) + epsilon) * gain

def rope_tables(where, head_size):
    half_size = head_size // 2
    frequency = rope_base ** (-2.0 * jnp.arange(half_size, dtype=jnp.float32) / head_size)
    angles = where.astype(jnp.float32)[:, None] * frequency[None, :]
    angles = jnp.concatenate([angles, angles], axis=-1)
    return (jnp.cos(angles), jnp.sin(angles))

def rotate(values, cosine, sine, head_count):
    row_count = values.shape[0]
    shaped = values.reshape(row_count, head_count, -1)
    half_size = shaped.shape[-1] // 2
    turned = jnp.concatenate([-shaped[..., half_size:], shaped[..., :half_size]], axis=-1)
    return (shaped * cosine[:, None, :] + turned * sine[:, None, :]).reshape(row_count, -1)

def slot_tables(routes):
    flat_routes = routes.reshape(-1)
    pair_count = flat_routes.shape[0]
    chosen = (flat_routes[:, None] == jnp.arange(EXPERTS)[None, :]).astype(jnp.int32)
    ranking = lax.optimization_barrier(jnp.sum((jnp.cumsum(chosen, axis=0) - 1) * chosen, axis=1))
    room = SEQS * N_CTX * CAP
    target = flat_routes * room + ranking
    pair_ids = jnp.arange(pair_count, dtype=jnp.int32)
    token_of = jnp.full((EXPERTS * room,), SEQS * SEQ, jnp.int32).at[target].set(pair_ids // TOP)
    pair_of = jnp.full((EXPERTS * room,), pair_count, jnp.int32).at[target].set(pair_ids)
    return (token_of.reshape(EXPERTS, room), pair_of.reshape(EXPERTS, room))

def attend_sequence(seq_tokens, where, length, w_query, w_key, w_value, w_output, norm_gains):
    a_low = low(rms_normed(seq_tokens, norm_gains[0]))
    q_raw = low_back(matmul(a_low, w_query))
    k_raw = low_back(matmul(a_low, w_key))
    v_low = low(low_back(matmul(a_low, w_value)))
    cosine, sine = rope_tables(where, HEAD_DIM)
    q_low = low(rotate(rms_normed(q_raw, norm_gains[1]), cosine, sine, HEADS))
    k_low = low(rotate(rms_normed(k_raw, norm_gains[2]), cosine, sine, HEADS))
    key_heads = k_low.reshape(SEQ, HEADS, HEAD_DIM)
    value_heads = v_low.reshape(SEQ, HEADS, HEAD_DIM)
    block_rows = math.gcd(SEQ, 512)
    factor = HEAD_DIM ** (-0.5)

    def one_block(pieces):
        query_block, query_pos = pieces
        scores = low_back(jnp.einsum('qhd,khd->hqk', query_block, key_heads, precision=highest) * factor)
        allowed = (where[None, :] <= query_pos[:, None]) & (where[None, :] < length)
        scores = jnp.where(allowed[None], scores, -1e+30)
        weights = low(jax.nn.softmax(scores, axis=-1))
        return jnp.einsum('hqk,khd->qhd', weights, value_heads, precision=highest)
    blocks = (q_low.reshape(SEQ // block_rows, block_rows, HEADS, HEAD_DIM), where.reshape(SEQ // block_rows, block_rows))
    attended = lax.map(jax.checkpoint(one_block), blocks).reshape(SEQ, D)
    attended_low = low(low_back(attended))
    return seq_tokens + low_back(matmul(attended_low, w_output))

def layer(tokens, w_query, w_key, w_value, w_output, w_router, norm_gains, w_gate, w_up, w_down, routes, positions, lengths, token_of, pair_of):

    def per_sequence(pieces):
        seq_tokens, where, length = pieces
        return attend_sequence(seq_tokens, where, length, w_query, w_key, w_value, w_output, norm_gains)
    first = lax.map(jax.checkpoint(per_sequence), (tokens, positions, lengths))
    flat_first = first.reshape(SEQS * SEQ, D)
    m_low = low(rms_normed(flat_first, norm_gains[3]))
    logits = low_back(matmul(m_low, w_router))
    router_probs = jax.nn.softmax(logits, axis=-1)
    picks = routes.reshape(SEQS * SEQ, TOP)
    gates = jnp.take_along_axis(router_probs, picks, axis=1)
    rows_padded = jnp.concatenate([m_low, jnp.zeros((1, D), m_low.dtype)], axis=0)
    gates_padded = jnp.concatenate([gates.reshape(-1), jnp.zeros((1,), gates.dtype)], axis=0)

    def expert_rows(token_idx, pair_idx, gate_w, up_w, down_w):
        taken = low_back(rows_padded[token_idx])
        gate_pre = low_back(matmul(taken, gate_w))
        up_pre = low_back(matmul(taken, up_w))
        hidden = low(jax.nn.silu(gate_pre) * up_pre)
        produced = low(low_back(matmul(hidden, down_w)))
        return produced * gates_padded[pair_idx][:, None]
    checked = jax.checkpoint(expert_rows)

    def add_expert(total, pieces):
        return (total.at[pieces[0]].add(checked(*pieces)), None)
    start_total = jnp.zeros((SEQS * SEQ + 1, D), flat_first.dtype)
    total, unused = lax.scan(add_expert, start_total, (token_of, pair_of, w_gate, w_up, w_down))
    return flat_first + total[:-1]

def reference(tokens, w_query, w_key, w_value, w_output, w_router, norm_gains, w_gate, w_up, w_down, routes, positions, lengths, cotangent):
    token_of, pair_of = slot_tables(routes)
    floats = tuple((value.astype(jnp.float32) for value in (tokens, w_query, w_key, w_value, w_output, w_router, norm_gains, w_gate, w_up, w_down)))

    def forward(*values):
        return layer(*values, routes, positions, lengths, token_of, pair_of)
    output, pull = jax.vjp(forward, *floats)
    grads = pull(cotangent.astype(jnp.float32).reshape(SEQS * SEQ, D))
    return (output.reshape(SEQS, SEQ, D).astype(jnp.bfloat16), grads[0], grads[1], grads[2], grads[3], grads[4], grads[5], grads[6], grads[7], grads[8], grads[9])
```

```python
import jax
import jax.numpy as jnp
from jax import lax
from jax.sharding import PartitionSpec as P

HEADS = 16

epsilon = 1e-05
rope_base = 10000.0
single = jnp.float32
half = jnp.bfloat16


def dot(left, right):
    return jnp.dot(left, right, preferred_element_type=single)


def dot_t(left, right):
    return lax.dot_general(left, right, (((1,), (1,)), ((), ())), preferred_element_type=single)


def t_dot(left, right):
    return lax.dot_general(left, right, (((0,), (0,)), ((), ())), preferred_element_type=single)


def inverse_rms(values):
    return lax.rsqrt(jnp.mean(values * values, axis=-1, keepdims=True) + epsilon)


def rope_tables(where, head_size):
    half_size = head_size // 2
    frequency = rope_base ** (-2.0 * jnp.arange(half_size, dtype=single) / head_size)
    angles = where.astype(single)[:, None] * frequency[None, :]
    angles = jnp.concatenate([angles, angles], axis=-1)
    return (jnp.cos(angles), jnp.sin(angles))


def rotate(values, cosine, sine, head_size):
    shaped = values.reshape(values.shape[0], -1, head_size)
    half_size = head_size // 2
    turned = jnp.concatenate([-shaped[..., half_size:], shaped[..., :half_size]], axis=-1)
    return (shaped * cosine[:, None, :] + turned * sine[:, None, :]).reshape(values.shape)


def swap(value, axis, bit):
    count = lax.axis_size(axis)
    return lax.ppermute(value, axis, [(i, i ^ bit) for i in range(count)])


def bits_down(count):
    bits = []
    bit = count // 2
    while bit >= 1:
        bits.append(bit)
        bit //= 2
    return bits


def xor_gather(value, axis):
    blocks = {0: value}
    for bit in bits_down(lax.axis_size(axis)):
        held = sorted(blocks)
        moved = swap(jnp.concatenate([blocks[j] for j in held], axis=0), axis, bit)
        for at, j in enumerate(held):
            blocks[j | bit] = moved[at * value.shape[0] : (at + 1) * value.shape[0]]
    return jnp.concatenate([blocks[j] for j in sorted(blocks)], axis=0)


def xor_scatter(value, axis):
    count = lax.axis_size(axis)
    rows = value.shape[0] // count
    held = value
    for bit in reversed(bits_down(count)):
        shaped = held.reshape(-1, 2, rows, held.shape[-1])
        got = swap(shaped[:, 1].astype(half), axis, bit)
        held = shaped[:, 0].astype(single) + got.astype(single)
        held = held.reshape(-1, held.shape[-1])
    return held


def xor_sum(value, axis):
    count = lax.axis_size(axis)
    blocks = value.reshape(-1, count, value.shape[-1] // count)
    for bit in reversed(bits_down(count)):
        got = swap(blocks, axis, bit)
        blocks = blocks + jnp.stack([got[:, j ^ bit] for j in range(count)], axis=1)
    return blocks.reshape(value.shape)


def doubling_gather(value, axes):
    for axis in reversed(axes):
        for bit in reversed(bits_down(lax.axis_size(axis))):
            other = swap(value, axis, bit)
            low = (lax.axis_index(axis) & bit) == 0
            value = jnp.concatenate(
                [jnp.where(low, value, other), jnp.where(low, other, value)], axis=0
            )
    return value


def halving_scatter(value, axes):
    for axis in axes:
        for bit in bits_down(lax.axis_size(axis)):
            rows = value.shape[0] // 2
            low = (lax.axis_index(axis) & bit) == 0
            kept = jnp.where(low, value[:rows], value[rows:])
            sent = jnp.where(low, value[rows:], value[:rows])
            value = kept + swap(sent, axis, bit)
    return value


def snake(outer, inner):
    order = []
    for a in range(outer):
        line = range(inner) if a % 2 == 0 else reversed(range(inner))
        order += [(a, b) for b in line]
    return order


class Ring:
    def __init__(self, axes, planes):
        outer, inner = lax.axis_size(axes[0]) // planes, lax.axis_size(axes[1])
        order = snake(outer, inner)
        self.axes, self.planes, self.count = axes, planes, len(order)
        flat = [[(a * planes + plane) * inner + b for a, b in order] for plane in range(planes)]
        place = [0] * (self.count * planes)
        self.forward, self.backward = [], []
        for line in flat:
            for at, index in enumerate(line):
                place[index] = at
                after = line[(at + 1) % self.count]
                self.forward.append((index, after))
                self.backward.append((after, index))
        self.flat = jnp.asarray(flat, jnp.int32)
        own = lax.axis_index(axes)
        self.place = jnp.asarray(place, jnp.int32)[own]
        self.plane = (own // inner) % planes

    def index(self, offset, other_plane=0):
        return self.flat[self.plane ^ other_plane, (self.place + offset) % self.count]

    def ahead(self, value):
        return lax.ppermute(value, self.axes, self.forward)

    def behind(self, value):
        return lax.ppermute(value, self.axes, self.backward)

    def gather(self, value):
        steps = [[(0, value)]]
        split = value.shape[0] // 2
        from_back = from_front = value
        for step in range(1, self.count // 2):
            from_back, from_front = self.ahead(from_back), self.behind(from_front)
            steps.append([(-step, from_back), (step, from_front)])
        last = jnp.concatenate(
            [self.ahead(from_back[:split]), self.behind(from_front[split:])], axis=0
        )
        steps.append([(self.count // 2, last)])
        return steps

    def gather_flat(self, value):
        out = jnp.zeros((self.count,) + value.shape, value.dtype)
        for step in self.gather(value):
            for offset, piece in step:
                out = lax.dynamic_update_index_in_dim(out, piece, self.index(offset), 0)
        return out

    def scatter(self, pick):
        middle = self.count // 2
        far = pick(middle)
        split = far.shape[0] // 2
        ahead, behind = far[:split], far[split:]
        for step in range(middle - 1, 0, -1):
            got_ahead, got_behind = self.ahead(ahead), self.behind(behind)
            own_ahead, own_behind = pick(step), pick(-step)
            if step == middle - 1:
                ahead = jnp.concatenate([add(own_ahead[:split], got_ahead), own_ahead[split:]])
                behind = jnp.concatenate([own_behind[:split], add(own_behind[split:], got_behind)])
            else:
                ahead, behind = add(own_ahead, got_ahead), add(own_behind, got_behind)
        got_ahead, got_behind = self.ahead(ahead), self.behind(behind)
        return pick(0).astype(single) + got_ahead.astype(single) + got_behind.astype(single)


def add(left, right):
    return (left.astype(single) + right.astype(single)).astype(half)


def both_halves(value):
    low = value.astype(half)
    if lax.axis_size("dp") == 2:
        return low.astype(single) + swap(low, "dp", 1).astype(single)
    return lax.psum(low, "dp").astype(single)


def trade(buffer):
    count = lax.axis_size("ctx") * lax.axis_size("expert")
    shaped = buffer.reshape(count, -1, buffer.shape[-1])
    moved = lax.all_to_all(shaped, ("ctx", "expert"), split_axis=0, concat_axis=0, tiled=True)
    return moved.reshape(buffer.shape)


def activate(gate_pre, up_pre):
    sigmoid = jax.nn.sigmoid(gate_pre)
    activated = gate_pre * sigmoid
    slope = sigmoid * (1.0 + gate_pre * (1.0 - sigmoid))
    return activated, slope


def experts_by_trade(m_low, gates, cot, picks, w_gate, w_up, w_down, expert_total, capacity):
    rows, width = m_low.shape
    top = picks.shape[1]
    locals_ = w_gate.shape[0]
    flat = (picks.reshape(-1)[:, None] == jnp.arange(expert_total)[None, :]).astype(jnp.int32)
    ranking = jnp.sum((jnp.cumsum(flat, axis=0) - 1) * flat, axis=1)
    slots = picks.reshape(-1) * capacity + ranking
    pair_rows = jnp.arange(rows * top) // top
    empty = jnp.zeros((expert_total * capacity, width), half)
    incoming = trade(empty.at[slots].set(m_low[pair_rows])).reshape(-1, locals_, capacity, width)

    def product(form, left, right):
        return jnp.einsum(form, left, right, preferred_element_type=single)

    gate_pre = product("sxcd,xdf->sxcf", incoming, w_gate)
    up_pre = product("sxcd,xdf->sxcf", incoming, w_up)
    activated, slope = activate(gate_pre, up_pre)
    hidden = (activated * up_pre).astype(half)
    produced = product("sxcf,xfd->sxcd", hidden, w_down).astype(half)
    returned = trade(produced.reshape(-1, width))
    picked = returned[slots].reshape(rows, top, width).astype(single)
    mixed = jnp.sum(gates[..., None] * picked, axis=1)
    grad_gates = jnp.sum(cot[:, None, :] * picked, axis=-1)
    back = (gates[..., None] * cot[:, None, :]).astype(half).reshape(-1, width)
    grad_in = trade(empty.at[slots].set(back)).reshape(-1, locals_, capacity, width)
    grad_hidden = product("sxcd,xfd->sxcf", grad_in, w_down)
    grad_down = product("sxcf,sxcd->xfd", hidden, grad_in)
    grad_gate_pre = (grad_hidden * up_pre * slope).astype(half)
    grad_up_pre = (grad_hidden * activated).astype(half)
    grad_gate = product("sxcd,sxcf->xdf", incoming, grad_gate_pre)
    grad_up = product("sxcd,sxcf->xdf", incoming, grad_up_pre)
    grad_rows = product("sxcf,xdf->sxcd", grad_gate_pre, w_gate)
    grad_rows = (grad_rows + product("sxcf,xdf->sxcd", grad_up_pre, w_up)).astype(half)
    grad_back = trade(grad_rows.reshape(-1, width))
    grad_m = jnp.sum(grad_back[slots].reshape(rows, top, width).astype(single), axis=1)
    chosen = picks[..., None] == jnp.arange(expert_total)[None, None, :]
    grad_probs = jnp.sum(jnp.where(chosen, grad_gates[..., None], 0.0), axis=1)
    return mixed, grad_m, grad_probs, (grad_gate, grad_up, grad_down)


def two_parts(value):
    high = lax.reduce_precision(value, 8, 7)
    return high.astype(half), (value - high).astype(half)


class ExpertsByRing:
    def __init__(self, routes_all, cot, w_gate, w_up, w_down, capacity):
        self.ring = Ring(("ctx", "expert"), 2)
        self.capacity = capacity
        self.w_gate, self.w_up, self.w_down = w_gate[0], w_up[0], w_down[0]
        me = lax.axis_index(("ctx", "expert"))
        chosen = jnp.any(routes_all == me.astype(routes_all.dtype), axis=-1)
        rows = chosen.shape[1]
        before = (jnp.arange(rows)[:, None] <= jnp.arange(rows)[None, :]).astype(half)
        rank = dot(chosen.astype(half), before).astype(jnp.int32) - 1
        self.slot = jnp.where(chosen, rank, -1)
        cot_all = lax.all_gather(cot, ("ctx", "expert"), axis=0, tiled=True)
        cot_all = cot_all.reshape(chosen.shape + cot.shape[-1:])
        one_hot = self.slot[:, None, :] == jnp.arange(capacity)[None, :, None]
        self.cot_rows = jnp.einsum(
            "sct,std->scd", one_hot.astype(half), cot_all, preferred_element_type=single
        ).astype(half)
        self.back = jnp.einsum(
            "scd,fd->scf", self.cot_rows, self.w_down, preferred_element_type=single
        )
        self.me = me

    def chunk(self, sources, pieces, width):
        slot = jnp.stack([self.slot[s] for s in sources])
        back = jnp.concatenate([self.back[s] for s in sources])
        cot_rows = jnp.concatenate([self.cot_rows[s] for s in sources])
        one_hot = (slot[:, None, :] == jnp.arange(self.capacity)[None, :, None]).astype(half)
        taken = jnp.einsum(
            "sct,std->scd", one_hot, jnp.stack(pieces), preferred_element_type=single
        )
        taken = taken.reshape(-1, taken.shape[-1])
        incoming = taken[:, :width].astype(half)
        tail = taken[:, width:]
        lane = jnp.arange(tail.shape[1])
        gate = jnp.sum(
            jnp.where((lane == self.me) | (lane == self.me + tail.shape[1] // 2), tail, 0.0),
            axis=-1,
            keepdims=True,
        )
        gate_pre = dot(incoming, self.w_gate)
        up_pre = dot(incoming, self.w_up)
        activated, slope = activate(gate_pre, up_pre)
        hidden = (activated * up_pre).astype(half)
        grad_g = jnp.sum(back * hidden.astype(single), axis=-1, keepdims=True)
        grad_hidden = gate * back
        grad_gate_pre = (grad_hidden * up_pre * slope).astype(half)
        grad_up_pre = (grad_hidden * activated).astype(half)
        grad_rows = (
            dot_t(grad_gate_pre, self.w_gate) + dot_t(grad_up_pre, self.w_up)
        ).astype(half)
        high, low = two_parts(grad_g)
        zero = jnp.zeros((), half)
        tail_out = jnp.where(lane == self.me, high, zero) + jnp.where(
            lane == self.me + tail.shape[1] // 2, low, zero
        )
        count = len(sources)
        home = jnp.einsum(
            "sct,scd->std",
            one_hot,
            jnp.concatenate([grad_rows, tail_out], axis=-1).reshape(count, self.capacity, -1),
            preferred_element_type=single,
        ).astype(half)
        return {
            "home": home,
            "one_hot": one_hot,
            "incoming": incoming,
            "hidden": hidden,
            "gate": gate,
            "ggp": grad_gate_pre,
            "gup": grad_up_pre,
            "back_rows": (gate * cot_rows.astype(single)).astype(half),
        }

    def run(self, m_low, gate_dense):
        rows, width = m_low.shape
        experts = gate_dense.shape[1]
        lanes = 64
        high, low = two_parts(gate_dense)
        fill = jnp.zeros((rows, lanes - experts), half)
        wide = jnp.concatenate([m_low, high, fill, low, fill], axis=1)
        done = []
        for step in self.ring.gather(wide):
            sources, pieces = [], []
            for offset, piece in step:
                sources.append(self.ring.index(offset))
                pieces.append(piece)
            for offset, piece in step:
                sources.append(self.ring.index(offset, 1))
                pieces.append(swap(piece, "ctx", 1))
            done.append(([offset for offset, piece in step], self.chunk(sources, pieces, width)))
        self.done = done

        def homes(name):
            kept = {}
            for offsets, out in done:
                for at, offset in enumerate(offsets):
                    kept[offset] = (out[name][at], out[name][at + len(offsets)])
            return kept

        def pick_from(kept):
            def pick(offset):
                own, other = kept[offset]
                return add(own, swap(other, "ctx", 1))

            return pick

        summed = self.ring.scatter(pick_from(homes("home")))
        grad_m = summed[:, :width]
        tail = summed[:, width:]
        grad_probs = tail[:, :experts] + tail[:, lanes : lanes + experts]

        def all_of(name):
            return jnp.concatenate([out[name] for offsets, out in done])

        incoming, hidden = all_of("incoming"), all_of("hidden")
        grads = (
            t_dot(incoming, all_of("ggp"))[None],
            t_dot(incoming, all_of("gup"))[None],
            t_dot(hidden, all_of("back_rows"))[None],
        )
        for offsets, out in done:
            produced = out["gate"] * dot(out["hidden"], self.w_down)
            count = 2 * len(offsets)
            out["mixed"] = jnp.einsum(
                "sct,scd->std",
                out["one_hot"],
                produced.astype(half).reshape(count, self.capacity, width),
                preferred_element_type=single,
            ).astype(half)
        mixed = self.ring.scatter(pick_from(homes("mixed")))
        return mixed, grad_m, grad_probs, grads


def on_device(
    tokens,
    w_query,
    w_key,
    w_value,
    w_output,
    w_router,
    norm_gains,
    w_gate,
    w_up,
    w_down,
    routes,
    positions,
    lengths,
    cotangent,
):
    dp_count, ctx_count, expert_count = (
        lax.axis_size("dp"),
        lax.axis_size("ctx"),
        lax.axis_size("expert"),
    )
    world = ("dp", "ctx", "expert")
    ctx = lax.axis_index("ctx")
    row_count, width = tokens.shape[1:]
    head_size = width // HEADS
    head_count = HEADS // ctx_count
    factor = head_size ** (-0.5)
    share = w_query.shape[0]
    own_width = width // ctx_count
    expert_total = w_router.shape[1]
    picks = routes[0]
    top = picks.shape[1]
    capacity = 5 * row_count * top // (4 * expert_total)
    all_rows = row_count * ctx_count
    cot = cotangent[0].astype(single)

    packed = jnp.concatenate(
        [w_router.reshape(-1), norm_gains.reshape(-1), picks.astype(half).reshape(-1)]
    )
    packed_size = packed.shape[0]
    packed = jnp.pad(packed, (0, -packed_size % 1024)).reshape(1, -1, 128)
    packed = doubling_gather(packed, world).reshape(dp_count * ctx_count * expert_count, -1)
    router_size, gain_size = share * expert_total, 4 * share
    router_w = packed[:, :router_size].reshape(width, expert_total)
    gains = packed[:, router_size : router_size + gain_size].reshape(-1, 4, share)
    gains = gains.transpose(1, 0, 2).reshape(4, width).astype(single)
    routes_all = packed[:, router_size + gain_size : packed_size]
    routes_all = routes_all.reshape(dp_count, -1, row_count, top)[lax.axis_index("dp")]

    def own_features(values):
        shaped = values.reshape(values.shape[:-1] + (dp_count, ctx_count, -1))
        return lax.dynamic_index_in_dim(shaped, ctx, values.ndim, keepdims=False).reshape(
            values.shape[:-1] + (own_width,)
        )

    pair_ring = Ring(("dp", "expert"), 1)
    shards = jnp.stack([w_query, w_key, w_value], axis=1).reshape(
        share, 3, dp_count, ctx_count, -1
    )

    def columns_for(j):
        return lax.dynamic_index_in_dim(shards, ctx ^ j, 3, keepdims=False).reshape(share, -1)

    blocks = [columns_for(0)]
    for j in range(1, ctx_count):
        blocks.append(swap(columns_for(j), "ctx", j))
    blocks = jnp.stack(blocks)[ctx ^ jnp.arange(ctx_count)]
    qkv_w = pair_ring.gather_flat(blocks.reshape(ctx_count * share, -1))
    qkv_w = qkv_w.reshape(dp_count, expert_count, ctx_count, share, -1).transpose(0, 2, 1, 3, 4)
    qkv_w = qkv_w.reshape(width, 3 * own_width)
    output_w = lax.all_gather(w_output, ("dp", "expert"), axis=0, tiled=True)

    x_all = xor_gather(tokens[0], "ctx").astype(single)
    all_pos = positions[0].reshape(ctx_count, row_count)[ctx ^ jnp.arange(ctx_count)].reshape(-1)
    inverse_a = inverse_rms(x_all)
    normed_a = x_all * inverse_a
    a_low = (normed_a * gains[0]).astype(half)
    qkv = dot(a_low, qkv_w)
    q_raw, k_raw = qkv[:, :own_width], qkv[:, own_width : 2 * own_width]
    v_low = qkv[:, 2 * own_width :].astype(half)
    squares = jnp.stack([jnp.sum(q_raw * q_raw, axis=-1), jnp.sum(k_raw * k_raw, axis=-1)])
    inverse = lax.rsqrt(xor_sum(squares, "ctx") / width + epsilon)
    inverse_q, inverse_k = inverse[0][:, None], inverse[1][:, None]
    normed_q, normed_k = q_raw * inverse_q, k_raw * inverse_k
    gain_q, gain_k = own_features(gains[1]), own_features(gains[2])
    cosine, sine = rope_tables(all_pos, head_size)
    q_low = rotate(normed_q * gain_q, cosine, sine, head_size).astype(half)
    k_low = rotate(normed_k * gain_k, cosine, sine, head_size).astype(half)

    def heads(values):
        return values.reshape(all_rows, head_count, head_size)

    if expert_total <= 16:
        layer = ExpertsByRing(routes_all, cotangent[0], w_gate, w_up, w_down, capacity)

    allowed = (all_pos[None, :] <= all_pos[:, None]) & (all_pos[None, :] < lengths[0])

    def all_scores():
        return (
            jnp.einsum("qhd,khd->hqk", heads(q_low), heads(k_low), preferred_element_type=single)
            * factor
        )

    scores = jnp.where(allowed[None], all_scores(), -1e30)
    top_score = jnp.max(scores, axis=-1)
    weights = jnp.where(allowed[None], jnp.exp(scores - top_score[..., None]), 0.0)
    total = jnp.sum(weights, axis=-1)
    log_total = top_score + jnp.log(total)
    attended = jnp.einsum(
        "hqk,khd->qhd", weights.astype(half), heads(v_low), preferred_element_type=single
    )
    attended = (attended / total.T[:, :, None]).reshape(all_rows, own_width)
    attended_low = attended.astype(half)
    start_x = tokens[0].astype(single)
    first = start_x + xor_scatter(dot(attended_low, output_w), "ctx")
    inverse_m = inverse_rms(first)
    normed_m = first * inverse_m
    m_low = (normed_m * gains[3]).astype(half)
    router_probs = jax.nn.softmax(dot(m_low, router_w), axis=-1)
    chosen = picks[..., None] == jnp.arange(expert_total)[None, None, :]
    if expert_total <= 16:
        gate_dense = jnp.where(jnp.any(chosen, axis=1), router_probs, 0.0)
        added, grad_m, grad_probs, expert_grads = layer.run(m_low, gate_dense)
    else:
        gates = jnp.sum(jnp.where(chosen, router_probs[:, None, :], 0.0), axis=-1)
        added, grad_m, grad_probs, expert_grads = experts_by_trade(
            m_low, gates, cot, picks, w_gate, w_up, w_down, expert_total, capacity
        )
    mixed = first + added
    expert_sums = [both_halves(grad) for grad in expert_grads]

    grad_logits = router_probs * (
        grad_probs - jnp.sum(router_probs * grad_probs, axis=-1, keepdims=True)
    )
    grad_logits_low = grad_logits.astype(half)
    grad_router = t_dot(m_low, grad_logits_low)
    grad_m = grad_m + dot_t(grad_logits_low, router_w)
    grad_gain_m = jnp.sum(grad_m * normed_m, axis=0)
    grad_normed = grad_m * gains[3]
    grad_first = cot + inverse_m * (
        grad_normed - normed_m * jnp.mean(grad_normed * normed_m, axis=-1, keepdims=True)
    )
    grad_attn = xor_gather(grad_first.astype(half), "ctx")
    grad_output = t_dot(attended_low, grad_attn)
    grad_o = dot_t(grad_attn, output_w).astype(half)
    delta = jnp.sum(heads(grad_o).astype(single) * heads(attended), axis=-1)
    probs = jnp.where(allowed[None], jnp.exp(all_scores() - log_total[..., None]), 0.0)
    grad_probs_attn = jnp.einsum(
        "qhd,khd->hqk", heads(grad_o), heads(v_low), preferred_element_type=single
    )
    grad_scores = (probs * (grad_probs_attn - delta.T[..., None])).astype(half)
    grad_q = (
        jnp.einsum("hqk,khd->qhd", grad_scores, heads(k_low), preferred_element_type=single)
        * factor
    ).reshape(all_rows, own_width)
    grad_k = (
        jnp.einsum("hqk,qhd->khd", grad_scores, heads(q_low), preferred_element_type=single)
        * factor
    ).reshape(all_rows, own_width)
    grad_v = jnp.einsum(
        "hqk,qhd->khd", probs.astype(half), heads(grad_o), preferred_element_type=single
    ).reshape(all_rows, own_width)
    turned_q = rotate(grad_q, cosine, -sine, head_size)
    turned_k = rotate(grad_k, cosine, -sine, head_size)
    grad_gain_q = jnp.sum(turned_q * normed_q, axis=0)
    grad_gain_k = jnp.sum(turned_k * normed_k, axis=0)
    grad_nq, grad_nk = turned_q * gain_q, turned_k * gain_k
    means = (
        xor_sum(
            jnp.stack([jnp.sum(grad_nq * normed_q, axis=-1), jnp.sum(grad_nk * normed_k, axis=-1)]),
            "ctx",
        )
        / width
    )
    grad_q_raw = inverse_q * (grad_nq - normed_q * means[0][:, None])
    grad_k_raw = inverse_k * (grad_nk - normed_k * means[1][:, None])
    grad_qkv = jnp.concatenate(
        [grad_q_raw.astype(half), grad_k_raw.astype(half), grad_v.astype(half)], axis=1
    )
    grad_a_part = dot_t(grad_qkv, qkv_w)
    grad_gain_a = jnp.sum(grad_a_part * normed_a, axis=0)
    grad_a = xor_scatter(grad_a_part, "ctx")
    grad_normed = grad_a * gains[0]
    normed_own = normed_a[:row_count]
    grad_x = grad_first + inverse_a[:row_count] * (
        grad_normed - normed_own * jnp.mean(grad_normed * normed_own, axis=-1, keepdims=True)
    )

    grad_qkv_w = t_dot(a_low, grad_qkv).astype(half)
    grad_qkv_w = grad_qkv_w.reshape(dp_count, ctx_count, expert_count, share, -1)
    grad_qkv_w = grad_qkv_w.transpose(0, 2, 1, 3, 4).reshape(
        dp_count * expert_count, ctx_count * share, -1
    )

    def part(offset):
        return lax.dynamic_index_in_dim(grad_qkv_w, pair_ring.index(offset), 0, keepdims=False)

    own_part = pair_ring.scatter(part).reshape(ctx_count, share, -1)
    low_part = own_part.astype(half)
    pieces = [lax.dynamic_index_in_dim(own_part, ctx, 0, keepdims=False)]
    for j in range(1, ctx_count):
        mine = lax.dynamic_index_in_dim(low_part, ctx ^ j, 0, keepdims=False)
        pieces.append(swap(mine, "ctx", j).astype(single))
    whole = jnp.stack(pieces)[ctx ^ jnp.arange(ctx_count)]
    whole = whole.reshape(ctx_count, share, 3, dp_count, -1).transpose(2, 1, 3, 0, 4)
    whole = whole.reshape(3, share, width)
    output_share = lax.psum_scatter(
        grad_output.astype(half), ("dp", "expert"), scatter_dimension=0, tiled=True
    ).astype(single)

    def spread(values):
        shaped = jnp.zeros((dp_count, ctx_count, own_width // dp_count), single)
        return lax.dynamic_update_index_in_dim(
            shaped, values.reshape(dp_count, -1), ctx, 1
        ).reshape(-1)

    gain_terms = jnp.stack(
        [grad_gain_a, spread(grad_gain_q), spread(grad_gain_k), grad_gain_m], axis=1
    )
    small = halving_scatter(jnp.concatenate([grad_router, gain_terms], axis=1), world)
    return (
        mixed.astype(half)[None],
        grad_x[None],
        whole[0],
        whole[1],
        whole[2],
        output_share,
        small[:, :expert_total],
        small[:, expert_total:].T,
        expert_sums[0],
        expert_sums[1],
        expert_sums[2],
    )


def solution(mesh):
    rows = P(("dp", "expert"), "ctx", None)
    shares = P(("dp", "ctx", "expert"), None)
    experts = P(("ctx", "expert"), None, None)
    gains = P(None, ("dp", "ctx", "expert"))
    return jax.shard_map(
        on_device,
        mesh=mesh,
        in_specs=(
            (rows,)
            + (shares,) * 5
            + (gains,)
            + (experts,) * 3
            + (rows, P(("dp", "expert"), None), P(("dp", "expert")), rows)
        ),
        out_specs=(rows, rows) + (shares,) * 5 + (gains,) + (experts,) * 3,
        check_vma=False,
    )
```

```python
import functools
import math

import jax
import jax.numpy as jnp
import numpy as np
from jax import lax
from jax.experimental import pallas as pl
from jax.experimental.pallas import tpu as pltpu
from jax.sharding import PartitionSpec as P

HEADS = 16

epsilon = 1e-05
rope_base = 10000.0
single = jnp.float32
half = jnp.bfloat16


def dot(left, right):
    return jnp.dot(left, right, preferred_element_type=single)


def dot_t(left, right):
    return lax.dot_general(left, right, (((1,), (1,)), ((), ())), preferred_element_type=single)


def t_dot(left, right):
    return lax.dot_general(left, right, (((0,), (0,)), ((), ())), preferred_element_type=single)


def inverse_rms(values):
    return lax.rsqrt(jnp.mean(values * values, axis=-1, keepdims=True) + epsilon)


def rope_tables(where, head_size):
    half_size = head_size // 2
    frequency = rope_base ** (-2.0 * jnp.arange(half_size, dtype=single) / head_size)
    angles = where.astype(single)[:, None] * frequency[None, :]
    angles = jnp.concatenate([angles, angles], axis=-1)
    return (jnp.cos(angles), jnp.sin(angles))


def rotate(values, cosine, sine, head_size):
    shaped = values.reshape(values.shape[0], -1, head_size)
    half_size = head_size // 2
    turned = jnp.concatenate([-shaped[..., half_size:], shaped[..., :half_size]], axis=-1)
    return (shaped * cosine[:, None, :] + turned * sine[:, None, :]).reshape(values.shape)


in_hbm = pl.BlockSpec(memory_space=pltpu.HBM)


def nothing(*refs):
    pass


def after(values, tokens, mebibytes=60):
    count = len(values)
    anywhere = pl.BlockSpec(memory_space=pl.ANY)
    specs = [in_hbm if v.size > 1 << 20 else anywhere for v in values]
    out = pl.pallas_call(
        nothing,
        out_shape=[jax.ShapeDtypeStruct(v.shape, v.dtype) for v in values],
        in_specs=specs + [anywhere] * len(tokens),
        out_specs=specs,
        input_output_aliases={i: i for i in range(count)},
        compiler_params=params(mebibytes),
        name="after",
    )(*values, *tokens)
    return list(out)


def params(mebibytes=48):
    return pltpu.CompilerParams(vmem_limit_bytes=mebibytes << 20)


def turn(values, cosine, sine):
    return values * cosine + pltpu.roll(values, values.shape[-1] // 2, 1) * sine


def rope_kernel(heads, qkv, inverse, cosine, sine, gains, q_out, k_out, v_out):
    width = q_out.shape[1]
    size = width // heads
    for at, out in enumerate((q_out, k_out)):
        scale = inverse[:, at : at + 1]
        for head in range(heads):
            cut = slice(head * size, (head + 1) * size)
            raw = qkv[:, at * width + head * size : at * width + (head + 1) * size]
            normed = raw * scale * gains[at : at + 1, cut]
            out[:, cut] = turn(normed, cosine[...], sine[...]).astype(half)
    v_out[...] = qkv[:, 2 * width :].astype(half)


def rope_forward(qkv, inverse, cosine, sine, gains, heads):
    rows, width = qkv.shape[0], qkv.shape[1] // 3
    block = math.gcd(rows, 256)

    def spec(columns):
        return pl.BlockSpec((block, columns), lambda i: (i, 0))

    size = width // heads
    return pl.pallas_call(
        functools.partial(rope_kernel, heads),
        grid=(rows // block,),
        in_specs=[spec(3 * width), spec(2), spec(size), spec(size)]
        + [pl.BlockSpec((2, width), lambda i: (0, 0))],
        out_specs=[spec(width)] * 3,
        out_shape=[jax.ShapeDtypeStruct((rows, width), half)] * 3,
        compiler_params=params(48),
        name="rope_forward",
    )(qkv, inverse, cosine, sine, gains)


def rope_back_kernel(heads, dq, dk, qkv, inverse, cosine, sine, gains, grad_n, sums, grad_gain):
    width = dq.shape[1]
    size = width // heads
    first = pl.program_id(0) == 0
    for at, grad in enumerate((dq, dk)):
        scale = inverse[:, at : at + 1]
        total = jnp.zeros((dq.shape[0], 1), single)
        for head in range(heads):
            cut = slice(head * size, (head + 1) * size)
            wide = slice(at * width + head * size, at * width + (head + 1) * size)
            turned = turn(grad[:, cut], cosine[...], -sine[...])
            normed = qkv[:, wide] * scale
            gained = jnp.sum(turned * normed, axis=0, keepdims=True)
            grad_gain[at : at + 1, cut] = gained + jnp.where(
                first, jnp.zeros_like(gained), grad_gain[at : at + 1, cut]
            )
            out = turned * gains[at : at + 1, cut]
            grad_n[:, wide] = out
            total = total + jnp.sum(out * normed, axis=-1, keepdims=True)
        sums[:, at : at + 1] = total


def rope_back(dq, dk, qkv, inverse, cosine, sine, gains, heads):
    rows, width = dq.shape
    block = math.gcd(rows, 256)

    def spec(columns):
        return pl.BlockSpec((block, columns), lambda i: (i, 0))

    size = width // heads
    fixed = pl.BlockSpec((2, width), lambda i: (0, 0))
    return pl.pallas_call(
        functools.partial(rope_back_kernel, heads),
        grid=(rows // block,),
        in_specs=[spec(width), spec(width), spec(2 * width), spec(2), spec(size), spec(size), fixed],
        out_specs=[spec(2 * width), spec(2), fixed],
        out_shape=[
            jax.ShapeDtypeStruct((rows, 2 * width), single),
            jax.ShapeDtypeStruct((rows, 2), single),
            jax.ShapeDtypeStruct((2, width), single),
        ],
        compiler_params=params(48),
        name="rope_back",
    )(dq, dk, qkv, inverse, cosine, sine, gains)


def norm_back_kernel(grad_n, qkv, inverse, means, dv, out):
    width = dv.shape[1]
    for at in range(2):
        cut = slice(at * width, (at + 1) * width)
        scale = inverse[:, at : at + 1]
        normed = qkv[:, cut] * scale
        out[:, cut] = (scale * (grad_n[:, cut] - normed * means[:, at : at + 1])).astype(half)
    out[:, 2 * width :] = dv[...].astype(half)


def norm_back(grad_n, qkv, inverse, means, dv):
    rows, width = dv.shape
    block = math.gcd(rows, 256)

    def spec(columns):
        return pl.BlockSpec((block, columns), lambda i: (i, 0))

    return pl.pallas_call(
        norm_back_kernel,
        grid=(rows // block,),
        in_specs=[spec(2 * width), spec(2 * width), spec(2), spec(2), spec(width)],
        out_specs=spec(3 * width),
        out_shape=jax.ShapeDtypeStruct((rows, 3 * width), half),
        compiler_params=params(48),
        name="norm_back",
    )(grad_n, qkv, inverse, means, dv)


def attend_kernel(factor, q, k, v, query_pos, key_pos, out, log_total):
    scores = dot_t(q[...], k[...]) * factor
    allowed = key_pos[...] <= query_pos[...]
    scores = jnp.where(allowed, scores, -1e30)
    top = jnp.max(scores, axis=-1, keepdims=True)
    weights = jnp.exp(scores - top)
    total = jnp.sum(weights, axis=-1, keepdims=True)
    log_total[0] = top + jnp.log(total)
    out[...] = (dot(weights.astype(half), v[...]) / total).astype(half)


def attend(q, k, v, query_pos, key_pos, heads):
    rows, width = q.shape
    size = width // heads
    block = math.gcd(rows, 512)
    some = pl.BlockSpec((block, size), lambda h, i: (i, h))
    every = pl.BlockSpec((rows, size), lambda h, i: (0, h))
    return pl.pallas_call(
        functools.partial(attend_kernel, size ** (-0.5)),
        grid=(heads, rows // block),
        in_specs=[
            some,
            every,
            every,
            pl.BlockSpec((block, 1), lambda h, i: (i, 0)),
            pl.BlockSpec((1, rows), lambda h, i: (0, 0)),
        ],
        out_specs=[some, pl.BlockSpec((1, block, 1), lambda h, i: (h, i, 0))],
        out_shape=[
            jax.ShapeDtypeStruct((rows, width), half),
            jax.ShapeDtypeStruct((heads, rows, 1), single),
        ],
        compiler_params=params(48),
        name="attend",
    )(q, k, v, query_pos, key_pos)


def attend_back_kernel(factor, q, k, v, grad_o, log_total, query_pos, key_pos, dq, dk, dv):
    scores = dot_t(q[...], k[...]) * factor
    allowed = key_pos[...] <= query_pos[...]
    probs = jnp.where(allowed, jnp.exp(scores - log_total[0]), 0.0)
    grad_probs = dot_t(grad_o[...], v[...])
    product = probs * grad_probs
    delta = jnp.sum(product, axis=-1, keepdims=True)
    grad_scores = (product - probs * delta).astype(half)
    dq[...] = dot(grad_scores, k[...]) * factor
    added_k = t_dot(grad_scores, q[...]) * factor
    added_v = t_dot(probs.astype(half), grad_o[...])

    @pl.when(pl.program_id(1) == 0)
    def first():
        dk[...] = added_k
        dv[...] = added_v

    @pl.when(pl.program_id(1) > 0)
    def later():
        dk[...] += added_k
        dv[...] += added_v


def attend_back(q, k, v, grad_o, log_total, query_pos, key_pos, heads):
    rows, width = q.shape
    size = width // heads
    block = math.gcd(rows, 512)
    some = pl.BlockSpec((block, size), lambda h, i: (i, h))
    every = pl.BlockSpec((rows, size), lambda h, i: (0, h))
    return pl.pallas_call(
        functools.partial(attend_back_kernel, size ** (-0.5)),
        grid=(heads, rows // block),
        in_specs=[
            some,
            every,
            every,
            some,
            pl.BlockSpec((1, block, 1), lambda h, i: (h, i, 0)),
            pl.BlockSpec((block, 1), lambda h, i: (i, 0)),
            pl.BlockSpec((1, rows), lambda h, i: (0, 0)),
        ],
        out_specs=[some, every, every],
        out_shape=[jax.ShapeDtypeStruct((rows, width), single)] * 3,
        compiler_params=params(48),
        name="attend_back",
    )(q, k, v, grad_o, log_total, query_pos, key_pos)


def chosen_rows(slot, capacity):
    places = lax.broadcasted_iota(jnp.int32, (capacity, slot.shape[-1]), 0)
    return jnp.where(places == slot, 1.0, 0.0).astype(half)


def empty(tag, shape, dtype):
    return pl.pallas_call(
        nothing,
        out_shape=jax.ShapeDtypeStruct(shape, dtype),
        out_specs=in_hbm,
        compiler_params=params(60),
        name="empty_" + tag,
    )()


def place_kernel(count, width, coords, *refs):
    pieces = refs[:count]
    qkv_out, output_out, sem = refs[count + 2 :]
    blocks = pieces[0].shape[0]
    cut = output_out.shape[2] // blocks
    copies = []

    def move(source, target):
        copy = pltpu.make_async_copy(source, target, sem.at[len(copies)])
        copy.start()
        copies.append(copy)

    for at, piece in enumerate(pieces):
        outer, inner, flat = coords[3 * at], coords[3 * at + 1], coords[3 * at + 2]
        move(piece.at[:, :, pl.ds(0, width)], qkv_out.at[outer, :, inner])
        for block in range(blocks):
            move(
                piece.at[block, :, pl.ds(width, cut)],
                output_out.at[flat, :, pl.ds(block * cut, cut)],
            )
    for copy in copies:
        copy.wait()


def place_units(coords, pieces, qkv_w, output_w):
    count, blocks = len(pieces), pieces[0].shape[0]
    return pl.pallas_call(
        functools.partial(place_kernel, count, qkv_w.shape[-1]),
        in_specs=[pl.BlockSpec(memory_space=pltpu.SMEM)]
        + [pl.BlockSpec(memory_space=pltpu.VMEM)] * count
        + [in_hbm] * 2,
        out_specs=[in_hbm] * 2,
        out_shape=[jax.ShapeDtypeStruct(v.shape, v.dtype) for v in (qkv_w, output_w)],
        compiler_params=params(60),
        scratch_shapes=[pltpu.SemaphoreType.DMA((count * (blocks + 1),))],
        input_output_aliases={count + 1: 0, count + 2: 1},
        name="place_units",
    )(coords, *pieces, qkv_w, output_w)


def units_kernel(coords, qkv_w, output_w, small, *refs):
    outs, sem = refs[:-1], refs[-1]
    blocks, width = qkv_w.shape[1], qkv_w.shape[-1]
    cut = output_w.shape[2] // blocks
    copies = []

    def move(source, target):
        copy = pltpu.make_async_copy(source, target, sem.at[len(copies)])
        copy.start()
        copies.append(copy)

    for at, out in enumerate(outs):
        unit = min(at, len(outs) - 2)
        held = out.shape[0]
        first = blocks - held if at == len(outs) - 1 else 0
        some = pl.ds(first, held)
        outer, inner, flat = (coords[3 * unit + k] for k in range(3))
        move(qkv_w.at[outer, some, inner], out.at[:, :, pl.ds(0, width)])
        move(small.at[outer, some, inner], out.at[:, :, pl.ds(width + cut, small.shape[-1])])
        for block in range(first, first + held):
            move(
                output_w.at[flat, :, pl.ds(block * cut, cut)],
                out.at[block - first, :, pl.ds(width, cut)],
            )
    for copy in copies:
        copy.wait()


def take_units(coords, qkv_w, output_w, small):
    count, blocks, share = coords.shape[0] // 3, qkv_w.shape[1], qkv_w.shape[3]
    width = qkv_w.shape[-1] + output_w.shape[2] // blocks + small.shape[-1]
    held = [blocks] * (count - 1) + [blocks // 2] * 2
    return pl.pallas_call(
        units_kernel,
        in_specs=[pl.BlockSpec(memory_space=pltpu.SMEM)] + [in_hbm] * 3,
        out_specs=[pl.BlockSpec(memory_space=pltpu.VMEM)] * len(held),
        out_shape=[jax.ShapeDtypeStruct((some, share, width), half) for some in held],
        compiler_params=params(60),
        scratch_shapes=[pltpu.SemaphoreType.DMA((len(held) * (blocks + 2),))],
        name="take_units",
    )(coords, qkv_w, output_w, small)


def product_kernel(kind, left, right, out):
    form = {"nn": dot, "nt": dot_t, "tn": t_dot}[kind]
    out[...] = form(left[...], right[...]).astype(out.dtype)


def product(kind, left, right, dtype, block=512):
    rows = left.shape[kind == "tn"]
    depth = left.shape[kind != "tn"]
    columns = right.shape[kind != "nt"]
    block = math.gcd(rows, block)
    some = (
        pl.BlockSpec((depth, block), lambda i: (0, i))
        if kind == "tn"
        else pl.BlockSpec((block, depth), lambda i: (i, 0))
    )
    return pl.pallas_call(
        functools.partial(product_kernel, kind),
        grid=(rows // block,),
        in_specs=[some, pl.BlockSpec(right.shape, lambda i: (0, 0))],
        out_specs=pl.BlockSpec((block, columns), lambda i: (i, 0)),
        out_shape=jax.ShapeDtypeStruct((rows, columns), dtype),
        compiler_params=params(56),
        name="product_" + kind,
    )(left, right)


def weights_kernel(left, right, weight, out, gained):
    grad = t_dot(left[...], right[...])
    out[...] = grad.astype(half)
    gained[...] = jnp.sum(grad * weight[...].astype(single), axis=-1, keepdims=True)


def weight_gradients(left, right, weight):
    depth, rows = left.shape
    columns = right.shape[1]
    block = math.gcd(rows, 512)
    part = pl.BlockSpec((block, columns), lambda i: (i, 0))
    return pl.pallas_call(
        weights_kernel,
        grid=(rows // block,),
        in_specs=[
            pl.BlockSpec((depth, block), lambda i: (0, i)),
            pl.BlockSpec((depth, columns), lambda i: (0, 0)),
            part,
        ],
        out_specs=[part, pl.BlockSpec((block, 1), lambda i: (i, 0))],
        out_shape=[
            jax.ShapeDtypeStruct((rows, columns), half),
            jax.ShapeDtypeStruct((rows, 1), single),
        ],
        compiler_params=params(56),
        name="weight_gradients",
    )(left, right, weight)


def norm_kernel(x, gain, out, inverse):
    values = x[...].astype(single)
    scale = inverse_rms(values)
    inverse[...] = scale
    out[...] = (values * scale * gain[...]).astype(half)


def norm_rows(x, gain):
    rows, width = x.shape
    block = math.gcd(rows, 256)
    part = pl.BlockSpec((block, width), lambda i: (i, 0))
    return pl.pallas_call(
        norm_kernel,
        grid=(rows // block,),
        in_specs=[part, pl.BlockSpec((1, width), lambda i: (0, 0))],
        out_specs=[part, pl.BlockSpec((block, 1), lambda i: (i, 0))],
        out_shape=[
            jax.ShapeDtypeStruct((rows, width), half),
            jax.ShapeDtypeStruct((rows, 1), single),
        ],
        compiler_params=params(56),
        name="norm_rows",
    )(x, gain)


def sum_kernel(own, got, out, token):
    out[...] = own[...].astype(single) + got[...].astype(single)
    token[...] = jnp.zeros_like(token)


def sum_up(own, got):
    rows, width = got.shape
    block = math.gcd(rows, 256)
    part = pl.BlockSpec((block, width), lambda i: (i, 0))
    return pl.pallas_call(
        sum_kernel,
        grid=(rows // block,),
        in_specs=[part, part],
        out_specs=[part, pl.BlockSpec((8, 128), lambda i: (0, 0))],
        out_shape=[
            jax.ShapeDtypeStruct(got.shape, single),
            jax.ShapeDtypeStruct((8, 128), single),
        ],
        compiler_params=params(60),
        name="sum_up",
    )(own, got)


def put_all_kernel(order, slot, rows, out):
    places = chosen_rows(slot[0], rows.shape[1])
    for col in range(0, out.shape[2], 512):
        cut = slice(col, col + 512)
        out[0, :, cut] = t_dot(places, rows[0, :, cut]).astype(half)


def put_all(order, slot, rows):
    count, capacity, width = rows.shape
    length = slot.shape[-1]
    return pl.pallas_call(
        put_all_kernel,
        grid_spec=pltpu.PrefetchScalarGridSpec(
            num_scalar_prefetch=1,
            grid=(count,),
            in_specs=[
                pl.BlockSpec((1, 1, length), lambda i, order: (i, 0, 0)),
                pl.BlockSpec((1, capacity, width), lambda i, order: (i, 0, 0)),
            ],
            out_specs=pl.BlockSpec((1, length, width), lambda i, order: (order[i], 0, 0)),
        ),
        out_shape=jax.ShapeDtypeStruct((count, length, width), half),
        compiler_params=params(60),
        cost_estimate=pl.CostEstimate(
            flops=0, bytes_accessed=8 * rows.size, transcendentals=0
        ),
        name="put_all",
    )(order, slot, rows)


TILE = 512


def pair_kernel(
    capacity,
    tail,
    order,
    slot,
    piece_a,
    piece_b,
    lanes,
    cot_all,
    gate_v,
    up_v,
    down_v,
    in_rows,
    in_hidden,
    in_gate,
    in_up,
    in_cot,
    home_a,
    home_b,
    all_rows,
    all_hidden,
    all_gate,
    all_up,
    all_cot,
    cot_v,
    cot_rows,
    rows,
    hidden,
    grad_gate,
    grad_up,
    load_sem,
    store_sem,
):
    width, inner = gate_v.shape
    start = order[2]
    loads, stores = [], []

    def load(source, target):
        copy = pltpu.make_async_copy(source, target, load_sem.at[len(loads)])
        copy.start()
        loads.append(copy)
        return copy

    def store(source, target):
        copy = pltpu.make_async_copy(source, target, store_sem.at[len(stores)])
        copy.start()
        stores.append(copy)

    span = pl.ds(pl.multiple_of(start * capacity, 32), 2 * capacity)
    get_cot = [load(cot_all.at[order[at]], cot_v.at[at]) for at in range(2)]
    homes, pieces = (home_a, home_b), (piece_a, piece_b)
    places = [chosen_rows(slot[at], capacity) for at in range(2)]
    parts = [slice(at * capacity, (at + 1) * capacity) for at in range(2)]
    gates = []
    for at in range(2):
        for col in range(0, width, TILE):
            cut = slice(col, col + TILE)
            rows[parts[at], cut] = dot(places[at], pieces[at][:, cut]).astype(half)
        picked = dot(places[at], pieces[at][:, width:])
        gates.append(jnp.sum(picked * lanes[...], axis=-1, keepdims=True))
    gate = jnp.concatenate(gates, axis=0)
    store(rows, all_rows.at[span])
    for at in range(2):
        get_cot[at].wait()
        for col in range(0, width, TILE):
            cut = slice(col, col + TILE)
            cot_rows[parts[at], cut] = dot(places[at], cot_v[at, :, cut]).astype(half)
    store(cot_rows, all_cot.at[span])
    grad_g = jnp.zeros((2 * capacity, 1), single)
    for col in range(0, inner, TILE):
        cut = slice(col, col + TILE)
        gate_pre = dot(rows[...], gate_v[:, cut])
        up_pre = dot(rows[...], up_v[:, cut])
        returned = dot_t(cot_rows[...], down_v[cut, :])
        activated, slope = activate(gate_pre, up_pre)
        kept = activated * up_pre
        hidden[:, cut] = (gate * kept).astype(half)
        grad_g = grad_g + jnp.sum(returned * kept, axis=-1, keepdims=True)
        grad_hidden = gate * returned
        grad_gate[:, cut] = (grad_hidden * up_pre * slope).astype(half)
        grad_up[:, cut] = (grad_hidden * activated).astype(half)
    store(hidden, all_hidden.at[span])
    store(grad_gate, all_gate.at[span])
    store(grad_up, all_up.at[span])
    for col in range(0, width, TILE):
        cut = slice(col, col + TILE)
        back = dot_t(grad_gate[...], gate_v[cut, :]) + dot_t(grad_up[...], up_v[cut, :])
        back = back.astype(half)
        for side in range(2):
            homes[side][:, cut] = t_dot(places[side], back[parts[side]]).astype(half)
    high = grad_g.astype(half).astype(single)
    ends = high * lanes[...] * tail[0:1] + (grad_g - high) * lanes[...] * tail[1:2]
    ends = ends.astype(half)
    for side in range(2):
        homes[side][:, width:] = t_dot(places[side], ends[parts[side]]).astype(half)
    for copy in stores:
        copy.wait()


def expert_pair(order, slot, pieces, lanes, tails, cot_all, weights, held, capacity):
    width, inner = weights[0].shape
    length, wide = pieces[0].shape
    in_vmem = pl.BlockSpec(memory_space=pltpu.VMEM)
    count = 2 * capacity

    def body(order, slot, a, b, lanes, tails, *refs):
        pair_kernel(capacity, tails, order, slot, a, b, lanes, *refs)

    out = pl.pallas_call(
        body,
        in_specs=[pl.BlockSpec(memory_space=pltpu.SMEM)]
        + [in_vmem] * 5
        + [in_hbm]
        + [in_vmem] * 3
        + [in_hbm] * 5,
        out_specs=[in_vmem] * 2 + [in_hbm] * 5,
        out_shape=[jax.ShapeDtypeStruct((length, wide), half)] * 2
        + [jax.ShapeDtypeStruct(value.shape, value.dtype) for value in held],
        scratch_shapes=[
            pltpu.VMEM((2, length, width), half),
            pltpu.VMEM((count, width), half),
            pltpu.VMEM((count, width), half),
            pltpu.VMEM((count, inner), half),
            pltpu.VMEM((count, inner), half),
            pltpu.VMEM((count, inner), half),
            pltpu.SemaphoreType.DMA((2,)),
            pltpu.SemaphoreType.DMA((5,)),
        ],
        input_output_aliases={10 + i: 2 + i for i in range(5)},
        compiler_params=params(34),
        name="expert_pair",
    )(order, slot, *pieces, lanes, tails, cot_all, *weights, *held)
    return out[:2], list(out[2:])


def swap(value, axis, bit):
    count = lax.axis_size(axis)
    return lax.ppermute(value, axis, [(i, i ^ bit) for i in range(count)])


def bits_down(count):
    bits = []
    bit = count // 2
    while bit >= 1:
        bits.append(bit)
        bit //= 2
    return bits


def xor_gather(value, axis, begun=None):
    blocks = {0: value}
    for bit in bits_down(lax.axis_size(axis)):
        held = sorted(blocks)
        if begun is not None and len(held) == 1:
            blocks[bit] = begun
            continue
        moved = swap(jnp.concatenate([blocks[j] for j in held], axis=0), axis, bit)
        for at, j in enumerate(held):
            blocks[j | bit] = moved[at * value.shape[0] : (at + 1) * value.shape[0]]
    return jnp.concatenate([blocks[j] for j in sorted(blocks)], axis=0)


def xor_scatter(value, axis):
    count = lax.axis_size(axis)
    rows = value.shape[0] // count
    held = value
    for bit in reversed(bits_down(count)):
        shaped = held.reshape(-1, 2, rows, held.shape[-1])
        got = swap(shaped[:, 1].astype(half), axis, bit)
        held = shaped[:, 0].astype(single) + got.astype(single)
        held = held.reshape(-1, held.shape[-1])
    return held


def xor_sum(value, axis):
    count = lax.axis_size(axis)
    blocks = value.reshape(-1, count, value.shape[-1] // count)
    for bit in reversed(bits_down(count)):
        got = swap(blocks, axis, bit)
        blocks = blocks + jnp.stack([got[:, j ^ bit] for j in range(count)], axis=1)
    return blocks.reshape(value.shape)


def doubling_gather(value, axes):
    for axis in reversed(axes):
        for bit in reversed(bits_down(lax.axis_size(axis))):
            other = swap(value, axis, bit)
            low = (lax.axis_index(axis) & bit) == 0
            value = jnp.concatenate(
                [jnp.where(low, value, other), jnp.where(low, other, value)], axis=0
            )
    return value


def halving_scatter(value, axes):
    for axis in axes:
        for bit in bits_down(lax.axis_size(axis)):
            rows = value.shape[0] // 2
            low = (lax.axis_index(axis) & bit) == 0
            kept = jnp.where(low, value[:rows], value[rows:])
            sent = jnp.where(low, value[rows:], value[:rows])
            value = kept + swap(sent, axis, bit)
    return value


def snake(outer, inner):
    order = []
    for a in range(outer):
        line = range(inner) if a % 2 == 0 else reversed(range(inner))
        order += [(a, b) for b in line]
    return order


class Ring:
    def __init__(self, axes, planes):
        outer, inner = lax.axis_size(axes[0]) // planes, lax.axis_size(axes[1])
        order = snake(outer, inner)
        self.axes, self.planes, self.count = axes, planes, len(order)
        flat = [[(a * planes + plane) * inner + b for a, b in order] for plane in range(planes)]
        self.forward, self.backward = [], []
        offsets = self.offsets()
        table = [None] * (self.count * planes)
        for plane, line in enumerate(flat):
            for at, index in enumerate(line):
                after = line[(at + 1) % self.count]
                self.forward.append((index, after))
                self.backward.append((after, index))
                table[index] = []
                for group in offsets:
                    for other in range(planes):
                        for offset in group:
                            table[index].append(flat[plane ^ other][(at + offset) % self.count])
        table = jnp.asarray(np.array(table, np.int32))
        self.order = lax.dynamic_slice(
            table,
            (lax.axis_index(axes), jnp.int32(0)),
            (1, table.shape[1]),
            allow_negative_indices=False,
        ).reshape(-1)

    def offsets(self):
        middle = self.count // 2
        return [[0]] + [[-step, step] for step in range(1, middle)] + [[middle]]

    def ahead(self, value):
        return lax.ppermute(value, self.axes, self.forward)

    def behind(self, value):
        return lax.ppermute(value, self.axes, self.backward)

    def gather(self, value, each, room=60):
        tokens = each(0, [value])
        split = value.shape[0] // 2
        from_back = from_front = value
        for step in range(1, self.count // 2):
            from_back, from_front = self.ahead(from_back), self.behind(from_front)
            if tokens:
                from_back, from_front = after([from_back, from_front], tokens, room)
            tokens = each(step, [from_back, from_front])
        last = jnp.concatenate(
            [self.ahead(from_back[:split]), self.behind(from_front[split:])], axis=0
        )
        if tokens:
            (last,) = after([last], tokens, room)
        each(self.count // 2, [last])

    def scatter(self, pick, between=None):
        middle = self.count // 2
        ahead, behind = pick(middle, 0), pick(middle, 1)
        split = ahead.shape[0]
        for step in range(middle - 1, 0, -1):
            tokens = between(step, [ahead, behind]) if between else []
            got_ahead, got_behind = self.ahead(ahead), self.behind(behind)
            own_ahead, own_behind = pick(step, 0), pick(step, 1)
            if tokens:
                own_ahead, own_behind = after([own_ahead, own_behind], tokens)
            if step == middle - 1:
                ahead = jnp.concatenate([add(own_ahead[:split], got_ahead), own_ahead[split:]])
                behind = jnp.concatenate([own_behind[:split], add(own_behind[split:], got_behind)])
            else:
                ahead, behind = add(own_ahead, got_ahead), add(own_behind, got_behind)
        tokens = between(0, [ahead, behind]) if between else []
        got_ahead, got_behind = self.ahead(ahead), self.behind(behind)
        own = pick(0, 0)
        if tokens:
            (own,) = after([own], tokens)
        return own.astype(single) + got_ahead.astype(single) + got_behind.astype(single)


def add(left, right):
    return (left.astype(single) + right.astype(single)).astype(half)


def trade(buffer):
    count = lax.axis_size("ctx") * lax.axis_size("expert")
    shaped = buffer.reshape(count, -1, buffer.shape[-1])
    moved = lax.all_to_all(shaped, ("ctx", "expert"), split_axis=0, concat_axis=0, tiled=True)
    return moved.reshape(buffer.shape)


def activate(gate_pre, up_pre):
    sigmoid = jax.nn.sigmoid(gate_pre)
    activated = gate_pre * sigmoid
    slope = sigmoid * (1.0 + gate_pre * (1.0 - sigmoid))
    return activated, slope


def experts_by_trade(m_low, gates, cot, picks, w_gate, w_up, w_down, expert_total, capacity):
    rows, width = m_low.shape
    top = picks.shape[1]
    locals_ = w_gate.shape[0]
    flat = (picks.reshape(-1)[:, None] == jnp.arange(expert_total)[None, :]).astype(jnp.int32)
    ranking = jnp.sum((jnp.cumsum(flat, axis=0) - 1) * flat, axis=1)
    slots = picks.reshape(-1) * capacity + ranking
    pair_rows = jnp.arange(rows * top) // top
    empty = jnp.zeros((expert_total * capacity, width), half)
    incoming = trade(empty.at[slots].set(m_low[pair_rows])).reshape(-1, locals_, capacity, width)

    def summed(form, left, right):
        return jnp.einsum(form, left, right, preferred_element_type=single)

    gate_pre = summed("sxcd,xdf->sxcf", incoming, w_gate)
    up_pre = summed("sxcd,xdf->sxcf", incoming, w_up)
    activated, slope = activate(gate_pre, up_pre)
    hidden = (activated * up_pre).astype(half)
    produced = summed("sxcf,xfd->sxcd", hidden, w_down).astype(half)
    returned = trade(produced.reshape(-1, width))
    picked = returned[slots].reshape(rows, top, width).astype(single)
    mixed = jnp.sum(gates[..., None] * picked, axis=1)
    grad_gates = jnp.sum(cot[:, None, :] * picked, axis=-1)
    back = (gates[..., None] * cot[:, None, :]).astype(half).reshape(-1, width)
    grad_in = trade(empty.at[slots].set(back)).reshape(-1, locals_, capacity, width)
    grad_hidden = summed("sxcd,xfd->sxcf", grad_in, w_down)
    grad_down = summed("sxcf,sxcd->xfd", hidden, grad_in)
    grad_gate_pre = (grad_hidden * up_pre * slope).astype(half)
    grad_up_pre = (grad_hidden * activated).astype(half)
    grad_gate = summed("sxcd,sxcf->xdf", incoming, grad_gate_pre)
    grad_up = summed("sxcd,sxcf->xdf", incoming, grad_up_pre)
    grad_rows = summed("sxcf,xdf->sxcd", grad_gate_pre, w_gate)
    grad_rows = (grad_rows + summed("sxcf,xdf->sxcd", grad_up_pre, w_up)).astype(half)
    grad_back = trade(grad_rows.reshape(-1, width))
    grad_m = jnp.sum(grad_back[slots].reshape(rows, top, width).astype(single), axis=1)
    chosen = picks[..., None] == jnp.arange(expert_total)[None, None, :]
    grad_probs = jnp.sum(jnp.where(chosen, grad_gates[..., None], 0.0), axis=1)
    return mixed, grad_m, grad_probs, [grad_down[0], grad_gate[0], grad_up[0]]


def two_parts(value):
    high = lax.reduce_precision(value, 8, 7)
    return high.astype(half), (value - high).astype(half)


def slots_of(routes_all):
    me = lax.axis_index(("ctx", "expert")).astype(routes_all.dtype)
    chosen = jnp.any(routes_all == me, axis=-1)
    rows = chosen.shape[1]
    before = (jnp.arange(rows)[:, None] <= jnp.arange(rows)[None, :]).astype(half)
    rank = dot(chosen.astype(half), before).astype(jnp.int32) - 1
    return jnp.where(chosen, rank, -1)


class ExpertsByRing:
    def __init__(self, slot, cot, w_gate, w_up, w_down, capacity):
        self.ring = Ring(("ctx", "expert"), 2)
        self.capacity = capacity
        self.weights = (w_gate[0], w_up[0], w_down[0])
        self.me = lax.axis_index(("ctx", "expert"))
        self.slot = slot[self.ring.order][:, None, :]
        cot_all = lax.all_gather(cot, ("ctx", "expert"), axis=0, tiled=True)
        self.cot_all = cot_all.reshape(slot.shape + cot.shape[-1:])

    def run(self, m_low, gate_dense, dp_sum):
        rows, width = m_low.shape
        inner = self.weights[0].shape[1]
        experts = gate_dense.shape[1]
        lanes = 64
        high, low = two_parts(gate_dense)
        fill = jnp.zeros((rows, lanes - experts), half)
        wide = jnp.concatenate([m_low, high, fill, low, fill], axis=1)
        lane = jnp.arange(2 * lanes)
        mine = (lane % lanes == self.me).astype(single)[None]
        tails = jnp.stack([lane < lanes, lane >= lanes]).astype(single)
        devices = self.slot.shape[0]
        total = devices * self.capacity
        held = [
            empty("rows", (total, width), half),
            empty("hidden", (total, inner), half),
            empty("gate", (total, inner), half),
            empty("up", (total, inner), half),
            empty("cot", (total, width), half),
        ]
        sums = []

        def pair(start, pieces):
            order = jnp.concatenate(
                [self.ring.order[start : start + 2], jnp.full((1,), start, jnp.int32)]
            )
            slot = self.slot[start : start + 2]
            homes, held[:] = expert_pair(
                order, slot, pieces, mine, tails, self.cot_all, self.weights, held, self.capacity
            )
            return homes

        def each(step, arrived):
            start = sum(2 * len(group) for group in self.ring.offsets()[:step])
            others = [swap(piece, "ctx", 1) for piece in arrived]
            if len(arrived) == 1:
                homes = pair(start, arrived + others)
                tokens = [homes[0]]
            else:
                homes = pair(start, arrived)
                tokens = [homes[0]]
                homes = homes + pair(start + 2, others)
            count = len(arrived)
            sums.append(
                [add(homes[at], swap(homes[at + count], "ctx", 1)) for at in range(count)]
            )
            return tokens

        self.ring.gather(wide, each, 1)
        incoming, hidden, gate, up, cot_rows = held
        grads = []
        work = [(hidden, cot_rows), (incoming, gate), (incoming, up)]

        def between(step, sent):
            if not work:
                return [] if step else dp_sum.arrived(0)
            left, right = work.pop(0)
            (right,) = after([right], sent)
            grads.append(product("tn", left, right, half))
            dp_sum.add(grads[-1])
            return grads[-1:]

        def pick(step, side):
            if step == len(sums) - 1:
                far = sums[step][0]
                split = far.shape[0] // 2
                return far[split:] if side else far[:split]
            return sums[step][-1 - side]

        summed = self.ring.scatter(pick, between)
        while work:
            between(0, [summed])
        grad_m = summed[:, :width]
        tail = summed[:, width:]
        grad_probs = tail[:, :experts] + tail[:, lanes : lanes + experts]
        self.hidden = hidden
        return grad_m, grad_probs

    def mixed(self, tokens):
        rows, width = self.slot.shape[-1], self.weights[0].shape[0]
        (hidden,) = after([self.hidden], tokens)
        produced = product("nn", hidden, self.weights[2], half, 320)
        return put_all(
            self.ring.order, self.slot, produced.reshape(-1, self.capacity, width)
        ).reshape(-1, width)


class DpSum:
    def __init__(self):
        self.two = lax.axis_size("dp") == 2
        self.grads, self.got, self.outs = [], [], {}

    def add(self, grad):
        self.grads.append(grad.astype(half))
        if self.two:
            self.got.append(swap(self.grads[-1], "dp", 1))

    def arrived(self, at):
        return self.got[at : at + 1]

    def finish(self, at):
        if self.two:
            self.outs[at], token = sum_up(self.grads[at], self.got[at])
            return [token]
        self.outs[at] = lax.psum(self.grads[at], "dp").astype(single)
        return []


def on_device(
    tokens,
    w_query,
    w_key,
    w_value,
    w_output,
    w_router,
    norm_gains,
    w_gate,
    w_up,
    w_down,
    routes,
    positions,
    lengths,
    cotangent,
):
    dp_count, ctx_count, expert_count = (
        lax.axis_size("dp"),
        lax.axis_size("ctx"),
        lax.axis_size("expert"),
    )
    world = ("dp", "ctx", "expert")
    ctx = lax.axis_index("ctx")
    row_count, width = tokens.shape[1:]
    head_size = width // HEADS
    head_count = HEADS // ctx_count
    share = w_query.shape[0]
    own_width = width // ctx_count
    expert_total = w_router.shape[1]
    picks = routes[0]
    top = picks.shape[1]
    capacity = 5 * row_count * top // (4 * expert_total)
    all_rows = row_count * ctx_count
    cot = cotangent[0].astype(single)

    packed = jnp.concatenate(
        [w_router.reshape(-1), norm_gains.reshape(-1), picks.astype(half).reshape(-1)]
    )
    packed_size = packed.shape[0]
    packed = jnp.pad(packed, (0, -packed_size % 1024)).reshape(1, -1, 128)
    router_size, gain_size = share * expert_total, 4 * share

    def own_features(values):
        shaped = values.reshape(values.shape[:-1] + (dp_count, ctx_count, -1))
        return lax.dynamic_index_in_dim(shaped, ctx, values.ndim, keepdims=False).reshape(
            values.shape[:-1] + (own_width,)
        )

    pair_ring = Ring(("dp", "expert"), 1)
    outer, inner = pair_ring.order // expert_count, pair_ring.order % expert_count
    coords = jnp.stack([outer, inner, pair_ring.order], axis=1).reshape(-1)
    shards = jnp.concatenate(
        [
            value.reshape(share, dp_count, ctx_count, -1)
            for value in (w_query, w_key, w_value)
        ],
        axis=1,
    )

    def columns_for(j):
        return lax.dynamic_index_in_dim(
            shards, ctx ^ j, 2, keepdims=False, allow_negative_indices=False
        ).reshape(share, -1)

    blocks = [columns_for(0)]
    for j in range(1, ctx_count):
        blocks.append(swap(columns_for(j), "ctx", j))
    by_ctx = ctx ^ jnp.arange(ctx_count)
    blocks = jnp.stack(blocks)[by_ctx].reshape(ctx_count * share, -1)
    output_blocks = [
        w_output[:, at * own_width : (at + 1) * own_width] for at in range(ctx_count)
    ]
    unit = jnp.concatenate([blocks, jnp.concatenate(output_blocks, axis=0)], axis=1)
    gathered = {
        "count": 0,
        "weights": (
            empty("qkv", (dp_count, ctx_count, expert_count, share, 3 * own_width), half),
            empty("output", (dp_count * expert_count, share, width), half),
        ),
    }

    def rows_ready(step, arrived):
        done = gathered["count"]
        gathered["count"] = done + len(arrived)
        gathered["weights"] = place_units(
            coords[3 * done : 3 * gathered["count"]],
            [piece.reshape(ctx_count, share, -1) for piece in arrived],
            *gathered["weights"],
        )
        result = list(gathered["weights"][1:])
        middle = pair_ring.count // 2
        if step == middle - 1:
            (gathered["cot"],) = after([cotangent[0]], arrived)
        if step == 1:
            (x_begun,) = after([gathered["x"]], arrived)
            gathered["x"] = xor_gather(tokens[0], "ctx", x_begun)
        if step == max(1, middle - 2):
            small = gathered["small"].reshape(dp_count * ctx_count * expert_count, -1)
            gathered["router"] = small[:, :router_size].reshape(width, expert_total)
            gains = small[:, router_size : router_size + gain_size].reshape(-1, 4, share)
            gathered["gains"] = gains.transpose(1, 0, 2).reshape(4, width).astype(single)
            routes_all = small[:, router_size + gain_size : packed_size]
            routes_all = routes_all.reshape(dp_count, -1, row_count, top)
            gathered["slot"] = slots_of(routes_all[lax.axis_index("dp")])
            gathered["a_low"], gathered["inverse_a"] = norm_rows(
                gathered["x"], gathered["gains"][:1]
            )
            result += [gathered["a_low"], cosine, sine, gathered["slot"]]
        return result

    all_pos = positions[0].reshape(ctx_count, row_count)[by_ctx].reshape(-1)
    cosine, sine = rope_tables(all_pos, head_size)
    sine = jnp.where(jnp.arange(head_size) < head_size // 2, -sine, sine)
    gathered["small"] = doubling_gather(packed, world)
    gathered["x"] = swap(tokens[0], "ctx", ctx_count // 2)
    (unit,) = after([unit], [gathered["small"]])
    pair_ring.gather(unit, rows_ready)
    gains, slot, router_w = gathered["gains"], gathered["slot"], gathered["router"]
    qkv_w, output_w = gathered["weights"]
    qkv_w = qkv_w.reshape(width, 3 * own_width)
    output_w = output_w.reshape(own_width, width)

    x_all = gathered["x"].astype(single)
    inverse_a, a_low = gathered["inverse_a"], gathered["a_low"]
    normed_a = x_all * inverse_a
    qkv = product("nn", a_low, qkv_w, single, 256)
    q_raw, k_raw = qkv[:, :own_width], qkv[:, own_width : 2 * own_width]
    squares = jnp.stack([jnp.sum(q_raw * q_raw, axis=-1), jnp.sum(k_raw * k_raw, axis=-1)])
    inverse = lax.rsqrt(xor_sum(squares, "ctx") / width + epsilon).T
    gains_qk = jnp.stack([own_features(gains[1]), own_features(gains[2])])
    q_low, k_low, v_low = rope_forward(qkv, inverse, cosine, sine, gains_qk, head_count)

    if expert_total <= 16:
        layer = ExpertsByRing(slot, gathered["cot"], w_gate, w_up, w_down, capacity)

    query_pos = all_pos[:, None]
    key_pos = jnp.where(all_pos < lengths[0], all_pos, 1 << 30)[None, :]
    attended_low, log_total = attend(q_low, k_low, v_low, query_pos, key_pos, head_count)
    first = tokens[0].astype(single) + xor_scatter(product("nn", attended_low, output_w, half, 256), "ctx")
    inverse_m = inverse_rms(first)
    normed_m = first * inverse_m
    m_low = (normed_m * gains[3]).astype(half)
    router_probs = jax.nn.softmax(dot(m_low, router_w), axis=-1)
    chosen = picks[..., None] == jnp.arange(expert_total)[None, None, :]
    dp_sum = DpSum()
    if expert_total <= 16:
        gate_dense = jnp.where(jnp.any(chosen, axis=1), router_probs, 0.0)
        grad_m, grad_probs = layer.run(m_low, gate_dense, dp_sum)
    else:
        gates = jnp.sum(jnp.where(chosen, router_probs[:, None, :], 0.0), axis=-1)
        added, grad_m, grad_probs, expert_grads = experts_by_trade(
            m_low, gates, cot, picks, w_gate, w_up, w_down, expert_total, capacity
        )
        for grad in expert_grads:
            dp_sum.add(grad)
    grad_logits = router_probs * (
        grad_probs - jnp.sum(router_probs * grad_probs, axis=-1, keepdims=True)
    )
    grad_logits_low = grad_logits.astype(half)
    grad_router = t_dot(m_low, grad_logits_low)
    grad_m = grad_m + dot_t(grad_logits_low, router_w)
    grad_gain_m = jnp.sum(grad_m * normed_m, axis=0)
    grad_normed = grad_m * gains[3]
    grad_first = cot + inverse_m * (
        grad_normed - normed_m * jnp.mean(grad_normed * normed_m, axis=-1, keepdims=True)
    )
    grad_first_low = grad_first.astype(half)
    begun = swap(grad_first_low, "ctx", ctx_count // 2)
    if expert_total <= 16:
        added = layer.mixed([grad_first_low])
        (begun,) = after([begun], [added])
        added = lax.psum_scatter(added, ("ctx", "expert"), scatter_dimension=0, tiled=True)
    grad_attn = xor_gather(grad_first_low, "ctx", begun)
    grad_output = product("tn", attended_low, grad_attn, half, 256)
    grad_o = product("nt", grad_attn, output_w, half, 256)
    (grad_o,) = after([grad_o], dp_sum.arrived(1))
    dq, dk, dv = attend_back(
        q_low, k_low, v_low, grad_o, log_total, query_pos, key_pos, head_count
    )
    grad_n, sums, grad_gain_qk = rope_back(
        dq, dk, qkv, inverse, cosine, sine, gains_qk, head_count
    )
    means = (xor_sum(sums.T, "ctx") / width).T
    grad_qkv = norm_back(grad_n, qkv, inverse, means, dv)
    grad_qkv_w, grad_gain_a = weight_gradients(a_low, grad_qkv, qkv_w)
    grad_gain_a = grad_gain_a[:, 0] / gains[0]

    def spread(values):
        shaped = jnp.zeros((dp_count, ctx_count, own_width // dp_count), single)
        return lax.dynamic_update_index_in_dim(
            shaped, values.reshape(dp_count, -1), ctx, 1
        ).reshape(-1)

    small = jnp.concatenate(
        [
            grad_router,
            jnp.stack(
                [grad_gain_a, spread(grad_gain_qk[0]), spread(grad_gain_qk[1]), grad_gain_m],
                axis=1,
            ),
        ],
        axis=1,
    ).astype(half)
    small = jnp.pad(small, ((0, 0), (0, -small.shape[1] % 128)))
    units = take_units(
        coords,
        grad_qkv_w.reshape(dp_count, ctx_count, expert_count, share, -1),
        grad_output.reshape(dp_count * expert_count, share, width),
        small.reshape(dp_count, ctx_count, expert_count, share, -1),
    )
    units = [value.reshape(-1, value.shape[-1]) for value in units]

    def part(step, side):
        if step == pair_ring.count // 2:
            return units[side - 2]
        return units[2 * step - side]

    late = []

    def beside(step, sent):
        if step == pair_ring.count // 2 - 1:
            (late_w,) = after([qkv_w], sent)
            late.append(product("nt", grad_qkv, late_w, half, 256))
            return late[:1] + dp_sum.arrived(2)
        if step == pair_ring.count // 2 - 2:
            return dp_sum.finish(0) + dp_sum.finish(1)
        return dp_sum.finish(2) if step == 1 else []

    own_sum = pair_ring.scatter(part, beside)
    grad_a = xor_scatter(late[0], "ctx")
    grad_normed = grad_a * gains[0]
    normed_own = normed_a[:row_count]
    grad_x = grad_first + inverse_a[:row_count] * (
        grad_normed - normed_own * jnp.mean(grad_normed * normed_own, axis=-1, keepdims=True)
    )
    own_sum = own_sum.reshape(ctx_count, share, -1)
    output_share = own_sum[..., 3 * own_width : 4 * own_width]
    output_share = jnp.concatenate([output_share[at] for at in range(ctx_count)], axis=1)
    sent = jnp.concatenate([own_sum[..., : 3 * own_width], own_sum[..., 4 * own_width :]], axis=-1)
    low_part = sent.astype(half)
    pieces = [lax.dynamic_index_in_dim(sent, ctx, 0, keepdims=False)]
    for j in range(1, ctx_count):
        mine = lax.dynamic_index_in_dim(low_part, ctx ^ j, 0, keepdims=False)
        pieces.append(swap(mine, "ctx", j).astype(single))
    small = sum(piece[:, 3 * own_width :] for piece in pieces)
    whole = jnp.stack([piece[:, : 3 * own_width] for piece in pieces])[by_ctx]
    whole = whole.reshape(ctx_count, share, 3, dp_count, -1).transpose(2, 1, 3, 0, 4)
    whole = whole.reshape(3, share, width)
    added, *_ = after([added], [own_sum])
    mixed = first + added.astype(single)
    return (
        mixed.astype(half)[None],
        grad_x[None],
        whole[0],
        whole[1],
        whole[2],
        output_share,
        small[:, :expert_total],
        small[:, expert_total : expert_total + 4].T,
        dp_sum.outs[1][None],
        dp_sum.outs[2][None],
        dp_sum.outs[0][None],
    )


def solution(mesh):
    rows = P(("dp", "expert"), "ctx", None)
    shares = P(("dp", "ctx", "expert"), None)
    experts = P(("ctx", "expert"), None, None)
    gains = P(None, ("dp", "ctx", "expert"))
    return jax.shard_map(
        on_device,
        mesh=mesh,
        in_specs=(
            (rows,)
            + (shares,) * 5
            + (gains,)
            + (experts,) * 3
            + (rows, P(("dp", "expert"), None), P(("dp", "expert")), rows)
        ),
        out_specs=(rows, rows) + (shares,) * 5 + (gains,) + (experts,) * 3,
        check_vma=False,
    )
```

```python
import functools
import math

import jax
import jax.numpy as jnp
import numpy as np
from jax import lax
from jax.experimental import pallas as pl
from jax.experimental.pallas import tpu as pltpu
from jax.sharding import PartitionSpec as P

HEADS = 16

epsilon = 1e-05
rope_base = 10000.0
single = jnp.float32
half = jnp.bfloat16


def dot(left, right):
    return jnp.dot(left, right, preferred_element_type=single)


def dot_t(left, right):
    return lax.dot_general(left, right, (((1,), (1,)), ((), ())), preferred_element_type=single)


def t_dot(left, right):
    return lax.dot_general(left, right, (((0,), (0,)), ((), ())), preferred_element_type=single)


def inverse_rms(values):
    return lax.rsqrt(jnp.mean(values * values, axis=-1, keepdims=True) + epsilon)


def rope_tables(where, head_size):
    half_size = head_size // 2
    frequency = rope_base ** (-2.0 * jnp.arange(half_size, dtype=single) / head_size)
    angles = where.astype(single)[:, None] * frequency[None, :]
    angles = jnp.concatenate([angles, angles], axis=-1)
    return (jnp.cos(angles), jnp.sin(angles))


def rotate(values, cosine, sine, head_size):
    shaped = values.reshape(values.shape[0], -1, head_size)
    half_size = head_size // 2
    turned = jnp.concatenate([-shaped[..., half_size:], shaped[..., :half_size]], axis=-1)
    return (shaped * cosine[:, None, :] + turned * sine[:, None, :]).reshape(values.shape)


in_hbm = pl.BlockSpec(memory_space=pltpu.HBM)


def nothing(*refs):
    pass


def after(values, tokens, mebibytes=60):
    count = len(values)
    anywhere = pl.BlockSpec(memory_space=pl.ANY)
    specs = [in_hbm if v.size > 1 << 20 else anywhere for v in values]
    out = pl.pallas_call(
        nothing,
        out_shape=[jax.ShapeDtypeStruct(v.shape, v.dtype) for v in values],
        in_specs=specs + [anywhere] * len(tokens),
        out_specs=specs,
        input_output_aliases={i: i for i in range(count)},
        compiler_params=params(mebibytes),
        name="after",
    )(*values, *tokens)
    return list(out)


def params(mebibytes=48):
    return pltpu.CompilerParams(vmem_limit_bytes=mebibytes << 20)


def turn(values, cosine, sine):
    return values * cosine + pltpu.roll(values, values.shape[-1] // 2, 1) * sine


def rope_kernel(heads, qkv, inverse, cosine, sine, gains, q_out, k_out, v_out):
    width = q_out.shape[1]
    size = width // heads
    for at, out in enumerate((q_out, k_out)):
        scale = inverse[:, at : at + 1]
        for head in range(heads):
            cut = slice(head * size, (head + 1) * size)
            raw = qkv[:, at * width + head * size : at * width + (head + 1) * size]
            normed = raw * scale * gains[at : at + 1, cut]
            out[:, cut] = turn(normed, cosine[...], sine[...]).astype(half)
    v_out[...] = qkv[:, 2 * width :].astype(half)


def rope_forward(qkv, inverse, cosine, sine, gains, heads):
    rows, width = qkv.shape[0], qkv.shape[1] // 3
    block = math.gcd(rows, 256)

    def spec(columns):
        return pl.BlockSpec((block, columns), lambda i: (i, 0))

    size = width // heads
    return pl.pallas_call(
        functools.partial(rope_kernel, heads),
        grid=(rows // block,),
        in_specs=[spec(3 * width), spec(2), spec(size), spec(size)]
        + [pl.BlockSpec((2, width), lambda i: (0, 0))],
        out_specs=[spec(width)] * 3,
        out_shape=[jax.ShapeDtypeStruct((rows, width), half)] * 3,
        compiler_params=params(48),
        name="rope_forward",
    )(qkv, inverse, cosine, sine, gains)


def rope_back_kernel(heads, dq, dk, qkv, inverse, cosine, sine, gains, grad_n, sums, grad_gain):
    width = dq.shape[1]
    size = width // heads
    first = pl.program_id(0) == 0
    for at, grad in enumerate((dq, dk)):
        scale = inverse[:, at : at + 1]
        total = jnp.zeros((dq.shape[0], 1), single)
        for head in range(heads):
            cut = slice(head * size, (head + 1) * size)
            wide = slice(at * width + head * size, at * width + (head + 1) * size)
            turned = turn(grad[:, cut], cosine[...], -sine[...])
            normed = qkv[:, wide] * scale
            gained = jnp.sum(turned * normed, axis=0, keepdims=True)
            grad_gain[at : at + 1, cut] = gained + jnp.where(
                first, jnp.zeros_like(gained), grad_gain[at : at + 1, cut]
            )
            out = turned * gains[at : at + 1, cut]
            grad_n[:, wide] = out
            total = total + jnp.sum(out * normed, axis=-1, keepdims=True)
        sums[:, at : at + 1] = total


def rope_back(dq, dk, qkv, inverse, cosine, sine, gains, heads):
    rows, width = dq.shape
    block = math.gcd(rows, 256)

    def spec(columns):
        return pl.BlockSpec((block, columns), lambda i: (i, 0))

    size = width // heads
    fixed = pl.BlockSpec((2, width), lambda i: (0, 0))
    return pl.pallas_call(
        functools.partial(rope_back_kernel, heads),
        grid=(rows // block,),
        in_specs=[spec(width), spec(width), spec(2 * width), spec(2), spec(size), spec(size), fixed],
        out_specs=[spec(2 * width), spec(2), fixed],
        out_shape=[
            jax.ShapeDtypeStruct((rows, 2 * width), single),
            jax.ShapeDtypeStruct((rows, 2), single),
            jax.ShapeDtypeStruct((2, width), single),
        ],
        compiler_params=params(48),
        name="rope_back",
    )(dq, dk, qkv, inverse, cosine, sine, gains)


def norm_back_kernel(grad_n, qkv, inverse, means, dv, out):
    width = dv.shape[1]
    for at in range(2):
        cut = slice(at * width, (at + 1) * width)
        scale = inverse[:, at : at + 1]
        normed = qkv[:, cut] * scale
        out[:, cut] = (scale * (grad_n[:, cut] - normed * means[:, at : at + 1])).astype(half)
    out[:, 2 * width :] = dv[...].astype(half)


def norm_back(grad_n, qkv, inverse, means, dv):
    rows, width = dv.shape
    block = math.gcd(rows, 256)

    def spec(columns):
        return pl.BlockSpec((block, columns), lambda i: (i, 0))

    return pl.pallas_call(
        norm_back_kernel,
        grid=(rows // block,),
        in_specs=[spec(2 * width), spec(2 * width), spec(2), spec(2), spec(width)],
        out_specs=spec(3 * width),
        out_shape=jax.ShapeDtypeStruct((rows, 3 * width), half),
        compiler_params=params(48),
        name="norm_back",
    )(grad_n, qkv, inverse, means, dv)


def attend_kernel(factor, q, k, v, query_pos, key_pos, out, log_total):
    scores = dot_t(q[...], k[...]) * factor
    allowed = key_pos[...] <= query_pos[...]
    scores = jnp.where(allowed, scores, -1e30)
    top = jnp.max(scores, axis=-1, keepdims=True)
    weights = jnp.exp(scores - top)
    total = jnp.sum(weights, axis=-1, keepdims=True)
    log_total[0] = top + jnp.log(total)
    out[...] = (dot(weights.astype(half), v[...]) / total).astype(half)


def attend(q, k, v, query_pos, key_pos, heads):
    rows, width = q.shape
    size = width // heads
    block = math.gcd(rows, 512)
    some = pl.BlockSpec((block, size), lambda h, i: (i, h))
    every = pl.BlockSpec((rows, size), lambda h, i: (0, h))
    return pl.pallas_call(
        functools.partial(attend_kernel, size ** (-0.5)),
        grid=(heads, rows // block),
        in_specs=[
            some,
            every,
            every,
            pl.BlockSpec((block, 1), lambda h, i: (i, 0)),
            pl.BlockSpec((1, rows), lambda h, i: (0, 0)),
        ],
        out_specs=[some, pl.BlockSpec((1, block, 1), lambda h, i: (h, i, 0))],
        out_shape=[
            jax.ShapeDtypeStruct((rows, width), half),
            jax.ShapeDtypeStruct((heads, rows, 1), single),
        ],
        compiler_params=params(48),
        name="attend",
    )(q, k, v, query_pos, key_pos)


def attend_back_kernel(factor, q, k, v, grad_o, log_total, query_pos, key_pos, dq, dk, dv):
    scores = dot_t(q[...], k[...]) * factor
    allowed = key_pos[...] <= query_pos[...]
    probs = jnp.where(allowed, jnp.exp(scores - log_total[0]), 0.0)
    grad_probs = dot_t(grad_o[...], v[...])
    product = probs * grad_probs
    delta = jnp.sum(product, axis=-1, keepdims=True)
    grad_scores = (product - probs * delta).astype(half)
    dq[...] = dot(grad_scores, k[...]) * factor
    added_k = t_dot(grad_scores, q[...]) * factor
    added_v = t_dot(probs.astype(half), grad_o[...])

    @pl.when(pl.program_id(1) == 0)
    def first():
        dk[...] = added_k
        dv[...] = added_v

    @pl.when(pl.program_id(1) > 0)
    def later():
        dk[...] += added_k
        dv[...] += added_v


def attend_back(q, k, v, grad_o, log_total, query_pos, key_pos, heads):
    rows, width = q.shape
    size = width // heads
    block = math.gcd(rows, 512)
    some = pl.BlockSpec((block, size), lambda h, i: (i, h))
    every = pl.BlockSpec((rows, size), lambda h, i: (0, h))
    return pl.pallas_call(
        functools.partial(attend_back_kernel, size ** (-0.5)),
        grid=(heads, rows // block),
        in_specs=[
            some,
            every,
            every,
            some,
            pl.BlockSpec((1, block, 1), lambda h, i: (h, i, 0)),
            pl.BlockSpec((block, 1), lambda h, i: (i, 0)),
            pl.BlockSpec((1, rows), lambda h, i: (0, 0)),
        ],
        out_specs=[some, every, every],
        out_shape=[jax.ShapeDtypeStruct((rows, width), single)] * 3,
        compiler_params=params(48),
        name="attend_back",
    )(q, k, v, grad_o, log_total, query_pos, key_pos)


def chosen_rows(slot, capacity):
    places = lax.broadcasted_iota(jnp.int32, (capacity, slot.shape[-1]), 0)
    return jnp.where(places == slot, 1.0, 0.0).astype(half)


def empty(tag, shape, dtype):
    return pl.pallas_call(
        nothing,
        out_shape=jax.ShapeDtypeStruct(shape, dtype),
        out_specs=in_hbm,
        compiler_params=params(60),
        name="empty_" + tag,
    )()


def place_kernel(count, width, coords, *refs):
    pieces = refs[:count]
    qkv_out, output_out, sem = refs[count + 2 :]
    blocks = pieces[0].shape[0]
    cut = output_out.shape[2] // blocks
    copies = []

    def move(source, target):
        copy = pltpu.make_async_copy(source, target, sem.at[len(copies)])
        copy.start()
        copies.append(copy)

    for at, piece in enumerate(pieces):
        outer, inner, flat = coords[3 * at], coords[3 * at + 1], coords[3 * at + 2]
        move(piece.at[:, :, pl.ds(0, width)], qkv_out.at[outer, :, inner])
        for block in range(blocks):
            move(
                piece.at[block, :, pl.ds(width, cut)],
                output_out.at[flat, :, pl.ds(block * cut, cut)],
            )
    for copy in copies:
        copy.wait()


def place_units(coords, pieces, qkv_w, output_w):
    count, blocks = len(pieces), pieces[0].shape[0]
    return pl.pallas_call(
        functools.partial(place_kernel, count, qkv_w.shape[-1]),
        in_specs=[pl.BlockSpec(memory_space=pltpu.SMEM)]
        + [pl.BlockSpec(memory_space=pltpu.VMEM)] * count
        + [in_hbm] * 2,
        out_specs=[in_hbm] * 2,
        out_shape=[jax.ShapeDtypeStruct(v.shape, v.dtype) for v in (qkv_w, output_w)],
        compiler_params=params(60),
        scratch_shapes=[pltpu.SemaphoreType.DMA((count * (blocks + 1),))],
        input_output_aliases={count + 1: 0, count + 2: 1},
        name="place_units",
    )(coords, *pieces, qkv_w, output_w)


def units_kernel(coords, qkv_w, output_w, small, *refs):
    outs, sem = refs[:-1], refs[-1]
    blocks, width = qkv_w.shape[1], qkv_w.shape[-1]
    cut = output_w.shape[2] // blocks
    copies = []

    def move(source, target):
        copy = pltpu.make_async_copy(source, target, sem.at[len(copies)])
        copy.start()
        copies.append(copy)

    for at, out in enumerate(outs):
        unit = min(at, len(outs) - 2)
        held = out.shape[0]
        first = blocks - held if at == len(outs) - 1 else 0
        some = pl.ds(first, held)
        outer, inner, flat = (coords[3 * unit + k] for k in range(3))
        move(qkv_w.at[outer, some, inner], out.at[:, :, pl.ds(0, width)])
        move(small.at[outer, some, inner], out.at[:, :, pl.ds(width + cut, small.shape[-1])])
        for block in range(first, first + held):
            move(
                output_w.at[flat, :, pl.ds(block * cut, cut)],
                out.at[block - first, :, pl.ds(width, cut)],
            )
    for copy in copies:
        copy.wait()


def take_units(coords, qkv_w, output_w, small):
    count, blocks, share = coords.shape[0] // 3, qkv_w.shape[1], qkv_w.shape[3]
    width = qkv_w.shape[-1] + output_w.shape[2] // blocks + small.shape[-1]
    held = [blocks] * (count - 1) + [blocks // 2] * 2
    return pl.pallas_call(
        units_kernel,
        in_specs=[pl.BlockSpec(memory_space=pltpu.SMEM)] + [in_hbm] * 3,
        out_specs=[pl.BlockSpec(memory_space=pltpu.VMEM)] * len(held),
        out_shape=[jax.ShapeDtypeStruct((some, share, width), half) for some in held],
        compiler_params=params(60),
        scratch_shapes=[pltpu.SemaphoreType.DMA((len(held) * (blocks + 2),))],
        name="take_units",
    )(coords, qkv_w, output_w, small)


def product_kernel(kind, left, right, out):
    form = {"nn": dot, "nt": dot_t, "tn": t_dot}[kind]
    out[...] = form(left[...], right[...]).astype(out.dtype)


def product(kind, left, right, dtype, block=512, part=(0, 1), cost=0):
    at, parts = part
    rows = left.shape[kind == "tn"] // parts
    depth = left.shape[kind != "tn"]
    columns = right.shape[kind != "nt"]
    block = math.gcd(rows, block)
    first = at * (rows // block)
    some = (
        pl.BlockSpec((depth, block), lambda i: (0, first + i))
        if kind == "tn"
        else pl.BlockSpec((block, depth), lambda i: (first + i, 0))
    )
    return pl.pallas_call(
        functools.partial(product_kernel, kind),
        grid=(rows // block,),
        in_specs=[some, pl.BlockSpec(right.shape, lambda i: (0, 0))],
        out_specs=pl.BlockSpec((block, columns), lambda i: (i, 0)),
        out_shape=jax.ShapeDtypeStruct((rows, columns), dtype),
        compiler_params=params(56),
        cost_estimate=pl.CostEstimate(flops=0, bytes_accessed=cost, transcendentals=0)
        if cost
        else None,
        name="product_" + kind,
    )(left, right)


def split_kernel(own_width, ctx, sums, *outs):
    for at, out in enumerate(outs):
        block = ctx[0] ^ (at + 1)
        out[:, : 3 * own_width] = sums[block, :, : 3 * own_width].astype(half)
        out[:, 3 * own_width :] = sums[block, :, 4 * own_width :].astype(half)


def split_blocks(ctx, sums, own_width):
    count, share, width = sums.shape
    return pl.pallas_call(
        functools.partial(split_kernel, own_width),
        in_specs=[
            pl.BlockSpec(memory_space=pltpu.SMEM),
            pl.BlockSpec(memory_space=pltpu.VMEM),
        ],
        out_shape=[jax.ShapeDtypeStruct((share, width - own_width), half)] * (count - 1),
        compiler_params=params(56),
        name="split_blocks",
    )(ctx, sums)


def join_kernel(own_width, parts, ctx, sums, *refs):
    got, outs = refs[:-5], refs[-5:]
    cut = own_width // parts
    width = outs[0].shape[1]
    total = sums[ctx[0], :, 4 * own_width :]
    for at in range(len(got) + 1):
        block = ctx[0] ^ at
        for which in range(3):
            for part in range(parts):
                first = (which * parts + part) * cut
                if at == 0:
                    value = sums[block, :, first : first + cut]
                else:
                    value = got[at - 1][:, first : first + cut].astype(single)
                place = pl.multiple_of(part * (width // parts) + block * cut, cut)
                outs[which][:, pl.ds(place, cut)] = value
        if at > 0:
            total = total + got[at - 1][:, 3 * own_width :].astype(single)
        outs[3][:, at * own_width : (at + 1) * own_width] = sums[
            at, :, 3 * own_width : 4 * own_width
        ]
    outs[4][...] = total


def join_blocks(ctx, sums, got, own_width, parts):
    count, share, width = sums.shape
    full = count * own_width
    return pl.pallas_call(
        functools.partial(join_kernel, own_width, parts),
        in_specs=[pl.BlockSpec(memory_space=pltpu.SMEM)]
        + [pl.BlockSpec(memory_space=pltpu.VMEM)] * count,
        out_shape=[jax.ShapeDtypeStruct((share, full), single)] * 4
        + [jax.ShapeDtypeStruct((share, width - 4 * own_width), single)],
        compiler_params=params(56),
        name="join_blocks",
    )(ctx, sums, *got)


def into_kernel(left, right, held, out):
    out[...] = t_dot(left[...], right[...]).astype(half)


def product_into(left, right, held, at):
    depth, rows = left.shape
    columns = right.shape[1]
    block = math.gcd(rows, 512)
    return pl.pallas_call(
        into_kernel,
        grid=(rows // block,),
        in_specs=[
            pl.BlockSpec((depth, block), lambda i: (0, i)),
            pl.BlockSpec((depth, columns), lambda i: (0, 0)),
            in_hbm,
        ],
        out_specs=pl.BlockSpec((block, columns), lambda i: (i, at)),
        out_shape=jax.ShapeDtypeStruct(held.shape, held.dtype),
        input_output_aliases={2: 0},
        compiler_params=params(56),
        name="product_into",
    )(left, right, held)


def weights_kernel(left, right, weight, out, gained):
    grad = t_dot(left[...], right[...])
    out[...] = grad.astype(half)
    gained[...] = jnp.sum(grad * weight[...].astype(single), axis=-1, keepdims=True)


def weight_gradients(left, right, weight):
    depth, rows = left.shape
    columns = right.shape[1]
    block = math.gcd(rows, 512)
    part = pl.BlockSpec((block, columns), lambda i: (i, 0))
    return pl.pallas_call(
        weights_kernel,
        grid=(rows // block,),
        in_specs=[
            pl.BlockSpec((depth, block), lambda i: (0, i)),
            pl.BlockSpec((depth, columns), lambda i: (0, 0)),
            part,
        ],
        out_specs=[part, pl.BlockSpec((block, 1), lambda i: (i, 0))],
        out_shape=[
            jax.ShapeDtypeStruct((rows, columns), half),
            jax.ShapeDtypeStruct((rows, 1), single),
        ],
        compiler_params=params(56),
        name="weight_gradients",
    )(left, right, weight)


def norm_kernel(gain, *refs):
    blocks, (out, inverse) = refs[:-2], refs[-2:]

    for at, block in enumerate(blocks):

        @pl.when(pl.program_id(0) == at)
        def own():
            values = block[...].astype(single)
            scale = inverse_rms(values)
            inverse[...] = scale
            out[...] = (values * scale * gain[...]).astype(half)


def norm_rows(blocks, gain):
    count = len(blocks)
    rows, width = blocks[0].shape
    return pl.pallas_call(
        norm_kernel,
        grid=(count,),
        in_specs=[pl.BlockSpec((1, width), lambda i: (0, 0))]
        + [pl.BlockSpec((rows, width), lambda i: (0, 0))] * count,
        out_specs=[
            pl.BlockSpec((rows, width), lambda i: (i, 0)),
            pl.BlockSpec((rows, 1), lambda i: (i, 0)),
        ],
        out_shape=[
            jax.ShapeDtypeStruct((count * rows, width), half),
            jax.ShapeDtypeStruct((count * rows, 1), single),
        ],
        compiler_params=params(56),
        name="norm_rows",
    )(gain, *blocks)


def stack_kernel(*refs):
    for at, block in enumerate(refs[:-1]):

        @pl.when(pl.program_id(0) == at)
        def own():
            refs[-1][...] = block[...]


def stack_rows(blocks):
    count = len(blocks)
    rows, width = blocks[0].shape
    return pl.pallas_call(
        stack_kernel,
        grid=(count,),
        in_specs=[pl.BlockSpec((rows, width), lambda i: (0, 0))] * count,
        out_specs=pl.BlockSpec((rows, width), lambda i: (i, 0)),
        out_shape=jax.ShapeDtypeStruct((count * rows, width), blocks[0].dtype),
        compiler_params=params(56),
        name="stack_rows",
    )(*blocks)


def sum_kernel(own, got, *refs):
    token, outs = refs[-1], refs[:-1]
    total = own[...].astype(single) + got[...].astype(single)
    cut = total.shape[1] // len(outs)
    for at, out in enumerate(outs):
        out[...] = total[:, at * cut : (at + 1) * cut]
    token[...] = jnp.zeros_like(token)


def sum_up(own, got, parts):
    rows, width = got.shape
    block = math.gcd(rows, 256)
    cut = width // parts
    whole = pl.BlockSpec((block, width), lambda i: (i, 0))
    *outs, token = pl.pallas_call(
        sum_kernel,
        grid=(rows // block,),
        in_specs=[whole, whole],
        out_specs=[pl.BlockSpec((block, cut), lambda i: (i, 0))] * parts
        + [pl.BlockSpec((8, 128), lambda i: (0, 0))],
        out_shape=[jax.ShapeDtypeStruct((rows, cut), single)] * parts
        + [jax.ShapeDtypeStruct((8, 128), single)],
        compiler_params=params(60),
        name="sum_up",
    )(own, got)
    return outs, token


def put_kernel(order, slot_a, slot_b, hidden_a, hidden_b, weight, out):
    rows = jnp.concatenate([hidden_a[0], hidden_b[0]], axis=0)
    capacity = hidden_a.shape[1]
    places = [chosen_rows(slot[0], capacity) for slot in (slot_a, slot_b)]
    for col in range(0, out.shape[2], 512):
        cut = slice(col, col + 512)
        produced = dot(rows, weight[:, cut]).astype(half)
        out[0, :, cut] = t_dot(places[0], produced[:capacity]).astype(half)
        out[1, :, cut] = t_dot(places[1], produced[capacity:]).astype(half)


def put_rows(order, slot, hidden, weight):
    count, capacity, inner = hidden.shape
    length, width = slot.shape[-1], weight.shape[1]

    def some(shape, side):
        return pl.BlockSpec((1,) + shape, lambda i, order: (order[2 * i + side], 0, 0))

    return pl.pallas_call(
        put_kernel,
        grid_spec=pltpu.PrefetchScalarGridSpec(
            num_scalar_prefetch=1,
            grid=(order.shape[0] // 2,),
            in_specs=[
                some((1, length), 0),
                some((1, length), 1),
                some((capacity, inner), 0),
                some((capacity, inner), 1),
                pl.BlockSpec(weight.shape, lambda i, order: (0, 0)),
            ],
            out_specs=pl.BlockSpec((2, length, width), lambda i, order: (i, 0, 0)),
        ),
        out_shape=jax.ShapeDtypeStruct((order.shape[0], length, width), half),
        compiler_params=params(60),
        name="put_rows",
    )(order, slot, slot, hidden, hidden, weight)


def add_kernel(split, own_a, own_b, got_a, got_b, ahead, behind):
    up, down = own_a[...].astype(single), own_b[...].astype(single)
    if split < up.shape[0]:
        ahead[:split] = (up[:split] + got_a[...].astype(single)).astype(half)
        ahead[split:] = own_a[split:]
        behind[:split] = own_b[:split]
        behind[split:] = (down[split:] + got_b[...].astype(single)).astype(half)
    else:
        ahead[...] = (up + got_a[...].astype(single)).astype(half)
        behind[...] = (down + got_b[...].astype(single)).astype(half)


def add_pair(own_a, own_b, got_a, got_b):
    return pl.pallas_call(
        functools.partial(add_kernel, got_a.shape[0]),
        out_shape=[jax.ShapeDtypeStruct(own_a.shape, half)] * 2,
        compiler_params=params(56),
        name="add_pair",
    )(own_a, own_b, got_a, got_b)


def combine_kernel(split, plus, minus, other_plus, other_minus, got_a, got_b, ahead, behind):
    up = plus[0].astype(single) + other_plus[0].astype(single)
    down = minus[0].astype(single) + other_minus[0].astype(single)
    rows = up.shape[0]
    if split < rows:
        ahead[:split] = (up[:split] + got_a[...].astype(single)).astype(half)
        ahead[split:] = up[split:].astype(half)
        behind[:split] = down[:split].astype(half)
        behind[split:] = (down[split:] + got_b[...].astype(single)).astype(half)
    else:
        ahead[...] = (up + got_a[...].astype(single)).astype(half)
        behind[...] = (down + got_b[...].astype(single)).astype(half)


def combine(own, other, step, got_a, got_b):
    length, width = own.shape[1:]
    plus = pl.BlockSpec((1, length, width), lambda i: (2 * step + 1, 0, 0))
    minus = pl.BlockSpec((1, length, width), lambda i: (2 * step, 0, 0))
    got = pl.BlockSpec(got_a.shape, lambda i: (0, 0))
    out = pl.BlockSpec((length, width), lambda i: (0, 0))
    return pl.pallas_call(
        functools.partial(combine_kernel, got_a.shape[0]),
        grid=(1,),
        in_specs=[plus, minus, plus, minus, got, got],
        out_specs=[out, out],
        out_shape=[jax.ShapeDtypeStruct((length, width), half)] * 2,
        compiler_params=params(56),
        name="combine",
    )(own, own, other, other, got_a, got_b)


def far_kernel(own, other, ahead, behind):
    total = own[0].astype(single) + other[0].astype(single)
    split = ahead.shape[0]
    ahead[...] = total[:split].astype(half)
    behind[...] = total[split:].astype(half)


def far_halves(own, other):
    count, length, width = own.shape
    part = pl.BlockSpec((1, length, width), lambda i: (1, 0, 0))
    out = pl.BlockSpec((length // 2, width), lambda i: (0, 0))
    return pl.pallas_call(
        far_kernel,
        grid=(1,),
        in_specs=[part, part],
        out_specs=[out, out],
        out_shape=[jax.ShapeDtypeStruct((length // 2, width), half)] * 2,
        compiler_params=params(56),
        name="far_halves",
    )(own, other)


def last_kernel(own, other, got_a, got_b, base, out):
    total = base[...] + own[0].astype(single) + other[0].astype(single)
    total = total + got_a[...].astype(single) + got_b[...].astype(single)
    out[...] = total.astype(half)


def last_sum(own, other, got_a, got_b, base):
    length, width = base.shape
    part = pl.BlockSpec((1, length, width), lambda i: (0, 0, 0))
    whole = pl.BlockSpec((length, width), lambda i: (0, 0))
    return pl.pallas_call(
        last_kernel,
        grid=(1,),
        in_specs=[part, part, whole, whole, whole],
        out_specs=whole,
        out_shape=jax.ShapeDtypeStruct((length, width), half),
        compiler_params=params(56),
        name="last_sum",
    )(own, other, got_a, got_b, base)


TILE = 512


def pair_kernel(
    capacity,
    tail,
    order,
    slot,
    piece_a,
    piece_b,
    lanes,
    cot_all,
    gate_v,
    up_v,
    down_v,
    in_rows,
    in_hidden,
    in_gate,
    in_up,
    in_cot,
    home_a,
    home_b,
    all_rows,
    all_hidden,
    all_gate,
    all_up,
    all_cot,
    cot_v,
    cot_rows,
    rows,
    hidden,
    grad_gate,
    grad_up,
    load_sem,
    store_sem,
):
    width, inner = gate_v.shape
    start = order[2]
    loads, stores = [], []

    def load(source, target):
        copy = pltpu.make_async_copy(source, target, load_sem.at[len(loads)])
        copy.start()
        loads.append(copy)
        return copy

    def store(source, target):
        copy = pltpu.make_async_copy(source, target, store_sem.at[len(stores)])
        copy.start()
        stores.append(copy)

    span = pl.ds(pl.multiple_of(start * capacity, 32), 2 * capacity)
    get_cot = [load(cot_all.at[order[at]], cot_v.at[at]) for at in range(2)]
    homes, pieces = (home_a, home_b), (piece_a, piece_b)
    places = [chosen_rows(slot[at], capacity) for at in range(2)]
    parts = [slice(at * capacity, (at + 1) * capacity) for at in range(2)]
    gates = []
    for at in range(2):
        for col in range(0, width, TILE):
            cut = slice(col, col + TILE)
            rows[parts[at], cut] = dot(places[at], pieces[at][:, cut]).astype(half)
        picked = dot(places[at], pieces[at][:, width:])
        gates.append(jnp.sum(picked * lanes[...], axis=-1, keepdims=True))
    gate = jnp.concatenate(gates, axis=0)
    store(rows, all_rows.at[span])
    for at in range(2):
        get_cot[at].wait()
        for col in range(0, width, TILE):
            cut = slice(col, col + TILE)
            cot_rows[parts[at], cut] = dot(places[at], cot_v[at, :, cut]).astype(half)
    store(cot_rows, all_cot.at[span])
    grad_g = jnp.zeros((2 * capacity, 1), single)
    for col in range(0, inner, TILE):
        cut = slice(col, col + TILE)
        gate_pre = dot(rows[...], gate_v[:, cut])
        up_pre = dot(rows[...], up_v[:, cut])
        returned = dot_t(cot_rows[...], down_v[cut, :])
        activated, slope = activate(gate_pre, up_pre)
        kept = activated * up_pre
        hidden[:, cut] = (gate * kept).astype(half)
        grad_g = grad_g + jnp.sum(returned * kept, axis=-1, keepdims=True)
        grad_hidden = gate * returned
        grad_gate[:, cut] = (grad_hidden * up_pre * slope).astype(half)
        grad_up[:, cut] = (grad_hidden * activated).astype(half)
    store(hidden, all_hidden.at[span])
    store(grad_gate, all_gate.at[span])
    store(grad_up, all_up.at[span])
    for col in range(0, width, TILE):
        cut = slice(col, col + TILE)
        back = dot_t(grad_gate[...], gate_v[cut, :]) + dot_t(grad_up[...], up_v[cut, :])
        back = back.astype(half)
        for side in range(2):
            homes[side][:, cut] = t_dot(places[side], back[parts[side]]).astype(half)
    high = grad_g.astype(half).astype(single)
    ends = high * lanes[...] * tail[0:1] + (grad_g - high) * lanes[...] * tail[1:2]
    ends = ends.astype(half)
    for side in range(2):
        homes[side][:, width:] = t_dot(places[side], ends[parts[side]]).astype(half)
    for copy in stores:
        copy.wait()


def expert_pair(order, slot, pieces, lanes, tails, cot_all, weights, held, capacity):
    width, inner = weights[0].shape
    length, wide = pieces[0].shape
    in_vmem = pl.BlockSpec(memory_space=pltpu.VMEM)
    count = 2 * capacity

    def body(order, slot, a, b, lanes, tails, *refs):
        pair_kernel(capacity, tails, order, slot, a, b, lanes, *refs)

    out = pl.pallas_call(
        body,
        in_specs=[pl.BlockSpec(memory_space=pltpu.SMEM)]
        + [in_vmem] * 5
        + [in_hbm]
        + [in_vmem] * 3
        + [in_hbm] * 5,
        out_specs=[in_vmem] * 2 + [in_hbm] * 5,
        out_shape=[jax.ShapeDtypeStruct((length, wide), half)] * 2
        + [jax.ShapeDtypeStruct(value.shape, value.dtype) for value in held],
        scratch_shapes=[
            pltpu.VMEM((2, length, width), half),
            pltpu.VMEM((count, width), half),
            pltpu.VMEM((count, width), half),
            pltpu.VMEM((count, inner), half),
            pltpu.VMEM((count, inner), half),
            pltpu.VMEM((count, inner), half),
            pltpu.SemaphoreType.DMA((2,)),
            pltpu.SemaphoreType.DMA((5,)),
        ],
        input_output_aliases={10 + i: 2 + i for i in range(5)},
        compiler_params=params(34),
        name="expert_pair",
    )(order, slot, *pieces, lanes, tails, cot_all, *weights, *held)
    return out[:2], list(out[2:])


def swap(value, axis, bit):
    count = lax.axis_size(axis)
    return lax.ppermute(value, axis, [(i, i ^ bit) for i in range(count)])


def bits_down(count):
    bits = []
    bit = count // 2
    while bit >= 1:
        bits.append(bit)
        bit //= 2
    return bits


def xor_gather(value, axis, begun=None):
    blocks = {0: value}
    for bit in bits_down(lax.axis_size(axis)):
        held = sorted(blocks)
        if begun is not None and len(held) == 1:
            blocks[bit] = begun
            continue
        for j in held:
            blocks[j | bit] = swap(blocks[j], axis, bit)
    return [blocks[j] for j in sorted(blocks)]


def xor_scatter(value, axis):
    count = lax.axis_size(axis)
    rows = value.shape[0] // count
    held = value
    for bit in reversed(bits_down(count)):
        shaped = held.reshape(-1, 2, rows, held.shape[-1])
        got = swap(shaped[:, 1].astype(half), axis, bit)
        held = shaped[:, 0].astype(single) + got.astype(single)
        held = held.reshape(-1, held.shape[-1])
    return held


def xor_sum(value, axis):
    count = lax.axis_size(axis)
    blocks = value.reshape(-1, count, value.shape[-1] // count)
    for bit in reversed(bits_down(count)):
        got = swap(blocks, axis, bit)
        blocks = blocks + jnp.stack([got[:, j ^ bit] for j in range(count)], axis=1)
    return blocks.reshape(value.shape)


def doubling_gather(value, axes):
    for axis in reversed(axes):
        for bit in reversed(bits_down(lax.axis_size(axis))):
            other = swap(value, axis, bit)
            low = (lax.axis_index(axis) & bit) == 0
            value = jnp.concatenate(
                [jnp.where(low, value, other), jnp.where(low, other, value)], axis=0
            )
    return value


def halving_scatter(value, axes):
    for axis in axes:
        for bit in bits_down(lax.axis_size(axis)):
            rows = value.shape[0] // 2
            low = (lax.axis_index(axis) & bit) == 0
            kept = jnp.where(low, value[:rows], value[rows:])
            sent = jnp.where(low, value[rows:], value[:rows])
            value = kept + swap(sent, axis, bit)
    return value


def snake(outer, inner):
    order = []
    for a in range(outer):
        line = range(inner) if a % 2 == 0 else reversed(range(inner))
        order += [(a, b) for b in line]
    return order


class Ring:
    def __init__(self, axes, planes):
        outer, inner = lax.axis_size(axes[0]) // planes, lax.axis_size(axes[1])
        order = snake(outer, inner)
        self.axes, self.planes, self.count = axes, planes, len(order)
        flat = [[(a * planes + plane) * inner + b for a, b in order] for plane in range(planes)]
        self.forward, self.backward = [], []
        offsets = self.offsets()
        table = [None] * (self.count * planes)
        for plane, line in enumerate(flat):
            for at, index in enumerate(line):
                after = line[(at + 1) % self.count]
                self.forward.append((index, after))
                self.backward.append((after, index))
                table[index] = []
                for group in offsets:
                    for other in range(planes):
                        for offset in group:
                            table[index].append(flat[plane ^ other][(at + offset) % self.count])
        table = jnp.asarray(np.array(table, np.int32))
        self.order = lax.dynamic_slice(
            table,
            (lax.axis_index(axes), jnp.int32(0)),
            (1, table.shape[1]),
            allow_negative_indices=False,
        ).reshape(-1)

    def offsets(self):
        middle = self.count // 2
        return [[0]] + [[-step, step] for step in range(1, middle)] + [[middle]]

    def ahead(self, value):
        return lax.ppermute(value, self.axes, self.forward)

    def behind(self, value):
        return lax.ppermute(value, self.axes, self.backward)

    def gather(self, value, each, room=60, first=()):
        tokens = each(0, [value])
        tokens = tokens + list(first)
        split = value.shape[0] // 2
        from_back = from_front = value
        for step in range(1, self.count // 2):
            from_back, from_front = self.ahead(from_back), self.behind(from_front)
            if tokens:
                from_back, from_front = after([from_back, from_front], tokens, room)
            tokens = each(step, [from_back, from_front])
        last = jnp.concatenate(
            [self.ahead(from_back[:split]), self.behind(from_front[split:])], axis=0
        )
        if tokens:
            (last,) = after([last], tokens, room)
        each(self.count // 2, [last])

    def scatter(self, pick, between=None):
        middle = self.count // 2
        ahead, behind = pick(middle, 0), pick(middle, 1)
        for step in range(middle - 1, 0, -1):
            tokens = between(step, [ahead, behind]) if between else []
            got_ahead, got_behind = self.ahead(ahead), self.behind(behind)
            own_ahead, own_behind = pick(step, 0), pick(step, 1)
            if tokens:
                own_ahead, own_behind = after([own_ahead, own_behind], tokens)
            ahead, behind = add_pair(own_ahead, own_behind, got_ahead, got_behind)
        tokens = between(0, [ahead, behind]) if between else []
        got_ahead, got_behind = self.ahead(ahead), self.behind(behind)
        own = pick(0, 0)
        if tokens:
            (own,) = after([own], tokens)
        return own.astype(single) + got_ahead.astype(single) + got_behind.astype(single)


def add(left, right):
    return (left.astype(single) + right.astype(single)).astype(half)


def trade(buffer):
    count = lax.axis_size("ctx") * lax.axis_size("expert")
    shaped = buffer.reshape(count, -1, buffer.shape[-1])
    moved = lax.all_to_all(shaped, ("ctx", "expert"), split_axis=0, concat_axis=0, tiled=True)
    return moved.reshape(buffer.shape)


def activate(gate_pre, up_pre):
    sigmoid = jax.nn.sigmoid(gate_pre)
    activated = gate_pre * sigmoid
    slope = sigmoid * (1.0 + gate_pre * (1.0 - sigmoid))
    return activated, slope


def experts_by_trade(m_low, gates, cot, picks, w_gate, w_up, w_down, expert_total, capacity):
    rows, width = m_low.shape
    top = picks.shape[1]
    locals_ = w_gate.shape[0]
    flat = (picks.reshape(-1)[:, None] == jnp.arange(expert_total)[None, :]).astype(jnp.int32)
    ranking = jnp.sum((jnp.cumsum(flat, axis=0) - 1) * flat, axis=1)
    slots = picks.reshape(-1) * capacity + ranking
    pair_rows = jnp.arange(rows * top) // top
    empty = jnp.zeros((expert_total * capacity, width), half)
    incoming = trade(empty.at[slots].set(m_low[pair_rows])).reshape(-1, locals_, capacity, width)

    def summed(form, left, right):
        return jnp.einsum(form, left, right, preferred_element_type=single)

    gate_pre = summed("sxcd,xdf->sxcf", incoming, w_gate)
    up_pre = summed("sxcd,xdf->sxcf", incoming, w_up)
    activated, slope = activate(gate_pre, up_pre)
    hidden = (activated * up_pre).astype(half)
    produced = summed("sxcf,xfd->sxcd", hidden, w_down).astype(half)
    returned = trade(produced.reshape(-1, width))
    picked = returned[slots].reshape(rows, top, width).astype(single)
    mixed = jnp.sum(gates[..., None] * picked, axis=1)
    grad_gates = jnp.sum(cot[:, None, :] * picked, axis=-1)
    back = (gates[..., None] * cot[:, None, :]).astype(half).reshape(-1, width)
    grad_in = trade(empty.at[slots].set(back)).reshape(-1, locals_, capacity, width)
    grad_hidden = summed("sxcd,xfd->sxcf", grad_in, w_down)
    grad_down = summed("sxcf,sxcd->xfd", hidden, grad_in)
    grad_gate_pre = (grad_hidden * up_pre * slope).astype(half)
    grad_up_pre = (grad_hidden * activated).astype(half)
    grad_gate = summed("sxcd,sxcf->xdf", incoming, grad_gate_pre)
    grad_up = summed("sxcd,sxcf->xdf", incoming, grad_up_pre)
    grad_rows = summed("sxcf,xdf->sxcd", grad_gate_pre, w_gate)
    grad_rows = (grad_rows + summed("sxcf,xdf->sxcd", grad_up_pre, w_up)).astype(half)
    grad_back = trade(grad_rows.reshape(-1, width))
    grad_m = jnp.sum(grad_back[slots].reshape(rows, top, width).astype(single), axis=1)
    chosen = picks[..., None] == jnp.arange(expert_total)[None, None, :]
    grad_probs = jnp.sum(jnp.where(chosen, grad_gates[..., None], 0.0), axis=1)
    return mixed, grad_m, grad_probs, [grad_down[0], grad_gate[0], grad_up[0]]


def two_parts(value):
    high = lax.reduce_precision(value, 8, 7)
    return high.astype(half), (value - high).astype(half)


def slots_of(routes_all):
    me = lax.axis_index(("ctx", "expert")).astype(routes_all.dtype)
    chosen = jnp.any(routes_all == me, axis=-1)
    rows = chosen.shape[1]
    before = (jnp.arange(rows)[:, None] <= jnp.arange(rows)[None, :]).astype(half)
    rank = dot(chosen.astype(half), before).astype(jnp.int32) - 1
    return jnp.where(chosen, rank, -1)


class ExpertsByRing:
    def __init__(self, slot, cot, w_gate, w_up, w_down, capacity):
        self.ring = Ring(("ctx", "expert"), 2)
        self.capacity = capacity
        self.weights = (w_gate[0], w_up[0], w_down[0])
        self.me = lax.axis_index(("ctx", "expert"))
        self.slot = slot[self.ring.order][:, None, :]
        cot_all = lax.all_gather(cot, ("ctx", "expert"), axis=0, tiled=True)
        self.cot_all = cot_all.reshape(slot.shape + cot.shape[-1:])

    def run(self, m_low, gate_dense, dp_sum):
        rows, width = m_low.shape
        inner = self.weights[0].shape[1]
        experts = gate_dense.shape[1]
        lanes = 64
        high, low = two_parts(gate_dense)
        fill = jnp.zeros((rows, lanes - experts), half)
        wide = jnp.concatenate([m_low, high, fill, low, fill], axis=1)
        lane = jnp.arange(2 * lanes)
        mine = (lane % lanes == self.me).astype(single)[None]
        tails = jnp.stack([lane < lanes, lane >= lanes]).astype(single)
        devices = self.slot.shape[0]
        total = devices * self.capacity
        held = [
            empty("rows", (total, width), half),
            empty("hidden", (total, inner), half),
            empty("gate", (total, inner), half),
            empty("up", (total, inner), half),
            empty("cot", (total, width), half),
        ]
        sums = []

        def pair(start, pieces):
            order = jnp.concatenate(
                [self.ring.order[start : start + 2], jnp.full((1,), start, jnp.int32)]
            )
            slot = self.slot[start : start + 2]
            homes, held[:] = expert_pair(
                order, slot, pieces, mine, tails, self.cot_all, self.weights, held, self.capacity
            )
            return homes

        def each(step, arrived):
            start = sum(2 * len(group) for group in self.ring.offsets()[:step])
            others = [swap(piece, "ctx", 1) for piece in arrived]
            if len(arrived) == 1:
                homes = pair(start, arrived + others)
                tokens = [homes[0]]
            else:
                homes = pair(start, arrived)
                tokens = [homes[0]]
                homes = homes + pair(start + 2, others)
            count = len(arrived)
            sums.append(
                [add(homes[at], swap(homes[at + count], "ctx", 1)) for at in range(count)]
            )
            return tokens

        self.ring.gather(wide, each, 1)
        incoming, hidden, gate, up, cot_rows = held
        grads = []
        work = [(hidden, cot_rows), (incoming, gate), (incoming, up)]

        def between(step, sent):
            if not work:
                return [] if step else dp_sum.arrived(0)
            left, right = work.pop(0)
            (right,) = after([right], sent)
            if len(grads) == 0:
                grads.append(product("tn", left, right, half))
            else:
                both = grads[1] if len(grads) > 1 else empty("pre", (width, 2 * inner), half)
                grads.append(product_into(left, right, both, len(grads) - 1))
            if len(grads) != 2:
                dp_sum.add(grads[-1])
            return grads[-1:]

        def pick(step, side):
            if step == len(sums) - 1:
                far = sums[step][0]
                split = far.shape[0] // 2
                return far[split:] if side else far[:split]
            return sums[step][-1 - side]

        summed = self.ring.scatter(pick, between)
        while work:
            between(0, [summed])
        grad_m = summed[:, :width]
        tail = summed[:, width:]
        grad_probs = tail[:, :experts] + tail[:, lanes : lanes + experts]
        self.hidden = hidden
        return grad_m, grad_probs

    def put(self, tokens):
        (hidden,) = after([self.hidden], tokens)
        hidden = hidden.reshape(-1, self.capacity, hidden.shape[-1])
        planes = [[], []]
        at = 0
        for group in self.ring.offsets():
            for plane in planes:
                plane.append(list(range(at, at + len(group))))
                at += len(group)
        parts = []
        for plane in reversed(planes):
            order = plane[0] + plane[-1] + sum(plane[1:-1], [])
            order = jnp.asarray(np.array(order, np.int32))
            parts.append(put_rows(order, self.slot, hidden, self.weights[2]))
        self.own = parts[1]
        self.other = swap(parts[0], "ctx", 1)
        return parts

    def send(self, step, tokens):
        ring = self.ring
        if step == ring.count // 2:
            (other,) = after([self.other], tokens)
            self.other = other
            ahead, behind = far_halves(self.own, other)
        else:
            got_a, got_b = after(self.got, tokens)
            ahead, behind = combine(self.own, self.other, step, got_a, got_b)
        self.got = [ring.ahead(ahead), ring.behind(behind)]
        return [ahead]

    def mixed(self, base, tokens):
        got_a, got_b = after(self.got, tokens)
        return last_sum(self.own, self.other, got_a, got_b, base)


class DpSum:
    def __init__(self):
        self.two = lax.axis_size("dp") == 2
        self.grads, self.got, self.outs = [], [], []

    def add(self, grad):
        self.grads.append(grad.astype(half))
        if self.two:
            self.got.append(swap(self.grads[-1], "dp", 1))

    def arrived(self, at):
        return self.got[at : at + 1]

    def finish(self, at):
        if self.two:
            outs, token = sum_up(self.grads[at], self.got[at], at + 1)
            self.outs += outs
            return [token]
        total = lax.psum(self.grads[at], "dp").astype(single)
        self.outs += jnp.split(total, at + 1, axis=1)
        return []

    def results(self):
        down, gate, up = self.outs
        return gate[None], up[None], down[None]


def on_device(
    tokens,
    w_query,
    w_key,
    w_value,
    w_output,
    w_router,
    norm_gains,
    w_gate,
    w_up,
    w_down,
    routes,
    positions,
    lengths,
    cotangent,
):
    dp_count, ctx_count, expert_count = (
        lax.axis_size("dp"),
        lax.axis_size("ctx"),
        lax.axis_size("expert"),
    )
    world = ("dp", "ctx", "expert")
    ctx = lax.axis_index("ctx")
    row_count, width = tokens.shape[1:]
    head_size = width // HEADS
    head_count = HEADS // ctx_count
    share = w_query.shape[0]
    own_width = width // ctx_count
    expert_total = w_router.shape[1]
    picks = routes[0]
    top = picks.shape[1]
    capacity = 5 * row_count * top // (4 * expert_total)
    all_rows = row_count * ctx_count
    cot = cotangent[0].astype(single)

    packed = jnp.concatenate(
        [w_router.reshape(-1), norm_gains.reshape(-1), picks.astype(half).reshape(-1)]
    )
    packed_size = packed.shape[0]
    packed = jnp.pad(packed, (0, -packed_size % 1024)).reshape(1, -1, 128)
    router_size, gain_size = share * expert_total, 4 * share

    def own_features(values):
        shaped = values.reshape(values.shape[:-1] + (dp_count, ctx_count, -1))
        return lax.dynamic_index_in_dim(shaped, ctx, values.ndim, keepdims=False).reshape(
            values.shape[:-1] + (own_width,)
        )

    pair_ring = Ring(("dp", "expert"), 1)
    outer, inner = pair_ring.order // expert_count, pair_ring.order % expert_count
    coords = jnp.stack([outer, inner, pair_ring.order], axis=1).reshape(-1)
    shards = jnp.concatenate(
        [
            value.reshape(share, dp_count, ctx_count, -1)
            for value in (w_query, w_key, w_value)
        ],
        axis=1,
    )

    def columns_for(j):
        return lax.dynamic_index_in_dim(
            shards, ctx ^ j, 2, keepdims=False, allow_negative_indices=False
        ).reshape(share, -1)

    blocks = [columns_for(0)]
    for j in range(1, ctx_count):
        blocks.append(swap(columns_for(j), "ctx", j))
    by_ctx = ctx ^ jnp.arange(ctx_count)
    blocks = jnp.stack(blocks)[by_ctx].reshape(ctx_count * share, -1)
    output_blocks = [
        w_output[:, at * own_width : (at + 1) * own_width] for at in range(ctx_count)
    ]
    unit = jnp.concatenate([blocks, jnp.concatenate(output_blocks, axis=0)], axis=1)
    gathered = {
        "count": 0,
        "weights": (
            empty("qkv", (dp_count, ctx_count, expert_count, share, 3 * own_width), half),
            empty("output", (dp_count * expert_count, share, width), half),
        ),
    }

    def rows_ready(step, arrived):
        done = gathered["count"]
        gathered["count"] = done + len(arrived)
        gathered["weights"] = place_units(
            coords[3 * done : 3 * gathered["count"]],
            [piece.reshape(ctx_count, share, -1) for piece in arrived],
            *gathered["weights"],
        )
        result = list(gathered["weights"][1:])
        middle = pair_ring.count // 2
        if step == middle - 1:
            (gathered["cot"],) = after([cotangent[0]], arrived)
        if step == 1:
            (x_begun,) = after([gathered["x"]], arrived)
            gathered["x"] = xor_gather(tokens[0], "ctx", x_begun)
        if step == max(1, middle - 2):
            small = gathered["small"].reshape(dp_count * ctx_count * expert_count, -1)
            gathered["router"] = small[:, :router_size].reshape(width, expert_total)
            gains = small[:, router_size : router_size + gain_size].reshape(-1, 4, share)
            gathered["gains"] = gains.transpose(1, 0, 2).reshape(4, width).astype(single)
            routes_all = small[:, router_size + gain_size : packed_size]
            routes_all = routes_all.reshape(dp_count, -1, row_count, top)
            gathered["slot"] = slots_of(routes_all[lax.axis_index("dp")])
            gathered["a_low"], gathered["inverse_a"] = norm_rows(
                gathered["x"], gathered["gains"][:1]
            )
            result += [gathered["a_low"], cosine, sine, gathered["slot"]]
        return result

    all_pos = positions[0].reshape(ctx_count, row_count)[by_ctx].reshape(-1)
    cosine, sine = rope_tables(all_pos, head_size)
    sine = jnp.where(jnp.arange(head_size) < head_size // 2, -sine, sine)
    gathered["small"] = doubling_gather(packed, world)
    gathered["x"] = swap(tokens[0], "ctx", ctx_count // 2)
    pair_ring.gather(unit, rows_ready, first=[gathered["small"]])
    gains, slot, router_w = gathered["gains"], gathered["slot"], gathered["router"]
    qkv_w, output_w = gathered["weights"]
    qkv_w = qkv_w.reshape(width, 3 * own_width)
    output_w = output_w.reshape(own_width, width)

    inverse_a, a_low = gathered["inverse_a"], gathered["a_low"]
    qkv = product("nn", a_low, qkv_w, single, 256)
    q_raw, k_raw = qkv[:, :own_width], qkv[:, own_width : 2 * own_width]
    squares = jnp.stack([jnp.sum(q_raw * q_raw, axis=-1), jnp.sum(k_raw * k_raw, axis=-1)])
    inverse = lax.rsqrt(xor_sum(squares, "ctx") / width + epsilon).T
    gains_qk = jnp.stack([own_features(gains[1]), own_features(gains[2])])
    q_low, k_low, v_low = rope_forward(qkv, inverse, cosine, sine, gains_qk, head_count)

    by_ring = ctx_count * expert_count == 16 and ctx_count % 2 == 0
    if by_ring:
        layer = ExpertsByRing(slot, gathered["cot"], w_gate, w_up, w_down, capacity)

    query_pos = all_pos[:, None]
    key_pos = jnp.where(all_pos < lengths[0], all_pos, 1 << 30)[None, :]
    attended_low, log_total = attend(q_low, k_low, v_low, query_pos, key_pos, head_count)
    first = tokens[0].astype(single) + xor_scatter(product("nn", attended_low, output_w, half, 256), "ctx")
    inverse_m = inverse_rms(first)
    normed_m = first * inverse_m
    m_low = (normed_m * gains[3]).astype(half)
    router_probs = jax.nn.softmax(dot(m_low, router_w), axis=-1)
    chosen = picks[..., None] == jnp.arange(expert_total)[None, None, :]
    dp_sum = DpSum()
    if by_ring:
        gate_dense = jnp.where(jnp.any(chosen, axis=1), router_probs, 0.0)
        grad_m, grad_probs = layer.run(m_low, gate_dense, dp_sum)
    else:
        gates = jnp.sum(jnp.where(chosen, router_probs[:, None, :], 0.0), axis=-1)
        added, grad_m, grad_probs, expert_grads = experts_by_trade(
            m_low, gates, cot, picks, w_gate, w_up, w_down, expert_total, capacity
        )
        dp_sum.add(expert_grads[0])
        dp_sum.add(jnp.concatenate(expert_grads[1:], axis=1))
    grad_logits = router_probs * (
        grad_probs - jnp.sum(router_probs * grad_probs, axis=-1, keepdims=True)
    )
    grad_logits_low = grad_logits.astype(half)
    grad_router = t_dot(m_low, grad_logits_low)
    grad_m = grad_m + dot_t(grad_logits_low, router_w)
    grad_gain_m = jnp.sum(grad_m * normed_m, axis=0)
    grad_normed = grad_m * gains[3]
    grad_first = cot + inverse_m * (
        grad_normed - normed_m * jnp.mean(grad_normed * normed_m, axis=-1, keepdims=True)
    )
    grad_first_low = grad_first.astype(half)
    begun = swap(grad_first_low, "ctx", ctx_count // 2)

    def send(step, values, tokens=()):
        return after(values, layer.send(step, list(tokens) or values[:1])) if by_ring else values

    if by_ring:
        (begun,) = send(4, [begun], layer.put([grad_first_low]))
        (begun,) = send(3, [begun])
    grad_attn = stack_rows(xor_gather(grad_first_low, "ctx", begun))
    grad_output = product("tn", attended_low, grad_attn, half, 256)
    grad_o = product("nt", grad_attn, output_w, half, 256)
    dq, dk, dv = attend_back(
        q_low, k_low, v_low, grad_o, log_total, query_pos, key_pos, head_count
    )
    dq, dk, dv = send(2, [dq, dk, dv])
    grad_n, sums, grad_gain_qk = rope_back(
        dq, dk, qkv, inverse, cosine, sine, gains_qk, head_count
    )
    means = (xor_sum(sums.T, "ctx") / width).T
    (means,) = send(1, [means])
    grad_qkv = norm_back(grad_n, qkv, inverse, means, dv)
    grad_qkv_w, grad_gain_a = weight_gradients(a_low, grad_qkv, qkv_w)
    grad_gain_a = grad_gain_a[:, 0] / gains[0]

    def spread(values):
        shaped = jnp.zeros((dp_count, ctx_count, own_width // dp_count), single)
        return lax.dynamic_update_index_in_dim(
            shaped, values.reshape(dp_count, -1), ctx, 1
        ).reshape(-1)

    small = jnp.concatenate(
        [
            grad_router,
            jnp.stack(
                [grad_gain_a, spread(grad_gain_qk[0]), spread(grad_gain_qk[1]), grad_gain_m],
                axis=1,
            ),
        ],
        axis=1,
    ).astype(half)
    small = jnp.pad(small, ((0, 0), (0, -small.shape[1] % 128)))
    units = take_units(
        coords,
        grad_qkv_w.reshape(dp_count, ctx_count, expert_count, share, -1),
        grad_output.reshape(dp_count * expert_count, share, width),
        small.reshape(dp_count, ctx_count, expert_count, share, -1),
    )
    units = [value.reshape(-1, value.shape[-1]) for value in units]

    def part(step, side):
        if step == pair_ring.count // 2:
            return units[side - 2]
        return units[2 * step - side]

    late = []

    def beside(step, sent):
        if step == pair_ring.count // 2 - 1:
            (late_w,) = after([qkv_w], sent)
            late.append(product("nt", grad_qkv, late_w, half, 256, cost=16 << 20))
            if by_ring:
                late.append(layer.mixed(first, sent))
            return late + dp_sum.finish(0) + dp_sum.arrived(1)
        if step == pair_ring.count // 2 - 2:
            return dp_sum.finish(1)
        return []

    own_sum = pair_ring.scatter(part, beside)
    grad_a = xor_scatter(late[0], "ctx")
    grad_normed = grad_a * gains[0]
    normed_own = tokens[0].astype(single) * inverse_a[:row_count]
    grad_x = grad_first + inverse_a[:row_count] * (
        grad_normed - normed_own * jnp.mean(grad_normed * normed_own, axis=-1, keepdims=True)
    )
    own_sum = own_sum.reshape(ctx_count, share, -1)
    ctx_only = ctx.astype(jnp.int32)[None]
    sent = split_blocks(ctx_only, own_sum, own_width)
    got = [swap(block, "ctx", j) for j, block in zip(range(1, ctx_count), sent)]
    query_share, key_share, value_share, output_share, small = join_blocks(
        ctx_only, own_sum, got, own_width, dp_count
    )
    mixed = late[1] if by_ring else first + added
    return (
        mixed.astype(half)[None],
        grad_x[None],
        query_share,
        key_share,
        value_share,
        output_share,
        small[:, :expert_total],
        small[:, expert_total : expert_total + 4].T,
        *dp_sum.results(),
    )


def solution(mesh):
    rows = P(("dp", "expert"), "ctx", None)
    shares = P(("dp", "ctx", "expert"), None)
    experts = P(("ctx", "expert"), None, None)
    gains = P(None, ("dp", "ctx", "expert"))
    return jax.shard_map(
        on_device,
        mesh=mesh,
        in_specs=(
            (rows,)
            + (shares,) * 5
            + (gains,)
            + (experts,) * 3
            + (rows, P(("dp", "expert"), None), P(("dp", "expert")), rows)
        ),
        out_specs=(rows, rows) + (shares,) * 5 + (gains,) + (experts,) * 3,
        check_vma=False,
    )
```

```python
import functools
import math

import jax
import jax.numpy as jnp
import numpy as np
from jax import lax
from jax.experimental import pallas as pl
from jax.experimental.pallas import tpu as pltpu
from jax.sharding import PartitionSpec as P

HEADS = 16

epsilon = 1e-05
rope_base = 10000.0
single = jnp.float32
half = jnp.bfloat16


def dot(left, right):
    return jnp.dot(left, right, preferred_element_type=single)


def dot_t(left, right):
    return lax.dot_general(left, right, (((1,), (1,)), ((), ())), preferred_element_type=single)


def t_dot(left, right):
    return lax.dot_general(left, right, (((0,), (0,)), ((), ())), preferred_element_type=single)


def inverse_rms(values):
    return lax.rsqrt(jnp.mean(values * values, axis=-1, keepdims=True) + epsilon)


def rope_tables(where, head_size):
    half_size = head_size // 2
    frequency = rope_base ** (-2.0 * jnp.arange(half_size, dtype=single) / head_size)
    angles = where.astype(single)[:, None] * frequency[None, :]
    angles = jnp.concatenate([angles, angles], axis=-1)
    return (jnp.cos(angles), jnp.sin(angles))


def rotate(values, cosine, sine, head_size):
    shaped = values.reshape(values.shape[0], -1, head_size)
    half_size = head_size // 2
    turned = jnp.concatenate([-shaped[..., half_size:], shaped[..., :half_size]], axis=-1)
    return (shaped * cosine[:, None, :] + turned * sine[:, None, :]).reshape(values.shape)


in_hbm = pl.BlockSpec(memory_space=pltpu.HBM)


def nothing(*refs):
    pass


def after(values, tokens, mebibytes=60):
    count = len(values)
    anywhere = pl.BlockSpec(memory_space=pl.ANY)
    specs = [in_hbm if v.size > 1 << 20 else anywhere for v in values]
    out = pl.pallas_call(
        nothing,
        out_shape=[jax.ShapeDtypeStruct(v.shape, v.dtype) for v in values],
        in_specs=specs + [anywhere] * len(tokens),
        out_specs=specs,
        input_output_aliases={i: i for i in range(count)},
        compiler_params=params(mebibytes),
        name="after",
    )(*values, *tokens)
    return list(out)


def params(mebibytes=48):
    return pltpu.CompilerParams(vmem_limit_bytes=mebibytes << 20)


def turn(values, cosine, sine):
    return values * cosine + pltpu.roll(values, values.shape[-1] // 2, 1) * sine


def rope_kernel(heads, qkv, inverse, cosine, sine, gains, q_out, k_out, v_out):
    width = q_out.shape[1]
    size = width // heads
    for at, out in enumerate((q_out, k_out)):
        scale = inverse[:, at : at + 1]
        for head in range(heads):
            cut = slice(head * size, (head + 1) * size)
            raw = qkv[:, at * width + head * size : at * width + (head + 1) * size]
            normed = raw * scale * gains[at : at + 1, cut]
            out[:, cut] = turn(normed, cosine[...], sine[...]).astype(half)
    v_out[...] = qkv[:, 2 * width :].astype(half)


def rope_forward(qkv, inverse, cosine, sine, gains, heads):
    rows, width = qkv.shape[0], qkv.shape[1] // 3
    block = math.gcd(rows, 256)

    def spec(columns):
        return pl.BlockSpec((block, columns), lambda i: (i, 0))

    size = width // heads
    return pl.pallas_call(
        functools.partial(rope_kernel, heads),
        grid=(rows // block,),
        in_specs=[spec(3 * width), spec(2), spec(size), spec(size)]
        + [pl.BlockSpec((2, width), lambda i: (0, 0))],
        out_specs=[spec(width)] * 3,
        out_shape=[jax.ShapeDtypeStruct((rows, width), half)] * 3,
        compiler_params=params(48),
        name="rope_forward",
    )(qkv, inverse, cosine, sine, gains)


def rope_back_kernel(heads, dq, dk, qkv, inverse, cosine, sine, gains, grad_n, sums, grad_gain):
    width = dq.shape[1]
    size = width // heads
    first = pl.program_id(0) == 0
    for at, grad in enumerate((dq, dk)):
        scale = inverse[:, at : at + 1]
        total = jnp.zeros((dq.shape[0], 1), single)
        for head in range(heads):
            cut = slice(head * size, (head + 1) * size)
            wide = slice(at * width + head * size, at * width + (head + 1) * size)
            turned = turn(grad[:, cut], cosine[...], -sine[...])
            normed = qkv[:, wide] * scale
            gained = jnp.sum(turned * normed, axis=0, keepdims=True)
            grad_gain[at : at + 1, cut] = gained + jnp.where(
                first, jnp.zeros_like(gained), grad_gain[at : at + 1, cut]
            )
            out = turned * gains[at : at + 1, cut]
            grad_n[:, wide] = out
            total = total + jnp.sum(out * normed, axis=-1, keepdims=True)
        sums[:, at : at + 1] = total


def rope_back(dq, dk, qkv, inverse, cosine, sine, gains, heads):
    rows, width = dq.shape
    block = math.gcd(rows, 256)

    def spec(columns):
        return pl.BlockSpec((block, columns), lambda i: (i, 0))

    size = width // heads
    fixed = pl.BlockSpec((2, width), lambda i: (0, 0))
    return pl.pallas_call(
        functools.partial(rope_back_kernel, heads),
        grid=(rows // block,),
        in_specs=[spec(width), spec(width), spec(2 * width), spec(2), spec(size), spec(size), fixed],
        out_specs=[spec(2 * width), spec(2), fixed],
        out_shape=[
            jax.ShapeDtypeStruct((rows, 2 * width), single),
            jax.ShapeDtypeStruct((rows, 2), single),
            jax.ShapeDtypeStruct((2, width), single),
        ],
        compiler_params=params(48),
        name="rope_back",
    )(dq, dk, qkv, inverse, cosine, sine, gains)


def norm_back_kernel(grad_n, qkv, inverse, means, dv, out):
    width = dv.shape[1]
    for at in range(2):
        cut = slice(at * width, (at + 1) * width)
        scale = inverse[:, at : at + 1]
        normed = qkv[:, cut] * scale
        out[:, cut] = (scale * (grad_n[:, cut] - normed * means[:, at : at + 1])).astype(half)
    out[:, 2 * width :] = dv[...].astype(half)


def norm_back(grad_n, qkv, inverse, means, dv):
    rows, width = dv.shape
    block = math.gcd(rows, 256)

    def spec(columns):
        return pl.BlockSpec((block, columns), lambda i: (i, 0))

    return pl.pallas_call(
        norm_back_kernel,
        grid=(rows // block,),
        in_specs=[spec(2 * width), spec(2 * width), spec(2), spec(2), spec(width)],
        out_specs=spec(3 * width),
        out_shape=jax.ShapeDtypeStruct((rows, 3 * width), half),
        compiler_params=params(48),
        name="norm_back",
    )(grad_n, qkv, inverse, means, dv)


def attend_kernel(factor, q, k, v, query_pos, key_pos, out, log_total):
    scores = dot_t(q[...], k[...]) * factor
    allowed = key_pos[...] <= query_pos[...]
    scores = jnp.where(allowed, scores, -1e30)
    top = jnp.max(scores, axis=-1, keepdims=True)
    weights = jnp.exp(scores - top)
    total = jnp.sum(weights, axis=-1, keepdims=True)
    log_total[0] = top + jnp.log(total)
    out[...] = (dot(weights.astype(half), v[...]) / total).astype(half)


def attend(q, k, v, query_pos, key_pos, heads):
    rows, width = q.shape
    size = width // heads
    block = math.gcd(rows, 512)
    some = pl.BlockSpec((block, size), lambda h, i: (i, h))
    every = pl.BlockSpec((rows, size), lambda h, i: (0, h))
    return pl.pallas_call(
        functools.partial(attend_kernel, size ** (-0.5)),
        grid=(heads, rows // block),
        in_specs=[
            some,
            every,
            every,
            pl.BlockSpec((block, 1), lambda h, i: (i, 0)),
            pl.BlockSpec((1, rows), lambda h, i: (0, 0)),
        ],
        out_specs=[some, pl.BlockSpec((1, block, 1), lambda h, i: (h, i, 0))],
        out_shape=[
            jax.ShapeDtypeStruct((rows, width), half),
            jax.ShapeDtypeStruct((heads, rows, 1), single),
        ],
        compiler_params=params(48),
        name="attend",
    )(q, k, v, query_pos, key_pos)


def attend_back_kernel(factor, q, k, v, grad_o, log_total, query_pos, key_pos, dq, dk, dv):
    scores = dot_t(q[...], k[...]) * factor
    allowed = key_pos[...] <= query_pos[...]
    probs = jnp.where(allowed, jnp.exp(scores - log_total[0]), 0.0)
    grad_probs = dot_t(grad_o[...], v[...])
    product = probs * grad_probs
    delta = jnp.sum(product, axis=-1, keepdims=True)
    grad_scores = (product - probs * delta).astype(half)
    dq[...] = dot(grad_scores, k[...]) * factor
    added_k = t_dot(grad_scores, q[...]) * factor
    added_v = t_dot(probs.astype(half), grad_o[...])

    @pl.when(pl.program_id(1) == 0)
    def first():
        dk[...] = added_k
        dv[...] = added_v

    @pl.when(pl.program_id(1) > 0)
    def later():
        dk[...] += added_k
        dv[...] += added_v


def attend_back(q, k, v, grad_o, log_total, query_pos, key_pos, heads):
    rows, width = q.shape
    size = width // heads
    block = math.gcd(rows, 512)
    some = pl.BlockSpec((block, size), lambda h, i: (i, h))
    every = pl.BlockSpec((rows, size), lambda h, i: (0, h))
    return pl.pallas_call(
        functools.partial(attend_back_kernel, size ** (-0.5)),
        grid=(heads, rows // block),
        in_specs=[
            some,
            every,
            every,
            some,
            pl.BlockSpec((1, block, 1), lambda h, i: (h, i, 0)),
            pl.BlockSpec((block, 1), lambda h, i: (i, 0)),
            pl.BlockSpec((1, rows), lambda h, i: (0, 0)),
        ],
        out_specs=[some, every, every],
        out_shape=[jax.ShapeDtypeStruct((rows, width), single)] * 3,
        compiler_params=params(48),
        name="attend_back",
    )(q, k, v, grad_o, log_total, query_pos, key_pos)


def chosen_rows(slot, capacity):
    places = lax.broadcasted_iota(jnp.int32, (capacity, slot.shape[-1]), 0)
    return jnp.where(places == slot, 1.0, 0.0).astype(half)


def empty(tag, shape, dtype):
    return pl.pallas_call(
        nothing,
        out_shape=jax.ShapeDtypeStruct(shape, dtype),
        out_specs=in_hbm,
        compiler_params=params(60),
        name="empty_" + tag,
    )()


def place_kernel(count, width, coords, *refs):
    pieces = refs[:count]
    qkv_out, output_out, sem = refs[count + 2 :]
    blocks = pieces[0].shape[0]
    cut = output_out.shape[2] // blocks
    copies = []

    def move(source, target):
        copy = pltpu.make_async_copy(source, target, sem.at[len(copies)])
        copy.start()
        copies.append(copy)

    for at, piece in enumerate(pieces):
        outer, inner, flat = coords[3 * at], coords[3 * at + 1], coords[3 * at + 2]
        move(piece.at[:, :, pl.ds(0, width)], qkv_out.at[outer, :, inner])
        for block in range(blocks):
            move(
                piece.at[block, :, pl.ds(width, cut)],
                output_out.at[flat, :, pl.ds(block * cut, cut)],
            )
    for copy in copies:
        copy.wait()


def place_units(coords, pieces, qkv_w, output_w):
    count, blocks = len(pieces), pieces[0].shape[0]
    return pl.pallas_call(
        functools.partial(place_kernel, count, qkv_w.shape[-1]),
        in_specs=[pl.BlockSpec(memory_space=pltpu.SMEM)]
        + [pl.BlockSpec(memory_space=pltpu.VMEM)] * count
        + [in_hbm] * 2,
        out_specs=[in_hbm] * 2,
        out_shape=[jax.ShapeDtypeStruct(v.shape, v.dtype) for v in (qkv_w, output_w)],
        compiler_params=params(60),
        scratch_shapes=[pltpu.SemaphoreType.DMA((count * (blocks + 1),))],
        input_output_aliases={count + 1: 0, count + 2: 1},
        name="place_units",
    )(coords, *pieces, qkv_w, output_w)


def units_kernel(coords, qkv_w, output_w, small, *refs):
    outs, sem = refs[:-1], refs[-1]
    blocks, width = qkv_w.shape[1], qkv_w.shape[-1]
    cut = output_w.shape[2] // blocks
    copies = []

    def move(source, target):
        copy = pltpu.make_async_copy(source, target, sem.at[len(copies)])
        copy.start()
        copies.append(copy)

    for at, out in enumerate(outs):
        unit = min(at, len(outs) - 2)
        held = out.shape[0]
        first = blocks - held if at == len(outs) - 1 else 0
        some = pl.ds(first, held)
        outer, inner, flat = (coords[3 * unit + k] for k in range(3))
        move(qkv_w.at[outer, some, inner], out.at[:, :, pl.ds(0, width)])
        move(small.at[outer, some, inner], out.at[:, :, pl.ds(width + cut, small.shape[-1])])
        for block in range(first, first + held):
            move(
                output_w.at[flat, :, pl.ds(block * cut, cut)],
                out.at[block - first, :, pl.ds(width, cut)],
            )
    for copy in copies:
        copy.wait()


def take_units(coords, qkv_w, output_w, small):
    count, blocks, share = coords.shape[0] // 3, qkv_w.shape[1], qkv_w.shape[3]
    width = qkv_w.shape[-1] + output_w.shape[2] // blocks + small.shape[-1]
    held = [blocks] * (count - 1) + [blocks // 2] * 2
    return pl.pallas_call(
        units_kernel,
        in_specs=[pl.BlockSpec(memory_space=pltpu.SMEM)] + [in_hbm] * 3,
        out_specs=[pl.BlockSpec(memory_space=pltpu.VMEM)] * len(held),
        out_shape=[jax.ShapeDtypeStruct((some, share, width), half) for some in held],
        compiler_params=params(60),
        scratch_shapes=[pltpu.SemaphoreType.DMA((len(held) * (blocks + 2),))],
        name="take_units",
    )(coords, qkv_w, output_w, small)


def product_kernel(kind, left, right, out):
    form = {"nn": dot, "nt": dot_t, "tn": t_dot}[kind]
    out[...] = form(left[...], right[...]).astype(out.dtype)


def product(kind, left, right, dtype, block=512, part=(0, 1), cost=0):
    at, parts = part
    rows = left.shape[kind == "tn"] // parts
    depth = left.shape[kind != "tn"]
    columns = right.shape[kind != "nt"]
    block = math.gcd(rows, block)
    first = at * (rows // block)
    some = (
        pl.BlockSpec((depth, block), lambda i: (0, first + i))
        if kind == "tn"
        else pl.BlockSpec((block, depth), lambda i: (first + i, 0))
    )
    return pl.pallas_call(
        functools.partial(product_kernel, kind),
        grid=(rows // block,),
        in_specs=[some, pl.BlockSpec(right.shape, lambda i: (0, 0))],
        out_specs=pl.BlockSpec((block, columns), lambda i: (i, 0)),
        out_shape=jax.ShapeDtypeStruct((rows, columns), dtype),
        compiler_params=params(56),
        cost_estimate=pl.CostEstimate(flops=0, bytes_accessed=cost, transcendentals=0)
        if cost
        else None,
        name="product_" + kind,
    )(left, right)


def split_kernel(own_width, ctx, sums, *outs):
    for at, out in enumerate(outs):
        block = ctx[0] ^ (at + 1)
        out[:, : 3 * own_width] = sums[block, :, : 3 * own_width].astype(half)
        out[:, 3 * own_width :] = sums[block, :, 4 * own_width :].astype(half)


def split_blocks(ctx, sums, own_width):
    count, share, width = sums.shape
    return pl.pallas_call(
        functools.partial(split_kernel, own_width),
        in_specs=[
            pl.BlockSpec(memory_space=pltpu.SMEM),
            pl.BlockSpec(memory_space=pltpu.VMEM),
        ],
        out_shape=[jax.ShapeDtypeStruct((share, width - own_width), half)] * (count - 1),
        compiler_params=params(56),
        name="split_blocks",
    )(ctx, sums)


def join_kernel(own_width, parts, ctx, sums, *refs):
    got, outs = refs[:-5], refs[-5:]
    cut = own_width // parts
    width = outs[0].shape[1]
    total = sums[ctx[0], :, 4 * own_width :]
    for at in range(len(got) + 1):
        block = ctx[0] ^ at
        for which in range(3):
            for part in range(parts):
                first = (which * parts + part) * cut
                if at == 0:
                    value = sums[block, :, first : first + cut]
                else:
                    value = got[at - 1][:, first : first + cut].astype(single)
                place = pl.multiple_of(part * (width // parts) + block * cut, cut)
                outs[which][:, pl.ds(place, cut)] = value
        if at > 0:
            total = total + got[at - 1][:, 3 * own_width :].astype(single)
        outs[3][:, at * own_width : (at + 1) * own_width] = sums[
            at, :, 3 * own_width : 4 * own_width
        ]
    outs[4][...] = total


def join_blocks(ctx, sums, got, own_width, parts):
    count, share, width = sums.shape
    full = count * own_width
    return pl.pallas_call(
        functools.partial(join_kernel, own_width, parts),
        in_specs=[pl.BlockSpec(memory_space=pltpu.SMEM)]
        + [pl.BlockSpec(memory_space=pltpu.VMEM)] * count,
        out_shape=[jax.ShapeDtypeStruct((share, full), single)] * 4
        + [jax.ShapeDtypeStruct((share, width - 4 * own_width), single)],
        compiler_params=params(56),
        name="join_blocks",
    )(ctx, sums, *got)


def into_kernel(left, right, held, out):
    out[...] = t_dot(left[...], right[...]).astype(half)


def product_into(left, right, held, at):
    depth, rows = left.shape
    columns = right.shape[1]
    block = math.gcd(rows, 512)
    return pl.pallas_call(
        into_kernel,
        grid=(rows // block,),
        in_specs=[
            pl.BlockSpec((depth, block), lambda i: (0, i)),
            pl.BlockSpec((depth, columns), lambda i: (0, 0)),
            in_hbm,
        ],
        out_specs=pl.BlockSpec((block, columns), lambda i: (i, at)),
        out_shape=jax.ShapeDtypeStruct(held.shape, held.dtype),
        input_output_aliases={2: 0},
        compiler_params=params(56),
        name="product_into",
    )(left, right, held)


def weights_kernel(left, right, weight, out, gained):
    grad = t_dot(left[...], right[...])
    out[...] = grad.astype(half)
    gained[...] = jnp.sum(grad * weight[...].astype(single), axis=-1, keepdims=True)


def weight_gradients(left, right, weight):
    depth, rows = left.shape
    columns = right.shape[1]
    block = math.gcd(rows, 512)
    part = pl.BlockSpec((block, columns), lambda i: (i, 0))
    return pl.pallas_call(
        weights_kernel,
        grid=(rows // block,),
        in_specs=[
            pl.BlockSpec((depth, block), lambda i: (0, i)),
            pl.BlockSpec((depth, columns), lambda i: (0, 0)),
            part,
        ],
        out_specs=[part, pl.BlockSpec((block, 1), lambda i: (i, 0))],
        out_shape=[
            jax.ShapeDtypeStruct((rows, columns), half),
            jax.ShapeDtypeStruct((rows, 1), single),
        ],
        compiler_params=params(56),
        name="weight_gradients",
    )(left, right, weight)


def norm_kernel(gain, *refs):
    blocks, (out, inverse) = refs[:-2], refs[-2:]

    for at, block in enumerate(blocks):

        @pl.when(pl.program_id(0) == at)
        def own():
            values = block[...].astype(single)
            scale = inverse_rms(values)
            inverse[...] = scale
            out[...] = (values * scale * gain[...]).astype(half)


def norm_rows(blocks, gain):
    count = len(blocks)
    rows, width = blocks[0].shape
    return pl.pallas_call(
        norm_kernel,
        grid=(count,),
        in_specs=[pl.BlockSpec((1, width), lambda i: (0, 0))]
        + [pl.BlockSpec((rows, width), lambda i: (0, 0))] * count,
        out_specs=[
            pl.BlockSpec((rows, width), lambda i: (i, 0)),
            pl.BlockSpec((rows, 1), lambda i: (i, 0)),
        ],
        out_shape=[
            jax.ShapeDtypeStruct((count * rows, width), half),
            jax.ShapeDtypeStruct((count * rows, 1), single),
        ],
        compiler_params=params(56),
        name="norm_rows",
    )(gain, *blocks)


def stack_kernel(*refs):
    for at, block in enumerate(refs[:-1]):

        @pl.when(pl.program_id(0) == at)
        def own():
            refs[-1][...] = block[...]


def stack_rows(blocks):
    count = len(blocks)
    rows, width = blocks[0].shape
    return pl.pallas_call(
        stack_kernel,
        grid=(count,),
        in_specs=[pl.BlockSpec((rows, width), lambda i: (0, 0))] * count,
        out_specs=pl.BlockSpec((rows, width), lambda i: (i, 0)),
        out_shape=jax.ShapeDtypeStruct((count * rows, width), blocks[0].dtype),
        compiler_params=params(56),
        name="stack_rows",
    )(*blocks)


def sum_kernel(own, got, *refs):
    token, outs = refs[-1], refs[:-1]
    total = own[...].astype(single) + got[...].astype(single)
    cut = total.shape[1] // len(outs)
    for at, out in enumerate(outs):
        out[...] = total[:, at * cut : (at + 1) * cut]
    token[...] = jnp.zeros_like(token)


def sum_up(own, got, parts):
    rows, width = got.shape
    block = math.gcd(rows, 256)
    cut = width // parts
    whole = pl.BlockSpec((block, width), lambda i: (i, 0))
    *outs, token = pl.pallas_call(
        sum_kernel,
        grid=(rows // block,),
        in_specs=[whole, whole],
        out_specs=[pl.BlockSpec((block, cut), lambda i: (i, 0))] * parts
        + [pl.BlockSpec((8, 128), lambda i: (0, 0))],
        out_shape=[jax.ShapeDtypeStruct((rows, cut), single)] * parts
        + [jax.ShapeDtypeStruct((8, 128), single)],
        compiler_params=params(60),
        name="sum_up",
    )(own, got)
    return outs, token


def put_kernel(order, slot_a, slot_b, hidden_a, hidden_b, weight, out):
    rows = jnp.concatenate([hidden_a[0], hidden_b[0]], axis=0)
    capacity = hidden_a.shape[1]
    places = [chosen_rows(slot[0], capacity) for slot in (slot_a, slot_b)]
    for col in range(0, out.shape[2], 512):
        cut = slice(col, col + 512)
        produced = dot(rows, weight[:, cut]).astype(half)
        out[0, :, cut] = t_dot(places[0], produced[:capacity]).astype(half)
        out[1, :, cut] = t_dot(places[1], produced[capacity:]).astype(half)


def put_rows(order, slot, hidden, weight):
    count, capacity, inner = hidden.shape
    length, width = slot.shape[-1], weight.shape[1]

    def some(shape, side):
        return pl.BlockSpec((1,) + shape, lambda i, order: (order[2 * i + side], 0, 0))

    return pl.pallas_call(
        put_kernel,
        grid_spec=pltpu.PrefetchScalarGridSpec(
            num_scalar_prefetch=1,
            grid=(order.shape[0] // 2,),
            in_specs=[
                some((1, length), 0),
                some((1, length), 1),
                some((capacity, inner), 0),
                some((capacity, inner), 1),
                pl.BlockSpec(weight.shape, lambda i, order: (0, 0)),
            ],
            out_specs=pl.BlockSpec((2, length, width), lambda i, order: (i, 0, 0)),
        ),
        out_shape=jax.ShapeDtypeStruct((order.shape[0], length, width), half),
        compiler_params=params(60),
        name="put_rows",
    )(order, slot, slot, hidden, hidden, weight)


def add_kernel(split, own_a, own_b, got_a, got_b, ahead, behind):
    up, down = own_a[...].astype(single), own_b[...].astype(single)
    if split < up.shape[0]:
        ahead[:split] = (up[:split] + got_a[...].astype(single)).astype(half)
        ahead[split:] = own_a[split:]
        behind[:split] = own_b[:split]
        behind[split:] = (down[split:] + got_b[...].astype(single)).astype(half)
    else:
        ahead[...] = (up + got_a[...].astype(single)).astype(half)
        behind[...] = (down + got_b[...].astype(single)).astype(half)


def add_pair(own_a, own_b, got_a, got_b):
    return pl.pallas_call(
        functools.partial(add_kernel, got_a.shape[0]),
        out_shape=[jax.ShapeDtypeStruct(own_a.shape, half)] * 2,
        compiler_params=params(56),
        name="add_pair",
    )(own_a, own_b, got_a, got_b)


def combine_kernel(split, plus, minus, other_plus, other_minus, got_a, got_b, ahead, behind):
    up = plus[0].astype(single) + other_plus[0].astype(single)
    down = minus[0].astype(single) + other_minus[0].astype(single)
    rows = up.shape[0]
    if split < rows:
        ahead[:split] = (up[:split] + got_a[...].astype(single)).astype(half)
        ahead[split:] = up[split:].astype(half)
        behind[:split] = down[:split].astype(half)
        behind[split:] = (down[split:] + got_b[...].astype(single)).astype(half)
    else:
        ahead[...] = (up + got_a[...].astype(single)).astype(half)
        behind[...] = (down + got_b[...].astype(single)).astype(half)


def combine(own, other, step, got_a, got_b):
    length, width = own.shape[1:]
    plus = pl.BlockSpec((1, length, width), lambda i: (2 * step + 1, 0, 0))
    minus = pl.BlockSpec((1, length, width), lambda i: (2 * step, 0, 0))
    got = pl.BlockSpec(got_a.shape, lambda i: (0, 0))
    out = pl.BlockSpec((length, width), lambda i: (0, 0))
    return pl.pallas_call(
        functools.partial(combine_kernel, got_a.shape[0]),
        grid=(1,),
        in_specs=[plus, minus, plus, minus, got, got],
        out_specs=[out, out],
        out_shape=[jax.ShapeDtypeStruct((length, width), half)] * 2,
        compiler_params=params(56),
        name="combine",
    )(own, own, other, other, got_a, got_b)


def far_kernel(own, other, ahead, behind):
    total = own[0].astype(single) + other[0].astype(single)
    split = ahead.shape[0]
    ahead[...] = total[:split].astype(half)
    behind[...] = total[split:].astype(half)


def far_halves(own, other):
    count, length, width = own.shape
    part = pl.BlockSpec((1, length, width), lambda i: (1, 0, 0))
    out = pl.BlockSpec((length // 2, width), lambda i: (0, 0))
    return pl.pallas_call(
        far_kernel,
        grid=(1,),
        in_specs=[part, part],
        out_specs=[out, out],
        out_shape=[jax.ShapeDtypeStruct((length // 2, width), half)] * 2,
        compiler_params=params(56),
        name="far_halves",
    )(own, other)


def last_kernel(own, other, got_a, got_b, base, out):
    total = base[...] + own[0].astype(single) + other[0].astype(single)
    total = total + got_a[...].astype(single) + got_b[...].astype(single)
    out[...] = total.astype(half)


def last_sum(own, other, got_a, got_b, base):
    length, width = base.shape
    part = pl.BlockSpec((1, length, width), lambda i: (0, 0, 0))
    whole = pl.BlockSpec((length, width), lambda i: (0, 0))
    return pl.pallas_call(
        last_kernel,
        grid=(1,),
        in_specs=[part, part, whole, whole, whole],
        out_specs=whole,
        out_shape=jax.ShapeDtypeStruct((length, width), half),
        compiler_params=params(56),
        name="last_sum",
    )(own, other, got_a, got_b, base)


TILE = 512


def pair_kernel(
    capacity,
    tail,
    order,
    slot,
    piece_a,
    piece_b,
    lanes,
    cot_all,
    gate_v,
    up_v,
    down_v,
    in_rows,
    in_hidden,
    in_gate,
    in_up,
    in_cot,
    home_a,
    home_b,
    all_rows,
    all_hidden,
    all_gate,
    all_up,
    all_cot,
    cot_v,
    cot_rows,
    rows,
    hidden,
    grad_gate,
    grad_up,
    load_sem,
    store_sem,
):
    width, inner = gate_v.shape
    start = order[2]
    loads, stores = [], []

    def load(source, target):
        copy = pltpu.make_async_copy(source, target, load_sem.at[len(loads)])
        copy.start()
        loads.append(copy)
        return copy

    def store(source, target):
        copy = pltpu.make_async_copy(source, target, store_sem.at[len(stores)])
        copy.start()
        stores.append(copy)

    span = pl.ds(pl.multiple_of(start * capacity, 32), 2 * capacity)
    get_cot = [load(cot_all.at[order[at]], cot_v.at[at]) for at in range(2)]
    homes, pieces = (home_a, home_b), (piece_a, piece_b)
    places = [chosen_rows(slot[at], capacity) for at in range(2)]
    parts = [slice(at * capacity, (at + 1) * capacity) for at in range(2)]
    gates = []
    for at in range(2):
        for col in range(0, width, TILE):
            cut = slice(col, col + TILE)
            rows[parts[at], cut] = dot(places[at], pieces[at][:, cut]).astype(half)
        picked = dot(places[at], pieces[at][:, width:])
        gates.append(jnp.sum(picked * lanes[...], axis=-1, keepdims=True))
    gate = jnp.concatenate(gates, axis=0)
    store(rows, all_rows.at[span])
    for at in range(2):
        get_cot[at].wait()
        for col in range(0, width, TILE):
            cut = slice(col, col + TILE)
            cot_rows[parts[at], cut] = dot(places[at], cot_v[at, :, cut]).astype(half)
    store(cot_rows, all_cot.at[span])
    grad_g = jnp.zeros((2 * capacity, 1), single)
    for col in range(0, inner, TILE):
        cut = slice(col, col + TILE)
        gate_pre = dot(rows[...], gate_v[:, cut])
        up_pre = dot(rows[...], up_v[:, cut])
        returned = dot_t(cot_rows[...], down_v[cut, :])
        activated, slope = activate(gate_pre, up_pre)
        kept = activated * up_pre
        hidden[:, cut] = (gate * kept).astype(half)
        grad_g = grad_g + jnp.sum(returned * kept, axis=-1, keepdims=True)
        grad_hidden = gate * returned
        grad_gate[:, cut] = (grad_hidden * up_pre * slope).astype(half)
        grad_up[:, cut] = (grad_hidden * activated).astype(half)
    store(hidden, all_hidden.at[span])
    store(grad_gate, all_gate.at[span])
    store(grad_up, all_up.at[span])
    for col in range(0, width, TILE):
        cut = slice(col, col + TILE)
        back = dot_t(grad_gate[...], gate_v[cut, :]) + dot_t(grad_up[...], up_v[cut, :])
        back = back.astype(half)
        for side in range(2):
            homes[side][:, cut] = t_dot(places[side], back[parts[side]]).astype(half)
    high = grad_g.astype(half).astype(single)
    ends = high * lanes[...] * tail[0:1] + (grad_g - high) * lanes[...] * tail[1:2]
    ends = ends.astype(half)
    for side in range(2):
        homes[side][:, width:] = t_dot(places[side], ends[parts[side]]).astype(half)
    for copy in stores:
        copy.wait()


def expert_pair(order, slot, pieces, lanes, tails, cot_all, weights, held, capacity):
    width, inner = weights[0].shape
    length, wide = pieces[0].shape
    in_vmem = pl.BlockSpec(memory_space=pltpu.VMEM)
    count = 2 * capacity

    def body(order, slot, a, b, lanes, tails, *refs):
        pair_kernel(capacity, tails, order, slot, a, b, lanes, *refs)

    out = pl.pallas_call(
        body,
        in_specs=[pl.BlockSpec(memory_space=pltpu.SMEM)]
        + [in_vmem] * 5
        + [in_hbm]
        + [in_vmem] * 3
        + [in_hbm] * 5,
        out_specs=[in_vmem] * 2 + [in_hbm] * 5,
        out_shape=[jax.ShapeDtypeStruct((length, wide), half)] * 2
        + [jax.ShapeDtypeStruct(value.shape, value.dtype) for value in held],
        scratch_shapes=[
            pltpu.VMEM((2, length, width), half),
            pltpu.VMEM((count, width), half),
            pltpu.VMEM((count, width), half),
            pltpu.VMEM((count, inner), half),
            pltpu.VMEM((count, inner), half),
            pltpu.VMEM((count, inner), half),
            pltpu.SemaphoreType.DMA((2,)),
            pltpu.SemaphoreType.DMA((5,)),
        ],
        input_output_aliases={10 + i: 2 + i for i in range(5)},
        compiler_params=params(34),
        name="expert_pair",
    )(order, slot, *pieces, lanes, tails, cot_all, *weights, *held)
    return out[:2], list(out[2:])


def swap(value, axis, bit):
    count = lax.axis_size(axis)
    return lax.ppermute(value, axis, [(i, i ^ bit) for i in range(count)])


def bits_down(count):
    bits = []
    bit = count // 2
    while bit >= 1:
        bits.append(bit)
        bit //= 2
    return bits


def xor_gather(value, axis, begun=None):
    blocks = {0: value}
    for bit in bits_down(lax.axis_size(axis)):
        held = sorted(blocks)
        if begun is not None and len(held) == 1:
            blocks[bit] = begun
            continue
        for j in held:
            blocks[j | bit] = swap(blocks[j], axis, bit)
    return [blocks[j] for j in sorted(blocks)]


def xor_scatter(value, axis):
    count = lax.axis_size(axis)
    rows = value.shape[0] // count
    held = value
    for bit in reversed(bits_down(count)):
        shaped = held.reshape(-1, 2, rows, held.shape[-1])
        got = swap(shaped[:, 1].astype(half), axis, bit)
        held = shaped[:, 0].astype(single) + got.astype(single)
        held = held.reshape(-1, held.shape[-1])
    return held


def xor_sum(value, axis):
    count = lax.axis_size(axis)
    blocks = value.reshape(-1, count, value.shape[-1] // count)
    for bit in reversed(bits_down(count)):
        got = swap(blocks, axis, bit)
        blocks = blocks + jnp.stack([got[:, j ^ bit] for j in range(count)], axis=1)
    return blocks.reshape(value.shape)


def doubling_gather(value, axes):
    for axis in reversed(axes):
        for bit in reversed(bits_down(lax.axis_size(axis))):
            other = swap(value, axis, bit)
            low = (lax.axis_index(axis) & bit) == 0
            value = jnp.concatenate(
                [jnp.where(low, value, other), jnp.where(low, other, value)], axis=0
            )
    return value


def halving_scatter(value, axes):
    for axis in axes:
        for bit in bits_down(lax.axis_size(axis)):
            rows = value.shape[0] // 2
            low = (lax.axis_index(axis) & bit) == 0
            kept = jnp.where(low, value[:rows], value[rows:])
            sent = jnp.where(low, value[rows:], value[:rows])
            value = kept + swap(sent, axis, bit)
    return value


def snake(outer, inner):
    order = []
    for a in range(outer):
        line = range(inner) if a % 2 == 0 else reversed(range(inner))
        order += [(a, b) for b in line]
    return order


class Ring:
    def __init__(self, axes, planes):
        outer, inner = lax.axis_size(axes[0]) // planes, lax.axis_size(axes[1])
        order = snake(outer, inner)
        self.axes, self.planes, self.count = axes, planes, len(order)
        flat = [[(a * planes + plane) * inner + b for a, b in order] for plane in range(planes)]
        self.forward, self.backward = [], []
        offsets = self.offsets()
        table = [None] * (self.count * planes)
        for plane, line in enumerate(flat):
            for at, index in enumerate(line):
                after = line[(at + 1) % self.count]
                self.forward.append((index, after))
                self.backward.append((after, index))
                table[index] = []
                for group in offsets:
                    for other in range(planes):
                        for offset in group:
                            table[index].append(flat[plane ^ other][(at + offset) % self.count])
        table = jnp.asarray(np.array(table, np.int32))
        self.order = lax.dynamic_slice(
            table,
            (lax.axis_index(axes), jnp.int32(0)),
            (1, table.shape[1]),
            allow_negative_indices=False,
        ).reshape(-1)

    def offsets(self):
        middle = self.count // 2
        return [[0]] + [[-step, step] for step in range(1, middle)] + [[middle]]

    def ahead(self, value):
        return lax.ppermute(value, self.axes, self.forward)

    def behind(self, value):
        return lax.ppermute(value, self.axes, self.backward)

    def gather(self, value, each, room=60, first=()):
        tokens = each(0, [value])
        tokens = tokens + list(first)
        split = value.shape[0] // 2
        from_back = from_front = value
        for step in range(1, self.count // 2):
            from_back, from_front = self.ahead(from_back), self.behind(from_front)
            if tokens:
                from_back, from_front = after([from_back, from_front], tokens, room)
            tokens = each(step, [from_back, from_front])
        last = jnp.concatenate(
            [self.ahead(from_back[:split]), self.behind(from_front[split:])], axis=0
        )
        if tokens:
            (last,) = after([last], tokens, room)
        each(self.count // 2, [last])

    def scatter(self, pick, between=None):
        middle = self.count // 2
        ahead, behind = pick(middle, 0), pick(middle, 1)
        for step in range(middle - 1, 0, -1):
            tokens = between(step, [ahead, behind]) if between else []
            got_ahead, got_behind = self.ahead(ahead), self.behind(behind)
            own_ahead, own_behind = pick(step, 0), pick(step, 1)
            if tokens:
                own_ahead, own_behind = after([own_ahead, own_behind], tokens)
            ahead, behind = add_pair(own_ahead, own_behind, got_ahead, got_behind)
        tokens = between(0, [ahead, behind]) if between else []
        got_ahead, got_behind = self.ahead(ahead), self.behind(behind)
        own = pick(0, 0)
        if tokens:
            (own,) = after([own], tokens)
        return own.astype(single) + got_ahead.astype(single) + got_behind.astype(single)


def add(left, right):
    return (left.astype(single) + right.astype(single)).astype(half)


def trade(buffer):
    count = lax.axis_size("ctx") * lax.axis_size("expert")
    shaped = buffer.reshape(count, -1, buffer.shape[-1])
    moved = lax.all_to_all(shaped, ("ctx", "expert"), split_axis=0, concat_axis=0, tiled=True)
    return moved.reshape(buffer.shape)


def activate(gate_pre, up_pre):
    sigmoid = jax.nn.sigmoid(gate_pre)
    activated = gate_pre * sigmoid
    slope = sigmoid * (1.0 + gate_pre * (1.0 - sigmoid))
    return activated, slope


def experts_by_trade(m_low, gates, cot, picks, w_gate, w_up, w_down, expert_total, capacity):
    rows, width = m_low.shape
    top = picks.shape[1]
    locals_ = w_gate.shape[0]
    flat = (picks.reshape(-1)[:, None] == jnp.arange(expert_total)[None, :]).astype(jnp.int32)
    ranking = jnp.sum((jnp.cumsum(flat, axis=0) - 1) * flat, axis=1)
    slots = picks.reshape(-1) * capacity + ranking
    pair_rows = jnp.arange(rows * top) // top
    empty = jnp.zeros((expert_total * capacity, width), half)
    incoming = trade(empty.at[slots].set(m_low[pair_rows])).reshape(-1, locals_, capacity, width)

    def summed(form, left, right):
        return jnp.einsum(form, left, right, preferred_element_type=single)

    gate_pre = summed("sxcd,xdf->sxcf", incoming, w_gate)
    up_pre = summed("sxcd,xdf->sxcf", incoming, w_up)
    activated, slope = activate(gate_pre, up_pre)
    hidden = (activated * up_pre).astype(half)
    produced = summed("sxcf,xfd->sxcd", hidden, w_down).astype(half)
    returned = trade(produced.reshape(-1, width))
    picked = returned[slots].reshape(rows, top, width).astype(single)
    mixed = jnp.sum(gates[..., None] * picked, axis=1)
    grad_gates = jnp.sum(cot[:, None, :] * picked, axis=-1)
    back = (gates[..., None] * cot[:, None, :]).astype(half).reshape(-1, width)
    grad_in = trade(empty.at[slots].set(back)).reshape(-1, locals_, capacity, width)
    grad_hidden = summed("sxcd,xfd->sxcf", grad_in, w_down)
    grad_down = summed("sxcf,sxcd->xfd", hidden, grad_in)
    grad_gate_pre = (grad_hidden * up_pre * slope).astype(half)
    grad_up_pre = (grad_hidden * activated).astype(half)
    grad_gate = summed("sxcd,sxcf->xdf", incoming, grad_gate_pre)
    grad_up = summed("sxcd,sxcf->xdf", incoming, grad_up_pre)
    grad_rows = summed("sxcf,xdf->sxcd", grad_gate_pre, w_gate)
    grad_rows = (grad_rows + summed("sxcf,xdf->sxcd", grad_up_pre, w_up)).astype(half)
    grad_back = trade(grad_rows.reshape(-1, width))
    grad_m = jnp.sum(grad_back[slots].reshape(rows, top, width).astype(single), axis=1)
    chosen = picks[..., None] == jnp.arange(expert_total)[None, None, :]
    grad_probs = jnp.sum(jnp.where(chosen, grad_gates[..., None], 0.0), axis=1)
    return mixed, grad_m, grad_probs, [grad_down[0], grad_gate[0], grad_up[0]]


def two_parts(value):
    high = lax.reduce_precision(value, 8, 7)
    return high.astype(half), (value - high).astype(half)


def slots_of(routes_all):
    me = lax.axis_index(("ctx", "expert")).astype(routes_all.dtype)
    chosen = jnp.any(routes_all == me, axis=-1)
    rows = chosen.shape[1]
    before = (jnp.arange(rows)[:, None] <= jnp.arange(rows)[None, :]).astype(half)
    rank = dot(chosen.astype(half), before).astype(jnp.int32) - 1
    return jnp.where(chosen, rank, -1)


class ExpertsByRing:
    def __init__(self, slot, cot, w_gate, w_up, w_down, capacity):
        self.ring = Ring(("ctx", "expert"), 2)
        self.capacity = capacity
        self.weights = (w_gate[0], w_up[0], w_down[0])
        self.me = lax.axis_index(("ctx", "expert"))
        self.slot = slot[self.ring.order][:, None, :]
        cot_all = lax.all_gather(cot, ("ctx", "expert"), axis=0, tiled=True)
        self.cot_all = cot_all.reshape(slot.shape + cot.shape[-1:])

    def run(self, m_low, gate_dense, dp_sum):
        rows, width = m_low.shape
        inner = self.weights[0].shape[1]
        experts = gate_dense.shape[1]
        lanes = 64
        high, low = two_parts(gate_dense)
        fill = jnp.zeros((rows, lanes - experts), half)
        wide = jnp.concatenate([m_low, high, fill, low, fill], axis=1)
        lane = jnp.arange(2 * lanes)
        mine = (lane % lanes == self.me).astype(single)[None]
        tails = jnp.stack([lane < lanes, lane >= lanes]).astype(single)
        devices = self.slot.shape[0]
        total = devices * self.capacity
        held = [
            empty("rows", (total, width), half),
            empty("hidden", (total, inner), half),
            empty("gate", (total, inner), half),
            empty("up", (total, inner), half),
            empty("cot", (total, width), half),
        ]
        sums = []

        def pair(start, pieces):
            order = jnp.concatenate(
                [self.ring.order[start : start + 2], jnp.full((1,), start, jnp.int32)]
            )
            slot = self.slot[start : start + 2]
            homes, held[:] = expert_pair(
                order, slot, pieces, mine, tails, self.cot_all, self.weights, held, self.capacity
            )
            return homes

        def each(step, arrived):
            start = sum(2 * len(group) for group in self.ring.offsets()[:step])
            others = [swap(piece, "ctx", 1) for piece in arrived]
            if len(arrived) == 1:
                homes = pair(start, arrived + others)
                tokens = [homes[0]]
            else:
                homes = pair(start, arrived)
                tokens = [homes[0]]
                homes = homes + pair(start + 2, others)
            count = len(arrived)
            sums.append(
                [add(homes[at], swap(homes[at + count], "ctx", 1)) for at in range(count)]
            )
            return tokens

        self.ring.gather(wide, each, 1)
        incoming, hidden, gate, up, cot_rows = held
        grads = []
        work = [(hidden, cot_rows), (incoming, gate), (incoming, up)]

        def between(step, sent):
            if not work:
                return [] if step else dp_sum.arrived(0)
            left, right = work.pop(0)
            (right,) = after([right], sent)
            if len(grads) == 0:
                grads.append(product("tn", left, right, half))
            else:
                both = grads[1] if len(grads) > 1 else empty("pre", (width, 2 * inner), half)
                grads.append(product_into(left, right, both, len(grads) - 1))
            if len(grads) != 2:
                dp_sum.add(grads[-1])
            return grads[-1:]

        def pick(step, side):
            if step == len(sums) - 1:
                far = sums[step][0]
                split = far.shape[0] // 2
                return far[split:] if side else far[:split]
            return sums[step][-1 - side]

        summed = self.ring.scatter(pick, between)
        while work:
            between(0, [summed])
        grad_m = summed[:, :width]
        tail = summed[:, width:]
        grad_probs = tail[:, :experts] + tail[:, lanes : lanes + experts]
        self.hidden = hidden
        return grad_m, grad_probs

    def put(self, tokens):
        (hidden,) = after([self.hidden], tokens)
        hidden = hidden.reshape(-1, self.capacity, hidden.shape[-1])
        planes = [[], []]
        at = 0
        for group in self.ring.offsets():
            for plane in planes:
                plane.append(list(range(at, at + len(group))))
                at += len(group)
        parts = []
        for plane in reversed(planes):
            order = plane[0] + plane[-1] + sum(plane[1:-1], [])
            order = jnp.asarray(np.array(order, np.int32))
            parts.append(put_rows(order, self.slot, hidden, self.weights[2]))
        self.own = parts[1]
        self.other = swap(parts[0], "ctx", 1)
        return parts

    def send(self, step, tokens):
        ring = self.ring
        if step == ring.count // 2:
            (other,) = after([self.other], tokens)
            self.other = other
            ahead, behind = far_halves(self.own, other)
        else:
            got_a, got_b = after(self.got, tokens)
            ahead, behind = combine(self.own, self.other, step, got_a, got_b)
        self.got = [ring.ahead(ahead), ring.behind(behind)]
        return [ahead]

    def mixed(self, base, tokens):
        got_a, got_b = after(self.got, tokens)
        return last_sum(self.own, self.other, got_a, got_b, base)


class DpSum:
    def __init__(self):
        self.two = lax.axis_size("dp") == 2
        self.grads, self.got, self.outs = [], [], []

    def add(self, grad):
        self.grads.append(grad.astype(half))
        if self.two:
            self.got.append(swap(self.grads[-1], "dp", 1))

    def arrived(self, at):
        return self.got[at : at + 1]

    def finish(self, at):
        if self.two:
            outs, token = sum_up(self.grads[at], self.got[at], at + 1)
            self.outs += outs
            return [token]
        total = lax.psum(self.grads[at], "dp").astype(single)
        self.outs += jnp.split(total, at + 1, axis=1)
        return []

    def results(self):
        down, gate, up = self.outs
        return gate[None], up[None], down[None]


def on_device(
    tokens,
    w_query,
    w_key,
    w_value,
    w_output,
    w_router,
    norm_gains,
    w_gate,
    w_up,
    w_down,
    routes,
    positions,
    lengths,
    cotangent,
):
    dp_count, ctx_count, expert_count = (
        lax.axis_size("dp"),
        lax.axis_size("ctx"),
        lax.axis_size("expert"),
    )
    world = ("dp", "ctx", "expert")
    ctx = lax.axis_index("ctx")
    row_count, width = tokens.shape[1:]
    head_size = width // HEADS
    head_count = HEADS // ctx_count
    share = w_query.shape[0]
    own_width = width // ctx_count
    expert_total = w_router.shape[1]
    picks = routes[0]
    top = picks.shape[1]
    capacity = 5 * row_count * top // (4 * expert_total)
    all_rows = row_count * ctx_count
    cot = cotangent[0].astype(single)

    packed = jnp.concatenate(
        [w_router.reshape(-1), norm_gains.reshape(-1), picks.astype(half).reshape(-1)]
    )
    packed_size = packed.shape[0]
    packed = jnp.pad(packed, (0, -packed_size % 1024)).reshape(1, -1, 128)
    router_size, gain_size = share * expert_total, 4 * share

    def own_features(values):
        shaped = values.reshape(values.shape[:-1] + (dp_count, ctx_count, -1))
        return lax.dynamic_index_in_dim(shaped, ctx, values.ndim, keepdims=False).reshape(
            values.shape[:-1] + (own_width,)
        )

    pair_ring = Ring(("dp", "expert"), 1)
    outer, inner = pair_ring.order // expert_count, pair_ring.order % expert_count
    coords = jnp.stack([outer, inner, pair_ring.order], axis=1).reshape(-1)
    shards = jnp.concatenate(
        [
            value.reshape(share, dp_count, ctx_count, -1)
            for value in (w_query, w_key, w_value)
        ],
        axis=1,
    )

    def columns_for(j):
        return lax.dynamic_index_in_dim(
            shards, ctx ^ j, 2, keepdims=False, allow_negative_indices=False
        ).reshape(share, -1)

    blocks = [columns_for(0)]
    for j in range(1, ctx_count):
        blocks.append(swap(columns_for(j), "ctx", j))
    by_ctx = ctx ^ jnp.arange(ctx_count)
    blocks = jnp.stack(blocks)[by_ctx].reshape(ctx_count * share, -1)
    output_blocks = [
        w_output[:, at * own_width : (at + 1) * own_width] for at in range(ctx_count)
    ]
    unit = jnp.concatenate([blocks, jnp.concatenate(output_blocks, axis=0)], axis=1)
    gathered = {
        "count": 0,
        "weights": (
            empty("qkv", (dp_count, ctx_count, expert_count, share, 3 * own_width), half),
            empty("output", (dp_count * expert_count, share, width), half),
        ),
    }

    def rows_ready(step, arrived):
        done = gathered["count"]
        gathered["count"] = done + len(arrived)
        gathered["weights"] = place_units(
            coords[3 * done : 3 * gathered["count"]],
            [piece.reshape(ctx_count, share, -1) for piece in arrived],
            *gathered["weights"],
        )
        result = list(gathered["weights"][1:])
        middle = pair_ring.count // 2
        if step == middle - 1:
            (gathered["cot"],) = after([cotangent[0]], arrived)
        if step == 1:
            (x_begun,) = after([gathered["x"]], arrived)
            gathered["x"] = xor_gather(tokens[0], "ctx", x_begun)
        if step == max(1, middle - 2):
            small = gathered["small"].reshape(dp_count * ctx_count * expert_count, -1)
            gathered["router"] = small[:, :router_size].reshape(width, expert_total)
            gains = small[:, router_size : router_size + gain_size].reshape(-1, 4, share)
            gathered["gains"] = gains.transpose(1, 0, 2).reshape(4, width).astype(single)
            routes_all = small[:, router_size + gain_size : packed_size]
            routes_all = routes_all.reshape(dp_count, -1, row_count, top)
            gathered["slot"] = slots_of(routes_all[lax.axis_index("dp")])
            gathered["a_low"], gathered["inverse_a"] = norm_rows(
                gathered["x"], gathered["gains"][:1]
            )
            result += [gathered["a_low"], cosine, sine, gathered["slot"]]
        return result

    all_pos = positions[0].reshape(ctx_count, row_count)[by_ctx].reshape(-1)
    cosine, sine = rope_tables(all_pos, head_size)
    sine = jnp.where(jnp.arange(head_size) < head_size // 2, -sine, sine)
    (packed,) = after([packed], [unit])
    gathered["small"] = doubling_gather(packed, world)
    gathered["x"] = swap(tokens[0], "ctx", ctx_count // 2)
    pair_ring.gather(unit, rows_ready, first=[gathered["small"]])
    gains, slot, router_w = gathered["gains"], gathered["slot"], gathered["router"]
    qkv_w, output_w = gathered["weights"]
    qkv_w = qkv_w.reshape(width, 3 * own_width)
    output_w = output_w.reshape(own_width, width)

    inverse_a, a_low = gathered["inverse_a"], gathered["a_low"]
    qkv = product("nn", a_low, qkv_w, single, 256)
    q_raw, k_raw = qkv[:, :own_width], qkv[:, own_width : 2 * own_width]
    squares = jnp.stack([jnp.sum(q_raw * q_raw, axis=-1), jnp.sum(k_raw * k_raw, axis=-1)])
    inverse = lax.rsqrt(xor_sum(squares, "ctx") / width + epsilon).T
    gains_qk = jnp.stack([own_features(gains[1]), own_features(gains[2])])
    q_low, k_low, v_low = rope_forward(qkv, inverse, cosine, sine, gains_qk, head_count)

    by_ring = ctx_count * expert_count == 16 and ctx_count % 2 == 0
    if by_ring:
        layer = ExpertsByRing(slot, gathered["cot"], w_gate, w_up, w_down, capacity)

    query_pos = all_pos[:, None]
    key_pos = jnp.where(all_pos < lengths[0], all_pos, 1 << 30)[None, :]
    attended_low, log_total = attend(q_low, k_low, v_low, query_pos, key_pos, head_count)
    first = tokens[0].astype(single) + xor_scatter(product("nn", attended_low, output_w, half, 256), "ctx")
    inverse_m = inverse_rms(first)
    normed_m = first * inverse_m
    m_low = (normed_m * gains[3]).astype(half)
    router_probs = jax.nn.softmax(dot(m_low, router_w), axis=-1)
    chosen = picks[..., None] == jnp.arange(expert_total)[None, None, :]
    dp_sum = DpSum()
    if by_ring:
        gate_dense = jnp.where(jnp.any(chosen, axis=1), router_probs, 0.0)
        grad_m, grad_probs = layer.run(m_low, gate_dense, dp_sum)
    else:
        gates = jnp.sum(jnp.where(chosen, router_probs[:, None, :], 0.0), axis=-1)
        added, grad_m, grad_probs, expert_grads = experts_by_trade(
            m_low, gates, cot, picks, w_gate, w_up, w_down, expert_total, capacity
        )
        dp_sum.add(expert_grads[0])
        dp_sum.add(jnp.concatenate(expert_grads[1:], axis=1))
    grad_logits = router_probs * (
        grad_probs - jnp.sum(router_probs * grad_probs, axis=-1, keepdims=True)
    )
    grad_logits_low = grad_logits.astype(half)
    grad_router = t_dot(m_low, grad_logits_low)
    grad_m = grad_m + dot_t(grad_logits_low, router_w)
    grad_gain_m = jnp.sum(grad_m * normed_m, axis=0)
    grad_normed = grad_m * gains[3]
    grad_first = cot + inverse_m * (
        grad_normed - normed_m * jnp.mean(grad_normed * normed_m, axis=-1, keepdims=True)
    )
    grad_first_low = grad_first.astype(half)
    begun = swap(grad_first_low, "ctx", ctx_count // 2)

    def send(step, values, tokens=()):
        return after(values, layer.send(step, list(tokens) or values[:1])) if by_ring else values

    if by_ring:
        (begun,) = send(4, [begun], layer.put([grad_first_low]))
        (begun,) = send(3, [begun])
    grad_attn = stack_rows(xor_gather(grad_first_low, "ctx", begun))
    grad_output = product("tn", attended_low, grad_attn, half, 256)
    grad_o = product("nt", grad_attn, output_w, half, 256)
    dq, dk, dv = attend_back(
        q_low, k_low, v_low, grad_o, log_total, query_pos, key_pos, head_count
    )
    dq, dk, dv = send(2, [dq, dk, dv])
    grad_n, sums, grad_gain_qk = rope_back(
        dq, dk, qkv, inverse, cosine, sine, gains_qk, head_count
    )
    means = (xor_sum(sums.T, "ctx") / width).T
    (means,) = send(1, [means])
    grad_qkv = norm_back(grad_n, qkv, inverse, means, dv)
    grad_qkv_w, grad_gain_a = weight_gradients(a_low, grad_qkv, qkv_w)
    grad_gain_a = grad_gain_a[:, 0] / gains[0]

    def spread(values):
        shaped = jnp.zeros((dp_count, ctx_count, own_width // dp_count), single)
        return lax.dynamic_update_index_in_dim(
            shaped, values.reshape(dp_count, -1), ctx, 1
        ).reshape(-1)

    small = jnp.concatenate(
        [
            grad_router,
            jnp.stack(
                [grad_gain_a, spread(grad_gain_qk[0]), spread(grad_gain_qk[1]), grad_gain_m],
                axis=1,
            ),
        ],
        axis=1,
    ).astype(half)
    small = jnp.pad(small, ((0, 0), (0, -small.shape[1] % 128)))
    units = take_units(
        coords,
        grad_qkv_w.reshape(dp_count, ctx_count, expert_count, share, -1),
        grad_output.reshape(dp_count * expert_count, share, width),
        small.reshape(dp_count, ctx_count, expert_count, share, -1),
    )
    units = [value.reshape(-1, value.shape[-1]) for value in units]

    def part(step, side):
        if step == pair_ring.count // 2:
            return units[side - 2]
        return units[2 * step - side]

    late = []

    def beside(step, sent):
        if step == pair_ring.count // 2 - 1:
            (late_w,) = after([qkv_w], sent)
            late.append(product("nt", grad_qkv, late_w, half, 256, cost=16 << 20))
            if by_ring:
                late.append(layer.mixed(first, sent))
            return late + dp_sum.finish(0) + dp_sum.arrived(1)
        if step == pair_ring.count // 2 - 2:
            return dp_sum.finish(1)
        return []

    own_sum = pair_ring.scatter(part, beside)
    grad_a = xor_scatter(late[0], "ctx")
    grad_normed = grad_a * gains[0]
    normed_own = tokens[0].astype(single) * inverse_a[:row_count]
    grad_x = grad_first + inverse_a[:row_count] * (
        grad_normed - normed_own * jnp.mean(grad_normed * normed_own, axis=-1, keepdims=True)
    )
    own_sum = own_sum.reshape(ctx_count, share, -1)
    ctx_only = ctx.astype(jnp.int32)[None]
    sent = split_blocks(ctx_only, own_sum, own_width)
    got = [swap(block, "ctx", j) for j, block in zip(range(1, ctx_count), sent)]
    query_share, key_share, value_share, output_share, small = join_blocks(
        ctx_only, own_sum, got, own_width, dp_count
    )
    mixed = late[1] if by_ring else first + added
    return (
        mixed.astype(half)[None],
        grad_x[None],
        query_share,
        key_share,
        value_share,
        output_share,
        small[:, :expert_total],
        small[:, expert_total : expert_total + 4].T,
        *dp_sum.results(),
    )


def solution(mesh):
    rows = P(("dp", "expert"), "ctx", None)
    shares = P(("dp", "ctx", "expert"), None)
    experts = P(("ctx", "expert"), None, None)
    gains = P(None, ("dp", "ctx", "expert"))
    return jax.shard_map(
        on_device,
        mesh=mesh,
        in_specs=(
            (rows,)
            + (shares,) * 5
            + (gains,)
            + (experts,) * 3
            + (rows, P(("dp", "expert"), None), P(("dp", "expert")), rows)
        ),
        out_specs=(rows, rows) + (shares,) * 5 + (gains,) + (experts,) * 3,
        check_vma=False,
    )
```
